128 devices in a mesh: dp: 16 (over z_lo, y, core), tensor: 8 (over z_hi, x).
Axes of the slice: x: 4, y: 4, z: 4 (z_hi: 2, z_lo: 2; z = z_hi * 2 + z_lo), core: 2. Of those that a mesh axis runs over, the one named last changes fastest.
Arguments:
- latent: bfloat16 [8192, 1408], P('dp'), may hold values from -6 to 6
- skip_input: bfloat16 [8192, 1408], P('dp'), may hold values from -6 to 6
- text_tokens: bfloat16 [333, 1024], replicated, may hold values from -6 to 6
- condition: bfloat16 [1408], replicated, may hold values from -5 to 5
- positions: int32 [8192, 2], P('dp'), may hold values from 0 to 31, as said below
- cotangent: bfloat16 [8192, 1408], P('dp'), may hold values from -6 to 6
- skip_w: bfloat16 [2816, 1408], P('tensor'), may hold values from -0.109375 to 0.109375
- skip_gain: float32 [1408], replicated, may hold values from 0.1 to 1.9
- norm1_gain: float32 [1408], replicated, may hold values from 0.1 to 1.9
- mod_w: bfloat16 [1408, 1408], replicated, may hold values from -0.15625 to 0.15625
- qkv_w: bfloat16 [1408, 3, 1408], P(None, None, 'tensor'), may hold values from -0.15625 to 0.15625
- qnorm_gain: float32 [88], replicated, may hold values from 0.1 to 1.9
- knorm_gain: float32 [88], replicated, may hold values from 0.1 to 1.9
- attn_out_w: bfloat16 [1408, 1408], P('tensor'), may hold values from -2.5 to 2.5
- norm2_gain: float32 [1408], replicated, may hold values from 0.1 to 1.9
- cq_w: bfloat16 [1408, 1408], P(None, 'tensor'), may hold values from -0.15625 to 0.15625
- ckv_w: bfloat16 [1024, 2, 1408], P(None, None, 'tensor'), may hold values from -0.1875 to 0.1875
- cqnorm_gain: float32 [88], replicated, may hold values from 0.1 to 1.9
- cknorm_gain: float32 [88], replicated, may hold values from 0.1 to 1.9
- cross_out_w: bfloat16 [1408, 1408], P('tensor'), may hold values from -1.75 to 1.75
- norm3_gain: float32 [1408], replicated, may hold values from 0.1 to 1.9
- fc1_w: bfloat16 [1408, 6144], P(None, 'tensor'), may hold values from -0.15625 to 0.15625
- fc2_w: bfloat16 [6144, 1408], P('tensor'), may hold values from -0.078125 to 0.078125
Outputs:
- output: bfloat16 [8192, 1408], P('dp')
- latent_grad: float32 [8192, 1408], P('dp')
- skip_grad: float32 [8192, 1408], P('dp')
- text_grad: float32 [333, 1024], replicated
- skip_w_grad: float32 [2816, 1408], P('tensor')
- skip_gain_grad: float32 [1408], replicated
- norm1_gain_grad: float32 [1408], replicated
- mod_w_grad: float32 [1408, 1408], replicated
- qkv_w_grad: float32 [1408, 3, 1408], P(None, None, 'tensor')
- qnorm_gain_grad: float32 [88], replicated
- knorm_gain_grad: float32 [88], replicated
- attn_out_w_grad: float32 [1408, 1408], P('tensor')
- norm2_gain_grad: float32 [1408], replicated
- cq_w_grad: float32 [1408, 1408], P(None, 'tensor')
- ckv_w_grad: float32 [1024, 2, 1408], P(None, None, 'tensor')
- cqnorm_gain_grad: float32 [88], replicated
- cknorm_gain_grad: float32 [88], replicated
- cross_out_w_grad: float32 [1408, 1408], P('tensor')
- norm3_gain_grad: float32 [1408], replicated
- fc1_w_grad: float32 [1408, 6144], P(None, 'tensor')
- fc2_w_grad: float32 [6144, 1408], P('tensor')
The draws below stay inside these ranges and needn't reach their ends.
Inputs may be any that keep to these rules, and one draw needn't show every extreme that they name: Within each latent of 1024 consecutive tokens, positions is a permutation of the places of a 32 by 32 grid: column 0 is the row, column 1 the column, each place once.
All inputs are finite; a program needn't handle non-finite values.
Results may differ from the reference program's by a relative error of at most 0.028.
Values may be sent and summed in bfloat16 or wider, within the bound.
No kernel may reach another device: no remote copies, remote signals or barrier semaphores. Data moves between devices by JAX's collectives and lax.ppermute only.
A program may use at most 192 MiB of HBM per device.

```python
import jax
import jax.numpy as jnp
from jax import lax

W = 1408
HEADS = 16
HD = 88
FF = 6144
TW = 1024
TEXT = 333
GRID = 32
TOKENS = 8192


def draw_positions(key, part):
    key = jax.random.fold_in(key, 11)
    latent_keys = jax.random.split(key, TOKENS // (GRID * GRID))
    order = jax.vmap(lambda one_key: jax.random.permutation(one_key, GRID * GRID))(latent_keys).reshape(-1).astype(jnp.int32)
    return jnp.stack([order // GRID, order % GRID], 1).astype(jnp.int32)


def levels(key, shape, cuts, low, top_value):
    def one(dim, parts):
        draws = jax.random.uniform(jax.random.fold_in(jax.random.fold_in(key, 6), dim), (parts,), jnp.float32, low / len(cuts), top_value / len(cuts))
        return jnp.repeat(jnp.exp(draws), shape[dim] // parts).reshape((-1,) + (1,) * (len(shape) - dim - 1))

    factor_of = one(*cuts[0])
    for cut in cuts[1:]:
        factor_of = factor_of * one(*cut)
    return factor_of


def scatter_about(rng, dims, width, most, cuts=(), kind=jnp.bfloat16):
    factor_of = levels(rng, dims, cuts, -0.22, 0.18) if cuts else 1.0
    result = jax.random.normal(rng, dims, jnp.float32) * width * factor_of
    return jnp.minimum(jnp.maximum(result, -most), most).astype(kind)


def setup_inputs(seed: int = 0) -> dict:
    splits = jax.random.split(jax.random.key(seed), 24)
    latent = scatter_about(splits[0], (TOKENS, W), 1.0, 6.0, ((0, 16),))
    skip_input = scatter_about(splits[1], (TOKENS, W), 1.0, 6.0, ((0, 16),))
    text_tokens = scatter_about(splits[2], (TEXT, TW), 1.0, 6.0)
    condition = scatter_about(splits[3], (W,), 1.0, 5.0)
    positions = draw_positions(jax.random.fold_in(splits[23], 71), 0)
    cotangent = scatter_about(splits[5], (TOKENS, W), 1.0, 6.0, ((0, 16),))
    skip_w = scatter_about(splits[6], (2 * W, W), (2 * W) ** -0.5, 0.109375, ((0, 8),))
    skip_gain = jnp.clip(1.0 + 0.18 * jax.random.normal(splits[7], (W,), jnp.float32), 0.1, 1.9)
    norm1_gain = jnp.clip(1.0 + 0.18 * jax.random.normal(splits[8], (W,), jnp.float32), 0.1, 1.9)
    mod_w = scatter_about(splits[9], (W, W), W ** -0.5, 0.15625)
    qkv_w = scatter_about(splits[10], (W, 3, W), W ** -0.5, 0.15625, ((2, 8),))
    qnorm_gain = jnp.clip(1.0 + 0.18 * jax.random.normal(splits[11], (HD,), jnp.float32), 0.1, 1.9)
    knorm_gain = jnp.clip(1.0 + 0.18 * jax.random.normal(splits[12], (HD,), jnp.float32), 0.1, 1.9)
    attn_out_w = scatter_about(splits[13], (W, W), (max(1, 4 * W // (GRID * GRID))) ** -0.5, 2.5, ((0, 8),))
    norm2_gain = jnp.clip(1.0 + 0.18 * jax.random.normal(splits[14], (W,), jnp.float32), 0.1, 1.9)
    cq_w = scatter_about(splits[15], (W, W), W ** -0.5, 0.15625, ((1, 8),))
    ckv_w = scatter_about(splits[16], (TW, 2, W), TW ** -0.5, 0.1875, ((2, 8),))
    cqnorm_gain = jnp.clip(1.0 + 0.18 * jax.random.normal(splits[17], (HD,), jnp.float32), 0.1, 1.9)
    cknorm_gain = jnp.clip(1.0 + 0.18 * jax.random.normal(splits[18], (HD,), jnp.float32), 0.1, 1.9)
    cross_out_w = scatter_about(splits[19], (W, W), (max(1, 3 * W // TEXT)) ** -0.5, 1.75, ((0, 8),))
    norm3_gain = jnp.clip(1.0 + 0.18 * jax.random.normal(splits[20], (W,), jnp.float32), 0.1, 1.9)
    fc1_w = scatter_about(splits[21], (W, FF), W ** -0.5, 0.15625, ((1, 8),))
    fc2_w = scatter_about(splits[22], (FF, W), FF ** -0.5, 0.078125, ((0, 8),))
    return {"latent": latent, "skip_input": skip_input, "text_tokens": text_tokens, "condition": condition, "positions": positions, "cotangent": cotangent, "skip_w": skip_w, "skip_gain": skip_gain, "norm1_gain": norm1_gain, "mod_w": mod_w, "qkv_w": qkv_w, "qnorm_gain": qnorm_gain, "knorm_gain": knorm_gain, "attn_out_w": attn_out_w, "norm2_gain": norm2_gain, "cq_w": cq_w, "ckv_w": ckv_w, "cqnorm_gain": cqnorm_gain, "cknorm_gain": cknorm_gain, "cross_out_w": cross_out_w, "norm3_gain": norm3_gain, "fc1_w": fc1_w, "fc2_w": fc2_w}


@jax.custom_vjp
def low(v):
    return lax.optimization_barrier(v.astype(jnp.bfloat16)).astype(jnp.float32)

@jax.custom_vjp
def low_back(v):
    return v

def low_keep(v):
    return (low(v), None)

def low_pass(kept, grad):
    return (grad,)

def back_keep(v):
    return (v, None)

def back_low(kept, grad):
    return (low(grad),)
low.defvjp(low_keep, low_pass)
low_back.defvjp(back_keep, back_low)

def product(left_side, right_side):
    return jnp.dot(left_side, right_side, precision=lax.Precision.HIGHEST)

def layer_norm(inputs, norm_gain):
    centered = inputs - lax.optimization_barrier(jnp.mean(inputs, -1, keepdims=True))
    variance = lax.optimization_barrier(jnp.mean(centered * centered, -1, keepdims=True))
    return centered * lax.rsqrt(variance + 1e-06) * norm_gain

def rotary_tables(positions, head_dim):
    quarter = head_dim // 4
    frequency = 10000.0 ** (-jnp.arange(quarter).astype(jnp.float32) / quarter)
    angles = positions.astype(jnp.float32)[:, :, None] * frequency
    return (jnp.cos(angles), jnp.sin(angles))

def rotate(inputs, cosine, sine_table):
    token_count, head_count, head_dim = inputs.shape
    pieces = inputs.reshape(token_count, head_count, 2, 2, head_dim // 4)
    first_half = pieces[:, :, :, 0]
    second = pieces[:, :, :, 1]
    cos_wide = cosine[:, None]
    sin_wide = sine_table[:, None]
    turned = jnp.stack([first_half * cos_wide - second * sin_wide, first_half * sin_wide + second * cos_wide], 3)
    return turned.reshape(token_count, head_count, head_dim)

def head_attention(operands):
    query_rows, key_rows, value_rows = operands
    raw_scores = product(query_rows, key_rows.T)
    scores = low_back(raw_scores) * query_rows.shape[-1] ** (-0.5)
    shares = jax.nn.softmax(scores, -1)
    return product(low(shares), value_rows)

def attention(query_rows, key_rows, value_rows):
    mapped = lax.map(jax.checkpoint(head_attention), (query_rows.transpose(1, 0, 2), key_rows.transpose(1, 0, 2), value_rows.transpose(1, 0, 2)))
    return mapped.transpose(1, 0, 2).reshape(query_rows.shape[0], -1)

def latent_attention(operands):
    return attention(operands[0], operands[1], operands[2])

def forward(latent, skip_input, text_tokens, weight_list, silu_cond, cosine, sine_table):
    skip_w, skip_gain, norm1_gain, mod_w, qkv_w, qnorm_gain, knorm_gain, attn_out_w, norm2_gain, cq_w, ckv_w, cqnorm_gain, cknorm_gain, cross_out_w, norm3_gain, fc1_w, fc2_w = weight_list
    token_count, model_width = latent.shape
    latent_len = GRID * GRID
    latent_count = token_count // latent_len
    joined = jnp.concatenate([latent, skip_input], 1)
    merged = low_back(product(low(joined), skip_w))
    hidden = layer_norm(merged, skip_gain)
    shift = product(silu_cond[None], mod_w)[0]
    normed = low(layer_norm(hidden, norm1_gain) + shift)
    projected = low_back(product(normed, qkv_w.reshape(model_width, 3 * model_width))).reshape(token_count, 3, HEADS, HD)
    queries = low(rotate(layer_norm(projected[:, 0], qnorm_gain), cosine, sine_table))
    key_rows = low(rotate(layer_norm(projected[:, 1], knorm_gain), cosine, sine_table))
    value_rows = low(projected[:, 2])
    grouped = (queries.reshape(latent_count, latent_len, HEADS, HD), key_rows.reshape(latent_count, latent_len, HEADS, HD), value_rows.reshape(latent_count, latent_len, HEADS, HD))
    attended = lax.map(latent_attention, grouped).reshape(token_count, model_width)
    mixed = low(low_back(attended))
    hidden = hidden + low_back(product(mixed, attn_out_w))
    normed = low(layer_norm(hidden, norm2_gain))
    cross_raw = low_back(product(normed, cq_w)).reshape(token_count, HEADS, HD)
    cross_q = low(layer_norm(cross_raw, cqnorm_gain))
    text_proj = low_back(product(text_tokens, ckv_w.reshape(TW, 2 * model_width))).reshape(TEXT, 2, HEADS, HD)
    cross_k = low(layer_norm(text_proj[:, 0], cknorm_gain))
    cross_v = low(text_proj[:, 1])
    mixed = low(low_back(attention(cross_q, cross_k, cross_v)))
    hidden = hidden + low_back(product(mixed, cross_out_w))
    normed = low(layer_norm(hidden, norm3_gain))
    pre_act = low_back(product(normed, fc1_w))
    active = low(jax.nn.gelu(pre_act, approximate=True))
    return hidden + low_back(product(active, fc2_w))

def reference(latent, skip_input, text_tokens, condition, positions, cotangent, skip_w, skip_gain, norm1_gain, mod_w, qkv_w, qnorm_gain, knorm_gain, attn_out_w, norm2_gain, cq_w, ckv_w, cqnorm_gain, cknorm_gain, cross_out_w, norm3_gain, fc1_w, fc2_w):
    cosine, sine_table = rotary_tables(positions, HD)
    silu_cond = low(jax.nn.silu(condition.astype(jnp.float32)))
    params = (skip_w, skip_gain, norm1_gain, mod_w, qkv_w, qnorm_gain, knorm_gain, attn_out_w, norm2_gain, cq_w, ckv_w, cqnorm_gain, cknorm_gain, cross_out_w, norm3_gain, fc1_w, fc2_w)
    floats = tuple((weight_item.astype(jnp.float32) for weight_item in params))

    def run_layer(latent_f, skip_f, text_f, weight_list):
        return forward(latent_f, skip_f, text_f, weight_list, silu_cond, cosine, sine_table)
    output, pullback = jax.vjp(run_layer, latent.astype(jnp.float32), skip_input.astype(jnp.float32), text_tokens.astype(jnp.float32), floats)
    grads = pullback(cotangent.astype(jnp.float32))
    weight_grads = grads[3]
    return (output.astype(jnp.bfloat16), grads[0], grads[1], grads[2], weight_grads[0], weight_grads[1], weight_grads[2], weight_grads[3], weight_grads[4], weight_grads[5], weight_grads[6], weight_grads[7], weight_grads[8], weight_grads[9], weight_grads[10], weight_grads[11], weight_grads[12], weight_grads[13], weight_grads[14], weight_grads[15], weight_grads[16])
```

```python
import jax
import jax.numpy as jnp
from jax import lax
from jax.experimental import pallas as pl
from jax.experimental.pallas import tpu as pltpu
from jax.sharding import PartitionSpec as P

BF16 = jnp.bfloat16
F32 = jnp.float32


def layer_norm(inputs, norm_gain):
    centered = inputs - jnp.mean(inputs, -1, keepdims=True)
    variance = jnp.mean(centered * centered, -1, keepdims=True)
    return centered * lax.rsqrt(variance + 1e-06) * norm_gain


def rotary_tables(positions, head_dim):
    quarter = head_dim // 4
    frequency = 10000.0 ** (-jnp.arange(quarter).astype(F32) / quarter)
    angles = positions.astype(F32)[:, :, None] * frequency
    cosine, sine = jnp.cos(angles), jnp.sin(angles)
    cos_wide = jnp.stack([cosine, cosine], 2).reshape(positions.shape[0], head_dim)
    sin_wide = jnp.stack([-sine, sine], 2).reshape(positions.shape[0], head_dim)
    return cos_wide, sin_wide


def left_product(inputs, grads):
    return lax.dot_general(
        inputs, grads, (((0,), (0,)), ((), ())), preferred_element_type=jnp.float32
    )


def right_product(grads, weight):
    return lax.dot_general(
        grads, weight, (((1,), (1,)), ((), ())), preferred_element_type=jnp.float32
    )


def exchange(blocks, axis="tensor"):
    return lax.all_to_all(blocks, axis, 0, 0, tiled=True)


def spread(block, axis="tensor"):
    count = lax.axis_size(axis)
    return jnp.broadcast_to(block[None], (count,) + block.shape)


def after(value, *earlier):
    return lax.optimization_barrier((value,) + earlier)[0]


def pad_rows(rows, multiple):
    extra = -rows.shape[0] % multiple
    return jnp.pad(rows, ((0, extra),) + ((0, 0),) * (rows.ndim - 1))


def permute_gather(block, axis="tensor"):
    count = lax.axis_size(axis)
    place = lax.axis_index(axis)
    out = jnp.zeros((count,) + block.shape, block.dtype)
    out = lax.dynamic_update_index_in_dim(out, block, place, 0)
    for step in range(1, count):
        got = lax.ppermute(block, axis, [(i, i ^ step) for i in range(count)])
        out = lax.dynamic_update_index_in_dim(out, got, place ^ step, 0)
    return out


def dp_slice(rows, unit):
    places = lax.axis_size("dp")
    each = -(-rows.shape[0] // (places * unit)) * unit
    rows = pad_rows(rows, each * places)
    return lax.dynamic_slice_in_dim(rows, lax.axis_index("dp") * each, each, 0)


def dp_routes():
    count = lax.axis_size("dp")
    place = lax.axis_index("dp")
    stages = []
    for low, size in ((0, 2), (1, 4), (3, 2)):
        part = place // (1 << low) % size
        routes = []
        for step in range(1, size):
            route = []
            for source in range(count):
                here = source // (1 << low) % size
                there = (here + step) % size
                route.append((source, source + ((there - here) << low)))
            routes.append(route)
        stages.append((size, part, routes))
    return stages


def scatter_dp(grad):
    for size, part, routes in dp_routes():
        rows = grad.shape[0] // size
        total = lax.dynamic_slice_in_dim(grad, part * rows, rows, 0).astype(F32)
        for step, route in enumerate(routes, 1):
            send = lax.dynamic_slice_in_dim(grad, (part + step) % size * rows, rows, 0)
            total = total + lax.ppermute(send.astype(BF16), "dp", route).astype(F32)
        grad = total
    return grad


def spread_dp(part_rows):
    rows_all = part_rows.astype(BF16)
    for size, part, routes in reversed(dp_routes()):
        rows = rows_all.shape[0]
        out = jnp.zeros((size * rows,) + rows_all.shape[1:], rows_all.dtype)
        out = lax.dynamic_update_slice_in_dim(out, rows_all, part * rows, 0)
        for step, route in enumerate(routes, 1):
            got = lax.ppermute(rows_all, "dp", route)
            out = lax.dynamic_update_slice_in_dim(out, got, (part - step) % size * rows, 0)
        rows_all = out
    return rows_all


def sum_dp(grad):
    return spread_dp(scatter_dp(grad))


def core_swap(block):
    count = lax.axis_size("dp")
    return lax.ppermute(block, "dp", [(i, i ^ 1) for i in range(count)])


def params(limit_mb, grid=0):
    return pltpu.CompilerParams(
        vmem_limit_bytes=limit_mb * 1024 * 1024,
        dimension_semantics=("arbitrary",) * grid if grid else None,
    )


def dot(left, right):
    return lax.dot_general(left, right, (((1,), (0,)), ((), ())), preferred_element_type=F32)


def dot_t(left, right):
    return lax.dot_general(left, right, (((1,), (1,)), ((), ())), preferred_element_type=F32)


def t_dot(left, right):
    return lax.dot_general(left, right, (((0,), (0,)), ((), ())), preferred_element_type=F32)


def norm_parts(rows):
    centered = rows - jnp.mean(rows, -1, keepdims=True)
    scale = lax.rsqrt(jnp.mean(centered * centered, -1, keepdims=True) + 1e-06)
    return centered * scale, scale


def norm_back(unit, scale, gain, grad):
    weighted = grad * gain
    rows = scale * (
        weighted
        - jnp.mean(weighted, -1, keepdims=True)
        - unit * jnp.mean(weighted * unit, -1, keepdims=True)
    )
    return rows, jnp.sum(grad * unit, 0, keepdims=True)


def add_blocks(blocks):
    total = blocks[0].astype(F32)
    for i in range(1, blocks.shape[0]):
        total = total + blocks[i].astype(F32)
    return total


def whole(shape):
    return pl.BlockSpec(shape, lambda *place: (0,) * len(shape))


def struct(shape, kind):
    return jax.ShapeDtypeStruct(shape, kind)


def swap(rows):
    quarter = rows.shape[1] // 4
    cut = [rows[:, i * quarter : (i + 1) * quarter] for i in range(4)]
    return jnp.concatenate([cut[1], cut[0], cut[3], cut[2]], 1)


def first_norms(got, skip_gain, norm1_gain, shift):
    count, rows, width = got.shape

    def kernel(got_ref, skip_ref, gain_ref, shift_ref, merged_ref, hidden_ref, out_ref):
        merged = add_blocks(got_ref)
        merged_ref[...] = merged
        hidden = norm_parts(merged)[0] * skip_ref[...]
        hidden_ref[...] = hidden
        normed = (norm_parts(hidden)[0] * gain_ref[...] + shift_ref[...]).astype(BF16)
        for i in range(count):
            out_ref[i] = normed

    return pl.pallas_call(
        kernel,
        out_shape=(
            struct((rows, width), F32),
            struct((rows, width), F32),
            struct((count, rows, width), BF16),
        ),
        compiler_params=params(32),
        name="first_norms",
    )(got, skip_gain[None], norm1_gain[None], shift[None])


def project(normed, weight, cos_wide, sin_wide, qgain, kgain):
    tokens, width = normed.shape
    each = weight.shape[1] // 3
    head = qgain.shape[0]
    heads = each // head
    block = 256

    def kernel(x_ref, w_ref, cos_ref, sin_ref, qg_ref, kg_ref, raw_ref, q_ref, kv_ref):
        out = dot(x_ref[...], w_ref[...])
        raw_ref[...] = out[:, : 2 * each]
        kv_ref[:, each : 2 * each] = out[:, 2 * each :].astype(BF16)
        cos, sin = cos_ref[...], sin_ref[...]
        for h in range(heads):
            for part, gain_ref, to_ref in ((0, qg_ref, q_ref), (1, kg_ref, kv_ref)):
                start = part * each + h * head
                rows = norm_parts(out[:, start : start + head])[0] * gain_ref[...]
                turned = rows * cos + swap(rows) * sin
                to_ref[:, h * head : (h + 1) * head] = turned.astype(BF16)

    row = lambda size: pl.BlockSpec((block, size), lambda i: (i, 0))
    return pl.pallas_call(
        kernel,
        grid=(tokens // block,),
        in_specs=[
            row(width),
            whole(weight.shape),
            row(head),
            row(head),
            whole((1, head)),
            whole((1, head)),
        ],
        out_specs=(row(2 * each), row(each), row(2 * each)),
        out_shape=(
            struct((tokens, 2 * each), F32),
            struct((tokens, each), BF16),
            struct((tokens, 2 * each), BF16),
        ),
        compiler_params=params(40, 1),
        name="project",
    )(normed, weight, cos_wide, sin_wide, qgain[None], kgain[None])


def self_attention(queries, own, other, out_w, head):
    tokens, each = queries.shape
    heads = each // head
    width = out_w.shape[1]
    keys = 2 * tokens
    scaling = head ** (-0.5)
    block = 256

    def kernel(q_ref, own_ref, other_ref, w_ref, mixed_ref, total_ref, out_ref, kv_ref):
        @pl.when(pl.program_id(0) == 0)
        def _():
            kv_ref[:tokens] = own_ref[...]
            kv_ref[tokens:] = other_ref[...]

        for h in range(heads):
            cut = slice(h * head, (h + 1) * head)
            scores = dot_t(q_ref[:, cut], kv_ref[:, cut]) * scaling
            most = jnp.max(scores, -1, keepdims=True)
            total = most + jnp.log(jnp.sum(jnp.exp(scores - most), -1, keepdims=True))
            total_ref[:, h : h + 1] = total
            shares = jnp.exp(scores - total).astype(BF16)
            mixture = dot(shares, kv_ref[:, each + h * head : each + (h + 1) * head])
            mixed_ref[:, cut] = mixture.astype(BF16)
        out_ref[...] = dot(mixed_ref[...], w_ref[...]).astype(BF16)

    row = lambda size: pl.BlockSpec((block, size), lambda i: (i, 0))
    return pl.pallas_call(
        kernel,
        grid=(tokens // block,),
        in_specs=[row(each), whole(own.shape), whole(other.shape), whole(out_w.shape)],
        out_specs=(row(each), row(heads), row(width)),
        out_shape=(
            struct((tokens, each), BF16),
            struct((tokens, heads), F32),
            struct((tokens, width), BF16),
        ),
        scratch_shapes=[pltpu.VMEM((keys, 2 * each), BF16)],
        compiler_params=params(48, 1),
        name="self_attention",
    )(queries, own, other, out_w)


def self_attention_back(queries, own, other, totals, grad, out_w, head):
    tokens, each = queries.shape
    heads = each // head
    width = out_w.shape[1]
    keys = 2 * tokens
    scaling = head ** (-0.5)
    block = 256
    steps = tokens // block

    def kernel(q_ref, own_ref, other_ref, total_ref, grad_ref, w_ref, dq_ref, down_ref, dother_ref, kv_ref, dkv_ref, dm_ref):
        step = pl.program_id(0)

        @pl.when(step == 0)
        def _():
            kv_ref[:tokens] = own_ref[...]
            kv_ref[tokens:] = other_ref[...]
            dkv_ref[...] = jnp.zeros_like(dkv_ref)

        dm_ref[...] = dot_t(grad_ref[...], w_ref[...]).astype(BF16)
        for h in range(heads):
            cut = slice(h * head, (h + 1) * head)
            vcut = slice(each + h * head, each + (h + 1) * head)
            rows, grads = q_ref[:, cut], dm_ref[:, cut]
            keys_h, values_h = kv_ref[:, cut], kv_ref[:, vcut]
            shares = jnp.exp(dot_t(rows, keys_h) * scaling - total_ref[:, h : h + 1])
            dshares = dot_t(grads, values_h)
            dkv_ref[:, vcut] += t_dot(shares.astype(BF16), grads)
            weighted = jnp.sum(shares * dshares, -1, keepdims=True)
            dscores = (shares * (dshares - weighted) * scaling).astype(BF16)
            dq_ref[:, cut] = dot(dscores, keys_h)
            dkv_ref[:, cut] += t_dot(dscores, rows)

        @pl.when(step == steps - 1)
        def _():
            down_ref[...] = dkv_ref[:tokens]
            dother_ref[...] = dkv_ref[tokens:].astype(BF16)

    row = lambda size: pl.BlockSpec((block, size), lambda i: (i, 0))
    return pl.pallas_call(
        kernel,
        grid=(steps,),
        in_specs=[
            row(each),
            whole(own.shape),
            whole(other.shape),
            row(heads),
            row(width),
            whole(out_w.shape),
        ],
        out_specs=(row(each), whole(own.shape), whole(own.shape)),
        out_shape=(
            struct((tokens, each), F32),
            struct(own.shape, F32),
            struct(own.shape, BF16),
        ),
        scratch_shapes=[
            pltpu.VMEM((keys, 2 * each), BF16),
            pltpu.VMEM((keys, 2 * each), F32),
            pltpu.VMEM((block, each), BF16),
        ],
        compiler_params=params(48, 1),
        name="self_attention_back",
    )(queries, own, other, totals, grad, out_w)


def project_back(raw, cos_wide, sin_wide, qgain, kgain, dq, down, arrived, weight):
    tokens = raw.shape[0]
    each = raw.shape[1] // 2
    head = qgain.shape[0]
    heads = each // head
    width = weight.shape[0]
    block = 256

    def kernel(raw_ref, cos_ref, sin_ref, qg_ref, kg_ref, dq_ref, down_ref, arr_ref, w_ref, dp_ref, out_ref, dqg_ref, dkg_ref):
        @pl.when(pl.program_id(0) == 0)
        def _():
            dqg_ref[...] = jnp.zeros_like(dqg_ref)
            dkg_ref[...] = jnp.zeros_like(dkg_ref)

        cos, sin = cos_ref[...], sin_ref[...]
        dkv = down_ref[...] + arr_ref[...].astype(F32)
        dp_ref[:, 2 * each :] = dkv[:, each:].astype(BF16)
        for h in range(heads):
            cut = slice(h * head, (h + 1) * head)
            for part, gain_ref, dgain_ref in ((0, qg_ref, dqg_ref), (1, kg_ref, dkg_ref)):
                turned = dq_ref[:, cut] if part == 0 else dkv[:, cut]
                grad = turned * cos - swap(turned) * sin
                start = part * each + h * head
                unit, scale = norm_parts(raw_ref[:, start : start + head])
                rows, dgain = norm_back(unit, scale, gain_ref[...], grad)
                dgain_ref[...] += dgain
                dp_ref[:, start : start + head] = rows.astype(BF16)
        out_ref[...] = dot_t(dp_ref[...], w_ref[...]).astype(BF16)

    row = lambda size: pl.BlockSpec((block, size), lambda i: (i, 0))
    return pl.pallas_call(
        kernel,
        grid=(tokens // block,),
        in_specs=[
            row(2 * each),
            row(head),
            row(head),
            whole((1, head)),
            whole((1, head)),
            row(each),
            row(2 * each),
            row(2 * each),
            whole(weight.shape),
        ],
        out_specs=(row(3 * each), row(width), whole((1, head)), whole((1, head))),
        out_shape=(
            struct((tokens, 3 * each), BF16),
            struct((tokens, width), BF16),
            struct((1, head), F32),
            struct((1, head), F32),
        ),
        compiler_params=params(40, 1),
        name="project_back",
    )(raw, cos_wide, sin_wide, qgain[None], kgain[None], dq, down, arrived, weight)


def text_scores(rows, keys_h, scaling, count):
    scores = dot_t(rows, keys_h) * scaling
    place = lax.broadcasted_iota(jnp.int32, scores.shape, 1)
    scores = jnp.where(place < count, scores, -1e30)
    most = jnp.max(scores, -1, keepdims=True)
    total = most + jnp.log(jnp.sum(jnp.exp(scores - most), -1, keepdims=True))
    return jnp.exp(scores - total)


def cross_layer(got, hidden_zero, pack, text, gains, head_gain, text_count):
    count, rows, width = got.shape
    head = head_gain.shape[0]
    each = text.shape[2] // 2
    heads = each // head
    scaling = head ** (-0.5)
    slices, _, deep, _ = pack.shape

    def kernel(got_ref, h0_ref, pack_ref, text_ref, g2_ref, g3_ref, hg_ref, h1_ref, h2_ref, n2_ref, raw_ref, mixed_ref, out_ref):
        step = pl.program_id(0)

        @pl.when(step == 0)
        def _():
            hidden = h0_ref[...] + add_blocks(got_ref)
            h1_ref[...] = hidden
            h2_ref[...] = hidden
            n2_ref[...] = (norm_parts(hidden)[0] * g2_ref[...]).astype(BF16)

        weights = pack_ref[:, 0].reshape(slices * deep, width)
        raw = dot_t(n2_ref[...], weights[each : 2 * each])
        raw_ref[0] = raw
        for h in range(heads):
            cut = slice(h * head, (h + 1) * head)
            vcut = slice(each + h * head, each + (h + 1) * head)
            queries = (norm_parts(raw[:, cut])[0] * hg_ref[...]).astype(BF16)
            shares = text_scores(queries, text_ref[0, :, cut], scaling, text_count)
            mixed_ref[0, :, cut] = dot(shares.astype(BF16), text_ref[0, :, vcut]).astype(BF16)
        h2_ref[...] += dot(mixed_ref[0], weights[:each])

        @pl.when(step == count - 1)
        def _():
            normed = (norm_parts(h2_ref[...])[0] * g3_ref[...]).astype(BF16)
            for i in range(count):
                out_ref[i] = normed

    one = lambda size: pl.BlockSpec((1, rows, size), lambda i: (i, 0, 0))
    return pl.pallas_call(
        kernel,
        grid=(count,),
        in_specs=[
            whole(got.shape),
            whole((rows, width)),
            pl.BlockSpec((slices, 1, deep, width), lambda i: (0, i, 0, 0)),
            pl.BlockSpec((1,) + text.shape[1:], lambda i: (i, 0, 0)),
            whole((1, width)),
            whole((1, width)),
            whole((1, head)),
        ],
        out_specs=(
            whole((rows, width)),
            whole((rows, width)),
            whole((rows, width)),
            one(each),
            one(each),
            whole(got.shape),
        ),
        out_shape=(
            struct((rows, width), F32),
            struct((rows, width), F32),
            struct((rows, width), BF16),
            struct((count, rows, each), F32),
            struct((count, rows, each), BF16),
            struct(got.shape, BF16),
        ),
        compiler_params=params(40, 1),
        name="cross_layer",
    )(got, hidden_zero, pack, text, gains[0][None], gains[1][None], head_gain[None])


def cross_layer_back(got, cot, hidden_one, hidden_two, pack, text, raw, mixed, gains, head_gain, text_count):
    count, rows, width = got.shape
    head = head_gain.shape[0]
    each = text.shape[2] // 2
    heads = each // head
    scaling = head ** (-0.5)
    slices, _, deep, _ = pack.shape

    def kernel(got_ref, cot_ref, h1_ref, h2_ref, pack_ref, text_ref, raw_ref, mixed_ref, g2_ref, g3_ref, hg_ref,
               res_ref, d2_ref, by_ref, out_ref, dg2_ref, dg3_ref, dhg_ref, acc_ref):
        step = pl.program_id(0)

        @pl.when(step == 0)
        def _():
            unit, scale = norm_parts(h2_ref[...])
            grad, dgain = norm_back(unit, scale, g3_ref[...], add_blocks(got_ref))
            dg3_ref[...] = dgain
            residual = cot_ref[...].astype(F32) + grad
            res_ref[...] = residual
            d2_ref[...] = residual.astype(BF16)
            acc_ref[...] = jnp.zeros_like(acc_ref)
            dhg_ref[...] = jnp.zeros_like(dhg_ref)

        weights = pack_ref[:, 0].reshape(slices * deep, width)
        by_ref[0, :, each : 2 * each] = mixed_ref[0]
        by_ref[0, :, 3 * each :] = dot_t(d2_ref[...], weights[:each]).astype(BF16)
        for h in range(heads):
            cut = slice(h * head, (h + 1) * head)
            vcut = slice(each + h * head, each + (h + 1) * head)
            unit, scale = norm_parts(raw_ref[0, :, cut])
            queries = (unit * hg_ref[...]).astype(BF16)
            by_ref[0, :, 2 * each + h * head : 2 * each + (h + 1) * head] = queries
            grads = by_ref[0, :, 3 * each + h * head : 3 * each + (h + 1) * head]
            keys_h = text_ref[0, :, cut]
            shares = text_scores(queries, keys_h, scaling, text_count)
            dshares = dot_t(grads, text_ref[0, :, vcut])
            weighted = jnp.sum(shares * dshares, -1, keepdims=True)
            dscores = (shares * (dshares - weighted) * scaling).astype(BF16)
            draw, dgain = norm_back(unit, scale, hg_ref[...], dot(dscores, keys_h))
            dhg_ref[...] += dgain
            by_ref[0, :, cut] = draw.astype(BF16)
        acc_ref[...] += dot(by_ref[0, :, :each], weights[each : 2 * each])

        @pl.when(step == count - 1)
        def _():
            unit, scale = norm_parts(h1_ref[...])
            grad, dgain = norm_back(unit, scale, g2_ref[...], acc_ref[...])
            dg2_ref[...] = dgain
            residual = res_ref[...] + grad
            res_ref[...] = residual
            rounded = residual.astype(BF16)
            for i in range(count):
                out_ref[i] = rounded

    one = lambda size: pl.BlockSpec((1, rows, size), lambda i: (i, 0, 0))
    return pl.pallas_call(
        kernel,
        grid=(count,),
        in_specs=[
            whole(got.shape),
            whole((rows, width)),
            whole((rows, width)),
            whole((rows, width)),
            pl.BlockSpec((slices, 1, deep, width), lambda i: (0, i, 0, 0)),
            pl.BlockSpec((1,) + text.shape[1:], lambda i: (i, 0, 0)),
            one(each),
            one(each),
            whole((1, width)),
            whole((1, width)),
            whole((1, head)),
        ],
        out_specs=(
            whole((rows, width)),
            whole((rows, width)),
            one(4 * each),
            whole(got.shape),
            whole((1, width)),
            whole((1, width)),
            whole((1, head)),
        ),
        out_shape=(
            struct((rows, width), F32),
            struct((rows, width), BF16),
            struct((count, rows, 4 * each), BF16),
            struct(got.shape, BF16),
            struct((1, width), F32),
            struct((1, width), F32),
            struct((1, head), F32),
        ),
        scratch_shapes=[pltpu.VMEM((rows, width), F32)],
        compiler_params=params(40, 1),
        name="cross_layer_back",
    )(got, cot, hidden_one, hidden_two, pack, text, raw, mixed, gains[0][None], gains[1][None], head_gain[None])


def text_back(by_head, text, head, text_count):
    tokens = by_head.shape[0]
    each = text.shape[1] // 2
    heads = each // head
    scaling = head ** (-0.5)

    def kernel(by_ref, text_ref, out_ref):
        for h in range(heads):
            cut = slice(h * head, (h + 1) * head)
            vcut = slice(each + h * head, each + (h + 1) * head)
            queries = by_ref[:, 2 * each + h * head : 2 * each + (h + 1) * head]
            grads = by_ref[:, 3 * each + h * head : 3 * each + (h + 1) * head]
            shares = text_scores(queries, text_ref[:, cut], scaling, text_count)
            dshares = dot_t(grads, text_ref[:, vcut])
            weighted = jnp.sum(shares * dshares, -1, keepdims=True)
            dscores = (shares * (dshares - weighted) * scaling).astype(BF16)
            out_ref[:, cut] = t_dot(dscores, queries).astype(BF16)
            out_ref[:, vcut] = t_dot(shares.astype(BF16), grads).astype(BF16)

    return pl.pallas_call(
        kernel,
        out_shape=struct(text.shape, BF16),
        compiler_params=params(40),
        name="text_back",
    )(by_head, text)


def last_norms(got, hidden_zero, merged, residual, gains, rows_two, rows_three, misc):
    count, rows, width = got.shape

    def kernel(got_ref, h0_ref, merged_ref, res_ref, g1_ref, gs_ref, two_ref, three_ref, misc_ref, out_ref):
        grad = add_blocks(got_ref)
        shift_grad = jnp.sum(grad, 0, keepdims=True)
        unit, scale = norm_parts(h0_ref[...])
        step, norm1_grad = norm_back(unit, scale, g1_ref[...], grad)
        residual = res_ref[...] + step
        unit, scale = norm_parts(merged_ref[...])
        step, skip_grad = norm_back(unit, scale, gs_ref[...], residual)
        small = [skip_grad, norm1_grad, two_ref[...], three_ref[...], shift_grad, misc_ref[...]]
        small = jnp.concatenate(small + [jnp.zeros((16 - len(small), width), F32)], 0).astype(BF16)
        step = step.astype(BF16)
        for i in range(count):
            out_ref[i, :rows] = step
            out_ref[i, rows:] = small

    return pl.pallas_call(
        kernel,
        out_shape=struct((count, rows + 16, width), BF16),
        compiler_params=params(32),
        name="last_norms",
    )(got, hidden_zero, merged, residual, gains[0][None], gains[1][None], rows_two, rows_three, misc)


def feed_forward(normed, cot, fc1_w, fc2_w):
    tokens, width = normed.shape
    hidden = fc1_w.shape[1]
    block = 256
    steps = hidden // block
    root = (2 / 3.141592653589793) ** 0.5

    def kernel(x_ref, cot_ref, w1_ref, w2_ref, active_ref, pre_ref, out_ref, acc_ref):
        step = pl.program_id(0)
        pre = dot(x_ref[...], w1_ref[...])
        square = pre * pre
        bent = jnp.tanh(root * pre * (1 + 0.044715 * square))
        half = 0.5 * (1 + bent)
        active_ref[...] = (pre * half).astype(BF16)
        slope = half + 0.5 * pre * (1 - bent * bent) * root * (1 + 3 * 0.044715 * square)
        pre_ref[...] = (dot_t(cot_ref[...], w2_ref[...]) * slope).astype(BF16)
        back = dot_t(pre_ref[...], w1_ref[...])

        @pl.when(step == 0)
        def _():
            acc_ref[...] = back

        @pl.when(step > 0)
        def _():
            acc_ref[...] += back

        @pl.when(step == steps - 1)
        def _():
            out_ref[...] = acc_ref[...].astype(BF16)

    return pl.pallas_call(
        kernel,
        grid=(steps,),
        in_specs=[
            whole(normed.shape),
            whole(cot.shape),
            pl.BlockSpec((width, block), lambda i: (0, i)),
            pl.BlockSpec((block, width), lambda i: (i, 0)),
        ],
        out_specs=(
            pl.BlockSpec((tokens, block), lambda i: (0, i)),
            pl.BlockSpec((tokens, block), lambda i: (0, i)),
            whole((tokens, width)),
        ),
        out_shape=(
            struct((tokens, hidden), BF16),
            struct((tokens, hidden), BF16),
            struct((tokens, width), BF16),
        ),
        scratch_shapes=[pltpu.VMEM((tokens, width), F32)],
        compiler_params=params(48, 1),
        name="feed_forward",
    )(normed, cot, fc1_w, fc2_w)


def local(
    latent,
    skip_input,
    text_tokens,
    condition,
    positions,
    cotangent,
    skip_w,
    skip_gain,
    norm1_gain,
    mod_w,
    qkv_w,
    qnorm_gain,
    knorm_gain,
    attn_out_w,
    norm2_gain,
    cq_w,
    ckv_w,
    cqnorm_gain,
    cknorm_gain,
    cross_out_w,
    norm3_gain,
    fc1_w,
    fc2_w,
):
    token_count, model_width = latent.shape
    head_dim = qnorm_gain.shape[0]
    local_width = cq_w.shape[1]
    local_heads = local_width // head_dim
    slab_width = skip_w.shape[0]
    hidden_width = fc1_w.shape[1]
    text_count, text_width = text_tokens.shape
    tensor_place = lax.axis_index("tensor")
    tensor_count = lax.axis_size("tensor")
    dp_count = lax.axis_size("dp")
    part_count = token_count // tensor_count
    blocks = (tensor_count, part_count, model_width)

    def own_rows(rows):
        return lax.dynamic_slice_in_dim(rows, tensor_place * part_count, part_count, 0)

    early_rows = 16 * dp_count * (-(-2 * local_width // (16 * dp_count))) - 2 * local_width
    cross_share = dp_slice(jnp.concatenate([cross_out_w, cq_w.T, skip_w[:early_rows]], 0), 16)
    cross_pack = lax.all_gather(permute_gather(cross_share), "dp", axis=0, tiled=False)
    skip_share = dp_slice(skip_w[early_rows:], 16)

    joined = jnp.concatenate([latent, skip_input], 1)
    joined_part = lax.dynamic_slice_in_dim(joined, tensor_place * slab_width, slab_width, 1)
    partial = jnp.dot(joined_part, skip_w, preferred_element_type=F32).astype(BF16)
    got = exchange(partial.reshape(blocks))
    silu_cond = jax.nn.silu(condition.astype(F32)).astype(BF16)
    shift = jnp.dot(silu_cond[None], mod_w, preferred_element_type=F32)[0]
    merged, hidden_zero, normed_out = first_norms(got, skip_gain, norm1_gain, shift)
    normed_one = exchange(normed_out).reshape(token_count, model_width)

    ckv_flat = ckv_w.reshape(text_width, 2 * local_width)
    text_proj = jnp.dot(text_tokens, ckv_flat, preferred_element_type=F32)
    text_proj = text_proj.reshape(text_count, 2, local_heads, head_dim)
    cross_key, cross_key_back = jax.vjp(layer_norm, text_proj[:, 0], cknorm_gain)
    text_pair = jnp.concatenate(
        [
            cross_key.astype(BF16).reshape(text_count, local_width),
            text_proj[:, 1].astype(BF16).reshape(text_count, local_width),
        ],
        1,
    )
    text_pair = pad_rows(text_pair, 16)
    text_pairs = exchange(spread(after(text_pair, normed_one)))

    qkv_flat = qkv_w.reshape(model_width, 3 * local_width)
    cos_wide, sin_wide = rotary_tables(positions, head_dim)
    raw, queries, own_pair = project(
        normed_one, qkv_flat, cos_wide, sin_wide, qnorm_gain, knorm_gain
    )
    other_pair = core_swap(own_pair)
    mixed_one, totals, partial = self_attention(
        queries, own_pair, other_pair, attn_out_w, head_dim
    )
    got = exchange(after(partial, text_pairs).reshape(blocks))
    cross_gains = (norm2_gain, norm3_gain)
    hidden_one, hidden_two, normed_two, cross_raw, mixed_two, normed_out = cross_layer(
        got, hidden_zero, cross_pack, text_pairs, cross_gains, cqnorm_gain, text_count
    )
    normed_three = exchange(normed_out).reshape(token_count, model_width)
    slow_rows = lax.all_gather(
        jnp.concatenate([after(normed_two, cross_pack), skip_share], 0), "tensor", axis=0, tiled=False
    )
    normed_two_all = slow_rows[:, :part_count].reshape(token_count, model_width)
    skip_pack = lax.all_gather(slow_rows[:, part_count:], "dp", axis=0, tiled=False)

    active, pre_grad, partial = feed_forward(normed_three, cotangent, fc1_w, fc2_w)
    got = exchange(partial.reshape(blocks))
    fc_grads = sum_dp(
        jnp.concatenate([left_product(pre_grad, normed_three), left_product(active, cotangent)], 0)
    )
    fc1_grad = fc_grads[:hidden_width].T.astype(F32)
    fc2_grad = fc_grads[hidden_width:].astype(F32)

    residual, out_grad_two, by_head, out_spread, norm2_grad, norm3_grad, cqnorm_grad = (
        cross_layer_back(
            got,
            own_rows(cotangent),
            hidden_one,
            hidden_two,
            cross_pack,
            text_pairs,
            cross_raw,
            mixed_two,
            cross_gains,
            cqnorm_gain,
            text_count,
        )
    )
    out_grad_one = exchange(out_spread).reshape(token_count, model_width)
    out_grad_two = lax.all_gather(out_grad_two, "tensor", axis=0, tiled=True)
    query_grad, own_grad, other_grad = self_attention_back(
        queries, own_pair, other_pair, totals, out_grad_one, attn_out_w, head_dim
    )
    arrived = core_swap(other_grad)
    projected_grad, partial, qnorm_grad, knorm_grad = project_back(
        raw,
        cos_wide,
        sin_wide,
        qnorm_gain,
        knorm_gain,
        query_grad,
        own_grad,
        arrived,
        qkv_flat,
    )
    got = exchange(partial.reshape(blocks))
    misc = jnp.concatenate([qnorm_grad, knorm_grad, cqnorm_grad], 1)
    misc = jnp.pad(misc, ((0, 0), (0, model_width - misc.shape[1])))
    merged_out = last_norms(
        got,
        hidden_zero,
        merged,
        residual,
        (norm1_gain, skip_gain),
        norm2_grad,
        norm3_grad,
        misc,
    )
    merged_small = exchange(merged_out)
    merged_grad = merged_small[:, :part_count].reshape(token_count, model_width)
    small = jnp.sum(merged_small[:, part_count:].astype(F32), 0)

    by_head = exchange(after(by_head, out_grad_one)).reshape(token_count, 4 * local_width)
    text_grads = text_back(by_head, text_pair, head_dim, text_count)
    late_grads = [
        left_product(projected_grad, normed_one),
        left_product(mixed_one, out_grad_one),
        left_product(by_head[:, :local_width], normed_two_all),
        left_product(by_head[:, local_width : 2 * local_width], out_grad_two),
        text_grads.reshape(-1, 8 * local_width),
    ]
    late_grads = sum_dp(pad_rows(jnp.concatenate(late_grads, 0), 16 * dp_count))
    qkv_rows = 3 * local_width
    qkv_grad = late_grads[:qkv_rows].T.astype(F32).reshape(model_width, 3, local_width)
    attn_out_grad, cq_grad, cross_out_grad = [
        late_grads[qkv_rows + i * local_width : qkv_rows + (i + 1) * local_width].astype(F32)
        for i in range(3)
    ]
    cq_grad = cq_grad.T
    text_rows = text_pair.shape[0] // 4
    text_grads = late_grads[qkv_rows + 3 * local_width :][:text_rows]
    text_grads = text_grads.reshape(-1, 2 * local_width)[:text_count].astype(F32)
    text_grads = text_grads.reshape(text_count, 2, local_heads, head_dim)

    skip_w_grad = left_product(joined_part, merged_grad)
    skip_small = sum_dp(pad_rows(jnp.concatenate([skip_w_grad, small], 0), 16 * dp_count))
    skip_w_grad = skip_small[:slab_width].astype(F32)
    small = skip_small[slab_width:].astype(F32)
    skip_gain_grad, norm1_grad, norm2_grad, norm3_grad, mod_vector = [small[i] for i in range(5)]
    qnorm_grad, knorm_grad, cqnorm_grad = [
        small[5, i * head_dim : (i + 1) * head_dim] for i in range(3)
    ]
    early_slices = early_rows // cross_share.shape[0]
    late_slices = (slab_width - early_rows) // skip_share.shape[0]
    skip_whole = jnp.concatenate(
        [
            pack.transpose(1, 0, 2, 3).reshape(tensor_count, -1, model_width)
            for pack in (cross_pack[-early_slices:], skip_pack[:late_slices])
        ],
        1,
    ).reshape(tensor_count * slab_width, model_width)
    latent_grad = right_product(merged_grad, skip_whole[:model_width])
    skip_grad = right_product(merged_grad, skip_whole[model_width:])

    key_raw_grad, cknorm_part = cross_key_back(text_grads[:, 0])
    text_proj_grad = (
        jnp.stack([key_raw_grad, text_grads[:, 1]], 1)
        .astype(BF16)
        .reshape(text_count, 2 * local_width)
    )
    ckv_grad = left_product(text_tokens, text_proj_grad).reshape(text_width, 2, local_width)
    text_part = right_product(text_proj_grad, ckv_flat)
    text_part = jnp.concatenate(
        [text_part, jnp.pad(cknorm_part, (0, text_width - head_dim))[None]], 0
    )
    text_part = pad_rows(text_part, 16 * tensor_count).astype(BF16)
    text_part = exchange(text_part.reshape(tensor_count, -1, text_width))
    text_part = jnp.sum(text_part.astype(F32), 0).astype(BF16)
    text_part = exchange(spread(text_part)).reshape(-1, text_width)
    text_grad = text_part[:text_count].astype(F32)
    cknorm_grad = text_part[text_count, :head_dim].astype(F32)

    partial = jnp.dot(active, fc2_w, preferred_element_type=F32).astype(BF16)
    got = exchange(after(partial, by_head).reshape(blocks))
    output = (hidden_two + jnp.sum(got.astype(F32), 0)).astype(BF16)
    output = lax.all_gather(output, "tensor", axis=0, tiled=True)
    mod_grad = silu_cond.astype(F32)[:, None] * mod_vector[None, :]
    return (
        output,
        latent_grad,
        skip_grad,
        text_grad,
        skip_w_grad,
        skip_gain_grad,
        norm1_grad,
        mod_grad,
        qkv_grad,
        qnorm_grad,
        knorm_grad,
        attn_out_grad,
        norm2_grad,
        cq_grad,
        ckv_grad,
        cqnorm_grad,
        cknorm_grad,
        cross_out_grad,
        norm3_grad,
        fc1_grad,
        fc2_grad,
    )


def solution(mesh):
    placed = (
        P("dp", None),
        P("dp", None),
        P(),
        P(),
        P("dp", None),
        P("dp", None),
        P("tensor", None),
        P(),
        P(),
        P(),
        P(None, None, "tensor"),
        P(),
        P(),
        P("tensor", None),
        P(),
        P(None, "tensor"),
        P(None, None, "tensor"),
        P(),
        P(),
        P("tensor", None),
        P(),
        P(None, "tensor"),
        P("tensor", None),
    )
    return jax.shard_map(
        local,
        mesh=mesh,
        in_specs=placed,
        out_specs=(
            P("dp", None),
            P("dp", None),
            P("dp", None),
            P(),
            P("tensor", None),
            P(),
            P(),
            P(),
            P(None, None, "tensor"),
            P(),
            P(),
            P("tensor", None),
            P(),
            P(None, "tensor"),
            P(None, None, "tensor"),
            P(),
            P(),
            P("tensor", None),
            P(),
            P(None, "tensor"),
            P("tensor", None),
        ),
        check_vma=False,
    )
```

```python
import jax
import jax.numpy as jnp
from jax import lax
from jax.experimental import pallas as pl
from jax.experimental.pallas import tpu as pltpu
from jax.sharding import PartitionSpec as P

BF16 = jnp.bfloat16
F32 = jnp.float32


def layer_norm(inputs, norm_gain):
    centered = inputs - jnp.mean(inputs, -1, keepdims=True)
    variance = jnp.mean(centered * centered, -1, keepdims=True)
    return centered * lax.rsqrt(variance + 1e-06) * norm_gain


def rotary_tables(positions, head_dim):
    quarter = head_dim // 4
    frequency = 10000.0 ** (-jnp.arange(quarter).astype(F32) / quarter)
    angles = positions.astype(F32)[:, :, None] * frequency
    cosine, sine = jnp.cos(angles), jnp.sin(angles)
    cos_wide = jnp.stack([cosine, cosine], 2).reshape(positions.shape[0], head_dim)
    sin_wide = jnp.stack([-sine, sine], 2).reshape(positions.shape[0], head_dim)
    return cos_wide, sin_wide


def left_product(inputs, grads):
    return lax.dot_general(
        inputs, grads, (((0,), (0,)), ((), ())), preferred_element_type=jnp.float32
    )


def right_product(grads, weight):
    return lax.dot_general(
        grads, weight, (((1,), (1,)), ((), ())), preferred_element_type=jnp.float32
    )


def exchange(blocks, axis="tensor"):
    return lax.all_to_all(blocks, axis, 0, 0, tiled=True)


def spread(block, axis="tensor"):
    count = lax.axis_size(axis)
    return jnp.broadcast_to(block[None], (count,) + block.shape)


def after(value, *earlier):
    return lax.optimization_barrier((value,) + earlier)[0]


def after_all(values, *earlier):
    return lax.optimization_barrier((tuple(values),) + earlier)[0]


def pad_rows(rows, multiple):
    extra = -rows.shape[0] % multiple
    return jnp.pad(rows, ((0, extra),) + ((0, 0),) * (rows.ndim - 1))


def ring_route(step):
    count = lax.axis_size("tensor")
    ring = count // 2
    return [(i, i // ring * ring + (i + step) % ring) for i in range(count)]


def ring_gather(block):
    ring = lax.axis_size("tensor") // 2
    got = {k: lax.ppermute(block, "tensor", ring_route(k)) for k in (1, 3, 2)}
    return [block] + [got[k] for k in range(1, ring)]


def ring_scatter(blocks):
    got = {k: lax.ppermute(blocks[k], "tensor", ring_route(-k)) for k in (1, 3, 2)}
    return [blocks[0]] + [got[k] for k in range(1, len(blocks))]


def place_blocks(blocks, half_blocks):
    ring = len(blocks)
    place = lax.axis_index("tensor")
    ring_place, half = place % ring, place // ring
    rows = blocks[0].shape[0]
    out = jnp.zeros((2 * ring * rows,) + blocks[0].shape[1:], blocks[0].dtype)
    for k in range(ring):
        at_ring = (ring_place - k) % ring
        for which, block in ((half, blocks[k]), (1 - half, half_blocks[k])):
            out = lax.dynamic_update_slice_in_dim(out, block, (which * ring + at_ring) * rows, 0)
    return out


def half_swap(block):
    count = lax.axis_size("tensor")
    return lax.ppermute(block, "tensor", [(i, (i + count // 2) % count) for i in range(count)])


def core_swap(block):
    count = lax.axis_size("dp")
    return lax.ppermute(block, "dp", [(i, i ^ 1) for i in range(count)])


def dp_slice(rows, unit):
    places = lax.axis_size("dp")
    each = -(-rows.shape[0] // (places * unit)) * unit
    rows = pad_rows(rows, each * places)
    return lax.dynamic_slice_in_dim(rows, lax.axis_index("dp") * each, each, 0)


def dp_routes():
    count = lax.axis_size("dp")
    place = lax.axis_index("dp")
    stages = []
    for low, size in ((0, 2), (1, 4), (3, 2)):
        part = place // (1 << low) % size
        routes = []
        for step in range(1, size):
            route = []
            for source in range(count):
                here = source // (1 << low) % size
                there = (here + step) % size
                route.append((source, source + ((there - here) << low)))
            routes.append(route)
        stages.append((size, part, routes))
    return stages


def join(*values):
    return lax.optimization_barrier(values)


def far_swap(block):
    dp_count, count = lax.axis_size("dp"), lax.axis_size("tensor")
    route = [
        (d * count + t, (d ^ 1) * count + (t + count // 2) % count)
        for d in range(dp_count)
        for t in range(count)
    ]
    return lax.ppermute(block, ("dp", "tensor"), route)


def low_swap(block):
    count = lax.axis_size("dp")
    return lax.ppermute(block, "dp", [(i, i ^ 8) for i in range(count)])


def low_groups():
    return [list(range(8)), list(range(8, 16))]


def scatter_low(rows):
    return lax.psum_scatter(
        rows, "dp", scatter_dimension=0, tiled=True, axis_index_groups=low_groups()
    )


def gather_low(rows):
    return lax.all_gather(rows, "dp", axis=0, tiled=False, axis_index_groups=low_groups())


def scatter_stage(stage, grads):
    size, part, routes = dp_routes()[stage]
    rows = grads.shape[1] // size
    cut = lambda place: lax.dynamic_slice_in_dim(grads, place * rows, rows, 1)
    total = cut(part).astype(F32)
    for step, route in enumerate(routes, 1):
        send = cut((part + step) % size).astype(BF16)
        total = total + lax.ppermute(send, "dp", route).astype(F32)
    return total


def half_sum(own, other):
    return own.astype(F32) + half_swap(other.astype(BF16)).astype(F32)


VMEM_LIMIT = 60 * 1024 * 1024


def cost(micros):
    return pl.CostEstimate(flops=0, transcendentals=0, bytes_accessed=int(micros * 3.3e6))


def call(kernel, micros, outs, ins, name, grid=None, in_specs=None, out_specs=None, scratch=()):
    extra = {}
    if grid:
        extra = {"grid": grid, "in_specs": in_specs, "out_specs": out_specs}
    return pl.pallas_call(
        kernel,
        out_shape=outs,
        scratch_shapes=scratch,
        compiler_params=pltpu.CompilerParams(
            vmem_limit_bytes=VMEM_LIMIT,
            dimension_semantics=("arbitrary",) * len(grid) if grid else None,
        ),
        cost_estimate=cost(micros),
        name=name,
        **extra,
    )(*ins)


def dot(left, right):
    return lax.dot_general(left, right, (((1,), (0,)), ((), ())), preferred_element_type=F32)


def dot_t(left, right):
    return lax.dot_general(left, right, (((1,), (1,)), ((), ())), preferred_element_type=F32)


def t_dot(left, right):
    return lax.dot_general(left, right, (((0,), (0,)), ((), ())), preferred_element_type=F32)


def norm_parts(rows):
    centered = rows - jnp.mean(rows, -1, keepdims=True)
    scale = lax.rsqrt(jnp.mean(centered * centered, -1, keepdims=True) + 1e-06)
    return centered * scale, scale


def norm_back(unit, scale, gain, grad):
    weighted = grad * gain
    rows = scale * (
        weighted
        - jnp.mean(weighted, -1, keepdims=True)
        - unit * jnp.mean(weighted * unit, -1, keepdims=True)
    )
    return rows, jnp.sum(grad * unit, 0, keepdims=True)


def add_all(refs):
    total = refs[0][...].astype(F32)
    for ref in refs[1:]:
        total = total + ref[...].astype(F32)
    return total


def stack(parts):
    return jnp.concatenate(parts, 0)


HBM = pl.BlockSpec(memory_space=pltpu.HBM)


def load_blocks(refs, x_ref, sems):
    rows = x_ref.shape[0] // len(refs)
    copies = [
        pltpu.make_async_copy(
            ref.at[pl.ds(0, rows)], x_ref.at[pl.ds(i * rows, rows)], sems.at[i]
        )
        for i, ref in enumerate(refs)
    ]
    for copy in copies:
        copy.start()
    for copy in copies:
        copy.wait()


def put_blocks(refs, value):
    rows = refs[0].shape[0]
    for i, ref in enumerate(refs):
        ref[...] = value[i * rows : (i + 1) * rows].astype(BF16)


def struct(shape, kind):
    return jax.ShapeDtypeStruct(shape, kind)


def whole(shape):
    return pl.BlockSpec(shape, lambda *place: (0,) * len(shape))


def at(shape, row):
    return pl.BlockSpec(shape, lambda *place: (row,) + (0,) * (len(shape) - 1))


def swap(rows):
    quarter = rows.shape[1] // 4
    cut = [rows[:, i * quarter : (i + 1) * quarter] for i in range(4)]
    return jnp.concatenate([cut[1], cut[0], cut[3], cut[2]], 1)


def pack_spec(rows, width, place, share=16):
    return pl.BlockSpec((rows // share, share, width), lambda *step: (0, place // share, 0))


def pack_rows(pack_ref):
    return pack_ref[...].reshape(-1, pack_ref.shape[2])


def first_norms(got, skip_gain, norm1_gain, shift, along):
    count, rows, width = got.shape

    def kernel(got_ref, skip_ref, gain_ref, shift_ref, along_ref, merged_ref, hidden_ref, out_ref):
        merged = add_all([got_ref.at[i] for i in range(count)])
        merged_ref[...] = merged
        hidden = norm_parts(merged)[0] * skip_ref[...]
        hidden_ref[...] = hidden
        out_ref[:rows] = (norm_parts(hidden)[0] * gain_ref[...] + shift_ref[...]).astype(BF16)
        out_ref[rows:] = along_ref[...]

    outs = (
        struct((rows, width), F32),
        struct((rows, width), F32),
        struct((rows + along.shape[0], width), BF16),
    )
    ins = (got, skip_gain[None], norm1_gain[None], shift[None], along)
    return call(kernel, 2.5, outs, ins, "first_norms")


def mid_norm(pieces, hidden, gain):
    def kernel(*refs):
        hidden_ref, gain_ref, new_ref, out_ref = refs[len(pieces) :]
        new = hidden_ref[...] + add_all(refs[: len(pieces)])
        new_ref[...] = new
        out_ref[...] = (norm_parts(new)[0] * gain_ref[...]).astype(BF16)

    outs = (struct(hidden.shape, F32), struct(hidden.shape, BF16))
    return call(kernel, 1.5, outs, (*pieces, hidden, gain[None]), "mid_norm")


def mid_norm_back(pieces, residual, hidden, gain):
    def kernel(*refs):
        res_ref, hidden_ref, gain_ref, new_ref, out_ref, dgain_ref = refs[len(pieces) :]
        unit, scale = norm_parts(hidden_ref[...])
        grad, dgain = norm_back(unit, scale, gain_ref[...], add_all(refs[: len(pieces)]))
        dgain_ref[...] = dgain
        new = res_ref[...].astype(F32) + grad
        new_ref[...] = new
        out_ref[...] = new.astype(BF16)

    width = hidden.shape[1]
    outs = (struct(hidden.shape, F32), struct(hidden.shape, BF16), struct((1, width), F32))
    return call(kernel, 2, outs, (*pieces, residual, hidden, gain[None]), "mid_norm_back")


def last_norms(pieces, hidden_zero, merged, residual, gains, rows_two, rows_three, misc):
    rows, width = merged.shape
    many = len(pieces)

    def kernel(*refs):
        h0_ref, merged_ref, res_ref, g1_ref, gs_ref, two_ref, three_ref, misc_ref, out_ref = refs[many:]
        grad = add_all(refs[:many])
        shift_grad = jnp.sum(grad, 0, keepdims=True)
        unit, scale = norm_parts(h0_ref[...])
        step, norm1_grad = norm_back(unit, scale, g1_ref[...], grad)
        residual = res_ref[...] + step
        unit, scale = norm_parts(merged_ref[...])
        step, skip_grad = norm_back(unit, scale, gs_ref[...], residual)
        small = [skip_grad, norm1_grad, two_ref[...], three_ref[...], shift_grad, misc_ref[...]]
        small = stack(small + [jnp.zeros((16 - len(small), width), F32)]).astype(BF16)
        out_ref[:rows] = step.astype(BF16)
        out_ref[rows:] = small

    ins = (*pieces, hidden_zero, merged, residual, gains[0][None], gains[1][None])
    ins += (rows_two, rows_three, misc)
    return call(kernel, 3, struct((rows + 16, width), BF16), ins, "last_norms")


def project(parts, weight, other, cos_wide, sin_wide, qgain, kgain):
    width = parts[0].shape[1]
    tokens = cos_wide.shape[0]
    wide = weight.shape[0]
    each = wide // 3
    head = qgain.shape[0]
    heads = each // head
    many = len(parts)

    def kernel(*refs):
        w_ref, o_ref, cos_ref, sin_ref, qg_ref, kg_ref = refs[many : many + 6]
        x_ref, unit_ref, scale_ref, q_ref, kv_ref, sems = refs[many + 6 :]
        load_blocks(refs[:many], x_ref, sems)
        cos, sin = cos_ref[...], sin_ref[...]
        for s in range(2):
            out = dot_t(x_ref[...], w_ref[...] if s == 0 else pack_rows(o_ref))
            base = 2 * each * s
            kv_ref[:, base + each : base + 2 * each] = out[:, 2 * each :].astype(BF16)
            for h in range(heads):
                cut = lambda start: slice(start + h * head, start + (h + 1) * head)
                turn = lambda v: (v * cos + swap(v) * sin).astype(BF16)
                for part, gain_ref in ((0, qg_ref), (1, kg_ref)):
                    unit, scale = norm_parts(out[:, cut(part * each)])
                    n = (s * 2 + part) * heads + h
                    unit_ref[:, cut(base + part * each)] = unit
                    scale_ref[:, n : n + 1] = scale
                    if part == 0:
                        q_ref[:, cut(each * s)] = turn(unit * gain_ref[...])
                    else:
                        kv_ref[:, cut(base)] = turn(unit * gain_ref[...])

    outs = (
        struct((tokens, width), BF16),
        struct((tokens, 4 * each), F32),
        struct((tokens, 4 * heads), F32),
        struct((tokens, 2 * each), BF16),
        struct((tokens, 4 * each), BF16),
    )
    ins = (*parts, weight, other, cos_wide, sin_wide, qgain[None], kgain[None])
    specs = [HBM] * many + [whole(item.shape) for item in ins[many:]]
    specs[many + 1] = pack_spec(wide, width, 0, 48)
    return call(
        kernel, 6, outs, ins, "project", (1,), specs, tuple(whole(o.shape) for o in outs),
        (pltpu.SemaphoreType.DMA((many,)),),
    )


def key_rows(refs, shard, start, size, each):
    first = 2 * each * shard + start
    second = 2 * each * (1 - shard) + start
    return stack(
        [
            ref[:, first : first + size] if i < 2 else ref[:, second : second + size]
            for i, ref in enumerate(refs)
        ]
    )


def self_attention(queries, pairs, out_w, pack, head):
    tokens, both = queries.shape
    each = both // 2
    heads = each // head
    width = out_w.shape[1]
    scaling = head ** (-0.5)

    def kernel(q_ref, a_ref, b_ref, c_ref, d_ref, w_ref, o_ref, mixed_ref, total_ref, *out_refs):
        refs = (a_ref, b_ref, c_ref, d_ref)
        for s in range(2):
            for h in range(heads):
                n = s * heads + h
                cut = slice(n * head, (n + 1) * head)
                scores = dot_t(q_ref[:, cut], key_rows(refs, s, h * head, head, each)) * scaling
                most = jnp.max(scores, -1, keepdims=True)
                total = most + jnp.log(jnp.sum(jnp.exp(scores - most), -1, keepdims=True))
                total_ref[:, n : n + 1] = total
                shares = jnp.exp(scores - total).astype(BF16)
                mixture = dot(shares, key_rows(refs, s, each + h * head, head, each))
                mixed_ref[:, cut] = mixture.astype(BF16)
        out = dot(mixed_ref[:, :each], w_ref[...])
        out = out + dot(mixed_ref[:, each:], pack_rows(o_ref))
        put_blocks(out_refs, out)

    outs = (
        struct((tokens, both), BF16),
        struct((tokens, 2 * heads), F32),
    ) + (struct((tokens // 4, width), BF16),) * 4
    ins = (queries, *pairs, out_w, pack)
    specs = [whole(item.shape) for item in ins]
    specs[-1] = pack_spec(each, width, 48)
    return call(
        kernel, 5, outs, ins, "self_attention", (1,), specs, tuple(whole(o.shape) for o in outs)
    )


def self_attention_back(queries, pairs, totals, parts, out_w, pack, head):
    tokens, both = queries.shape
    each = both // 2
    heads = each // head
    rows, width = parts[0].shape
    scaling = head ** (-0.5)
    many = len(parts)

    def kernel(*refs):
        q_ref, a_ref, b_ref, c_ref, d_ref, total_ref, w_ref, o_ref = refs[many : many + 8]
        x_ref, dq_ref, own_ref, half_ref, core_ref, far_ref, dm_ref, sems = refs[many + 8 :]
        pair_refs = (a_ref, b_ref, c_ref, d_ref)
        load_blocks(refs[:many], x_ref, sems)
        dm_ref[:, :each] = dot_t(x_ref[...], w_ref[...]).astype(BF16)
        dm_ref[:, each:] = dot_t(x_ref[...], pack_rows(o_ref)).astype(BF16)

        def put(grads, shard, start):
            first = 2 * each * shard + start
            second = 2 * each * (1 - shard) + start
            cut = lambda i: grads[i * tokens : (i + 1) * tokens]
            own_ref[:, first : first + head] = cut(0)
            core_ref[:, first : first + head] = cut(1).astype(BF16)
            half_ref[:, second : second + head] = cut(2).astype(BF16)
            far_ref[:, second : second + head] = cut(3).astype(BF16)

        for s in range(2):
            for h in range(heads):
                n = s * heads + h
                cut = slice(n * head, (n + 1) * head)
                mine, grads = q_ref[:, cut], dm_ref[:, cut]
                keys_h = key_rows(pair_refs, s, h * head, head, each)
                values_h = key_rows(pair_refs, s, each + h * head, head, each)
                shares = jnp.exp(dot_t(mine, keys_h) * scaling - total_ref[:, n : n + 1])
                dshares = dot_t(grads, values_h)
                put(t_dot(shares.astype(BF16), grads), s, each + h * head)
                weighted = jnp.sum(shares * dshares, -1, keepdims=True)
                dscores = (shares * (dshares - weighted) * scaling).astype(BF16)
                dq_ref[:, cut] = dot(dscores, keys_h)
                put(t_dot(dscores, mine), s, h * head)

    outs = (
        struct((tokens, width), BF16),
        struct((tokens, both), F32),
        struct((tokens, 4 * each), F32),
        struct((tokens, 4 * each), BF16),
        struct((tokens, 4 * each), BF16),
        struct((tokens, 4 * each), BF16),
    )
    ins = (*parts, queries, *pairs, totals, out_w, pack)
    specs = [HBM] * many + [whole(item.shape) for item in ins[many:]]
    specs[-1] = pack_spec(each, width, 48)
    return call(
        kernel, 9, outs, ins, "self_attention_back", (1,), specs,
        tuple(whole(o.shape) for o in outs),
        (pltpu.VMEM((tokens, both), BF16), pltpu.SemaphoreType.DMA((many,))),
    )


def project_back(units, scales, cos_wide, sin_wide, qgain, kgain, dq, own, core, half, far, weight, other):
    tokens = units.shape[0]
    wide, width = weight.shape
    each = wide // 3
    head = qgain.shape[0]
    heads = each // head

    def kernel(unit_ref, scale_ref, cos_ref, sin_ref, qg_ref, kg_ref, dq_ref, own_ref, core_ref, half_ref, far_ref, w_ref, o_ref,
               mine_ref, other_ref, dqg_ref, dkg_ref, *out_refs):
        cos, sin = cos_ref[...], sin_ref[...]
        dkv = own_ref[...] + core_ref[...].astype(F32)
        dkv = dkv + half_ref[...].astype(F32) + far_ref[...].astype(F32)
        dgains = [jnp.zeros((1, head), F32), jnp.zeros((1, head), F32)]
        for s, to_ref in ((0, mine_ref), (1, other_ref)):
            base = 2 * each * s
            to_ref[:, 2 * each : 3 * each] = dkv[:, base + each : base + 2 * each].astype(BF16)
            for h in range(heads):
                cut = lambda start: slice(start + h * head, start + (h + 1) * head)
                for part, gain_ref in ((0, qg_ref), (1, kg_ref)):
                    turned = dq_ref[:, cut(each * s)] if part == 0 else dkv[:, cut(base)]
                    grad = turned * cos - swap(turned) * sin
                    n = (s * 2 + part) * heads + h
                    unit = unit_ref[:, cut(base + part * each)]
                    grad, dgain = norm_back(unit, scale_ref[:, n : n + 1], gain_ref[...], grad)
                    dgains[part] = dgains[part] + dgain
                    to_ref[:, cut(part * each)] = grad.astype(BF16)
        dqg_ref[...], dkg_ref[...] = dgains
        out = dot(mine_ref[...], w_ref[...])
        put_blocks(out_refs, out + dot(other_ref[...], pack_rows(o_ref)))

    outs = (
        struct((tokens, wide), BF16),
        struct((tokens, wide), BF16),
        struct((1, head), F32),
        struct((1, head), F32),
    ) + (struct((tokens // 4, width), BF16),) * 4
    ins = (units, scales, cos_wide, sin_wide, qgain[None], kgain[None], dq, own, core, half, far, weight, other)
    specs = [whole(item.shape) for item in ins]
    specs[-1] = pack_spec(wide, width, 0, 48)
    return call(
        kernel, 8, outs, ins, "project_back", (1,), specs, tuple(whole(o.shape) for o in outs)
    )


def text_shares(scores, scaling, count):
    place = lax.broadcasted_iota(jnp.int32, scores.shape, 1)
    scores = jnp.where(place < count, scores * scaling, -1e30)
    most = jnp.max(scores, -1, keepdims=True)
    total = most + jnp.log(jnp.sum(jnp.exp(scores - most), -1, keepdims=True))
    return jnp.exp(scores - total)


def cross_layer(parts, cq_w, out_w, pack, text, other_text, gain, text_count):
    rows, width = parts[0].shape
    tokens = rows * len(parts)
    each = cq_w.shape[0]
    head = gain.shape[0]
    heads = each // head
    scaling = head ** (-0.5)
    many = len(parts)

    def kernel(*refs):
        cq_ref, w_ref, ocq_ref, ow_ref, text_ref, otext_ref, gain_ref = refs[many : many + 7]
        x_ref, raw_ref, mixed_ref, *out_refs, sems = refs[many + 7 :]
        load_blocks(refs[:many], x_ref, sems)
        raw_ref[:, :each] = dot_t(x_ref[...], cq_ref[...])
        raw_ref[:, each:] = dot_t(x_ref[...], pack_rows(ocq_ref))
        for s, keys_ref in ((0, text_ref), (1, otext_ref)):
            for h in range(heads):
                n = s * heads + h
                cut = slice(n * head, (n + 1) * head)
                mine = (norm_parts(raw_ref[:, cut])[0] * gain_ref[...]).astype(BF16)
                scores = dot_t(mine, keys_ref[:, h * head : (h + 1) * head])
                shares = text_shares(scores, scaling, text_count).astype(BF16)
                values = keys_ref[:, each + h * head : each + (h + 1) * head]
                mixed_ref[:, cut] = dot(shares, values).astype(BF16)
        out = dot(mixed_ref[:, :each], w_ref[...])
        out = out + dot(mixed_ref[:, each:], pack_rows(ow_ref))
        put_blocks(out_refs, out)

    outs = (
        struct((tokens, width), BF16),
        struct((tokens, 2 * each), F32),
        struct((tokens, 2 * each), BF16),
    ) + (struct((rows, width), BF16),) * many
    ins = (*parts, cq_w, out_w, pack, pack, text, other_text, gain[None])
    specs = [HBM] * many + [whole(item.shape) for item in ins[many:]]
    specs[many + 2] = pack_spec(each, width, 64)
    specs[many + 3] = pack_spec(each, width, 80)
    return call(
        kernel, 7, outs, ins, "cross_layer", (1,), specs, tuple(whole(o.shape) for o in outs),
        (pltpu.SemaphoreType.DMA((many,)),),
    )


def cross_layer_back(parts, raw, cq_w, out_w, pack, text, other_text, gain, text_count):
    rows, width = parts[0].shape
    tokens = rows * len(parts)
    each = cq_w.shape[0]
    head = gain.shape[0]
    heads = each // head
    scaling = head ** (-0.5)
    many = len(parts)

    def kernel(*refs):
        raw_ref, cq_ref, w_ref, ocq_ref, ow_ref, text_ref, otext_ref, gain_ref = refs[many : many + 8]
        x_ref, draw_ref, dtext_ref, dother_ref, dgain_ref, *out_refs, dm_ref, sems = refs[many + 8 :]
        load_blocks(refs[:many], x_ref, sems)
        dm_ref[:, :each] = dot_t(x_ref[...], w_ref[...]).astype(BF16)
        dm_ref[:, each:] = dot_t(x_ref[...], pack_rows(ow_ref)).astype(BF16)
        dgain = jnp.zeros((1, head), F32)
        for s, keys_ref, to_ref in ((0, text_ref, dtext_ref), (1, otext_ref, dother_ref)):
            for h in range(heads):
                n = s * heads + h
                cut = slice(n * head, (n + 1) * head)
                kcut = slice(h * head, (h + 1) * head)
                vcut = slice(each + h * head, each + (h + 1) * head)
                unit, scale = norm_parts(raw_ref[:, cut])
                mine = (unit * gain_ref[...]).astype(BF16)
                shares = text_shares(dot_t(mine, keys_ref[:, kcut]), scaling, text_count)
                dshares = dot_t(dm_ref[:, cut], keys_ref[:, vcut])
                to_ref[:, vcut] = t_dot(shares.astype(BF16), dm_ref[:, cut]).astype(BF16)
                weighted = jnp.sum(shares * dshares, -1, keepdims=True)
                dscores = (shares * (dshares - weighted) * scaling).astype(BF16)
                to_ref[:, kcut] = t_dot(dscores, mine).astype(BF16)
                grad, step = norm_back(unit, scale, gain_ref[...], dot(dscores, keys_ref[:, kcut]))
                dgain = dgain + step
                draw_ref[:, cut] = grad.astype(BF16)
        dgain_ref[...] = dgain
        out = dot(draw_ref[:, :each], cq_ref[...])
        out = out + dot(draw_ref[:, each:], pack_rows(ocq_ref))
        put_blocks(out_refs, out)

    outs = (
        struct((tokens, width), BF16),
        struct((tokens, 2 * each), BF16),
        struct(text.shape, BF16),
        struct(text.shape, BF16),
        struct((1, head), F32),
    ) + (struct((rows, width), BF16),) * many
    ins = (*parts, raw, cq_w, out_w, pack, pack, text, other_text, gain[None])
    specs = [HBM] * many + [whole(item.shape) for item in ins[many:]]
    specs[many + 3] = pack_spec(each, width, 64)
    specs[many + 4] = pack_spec(each, width, 80)
    return call(
        kernel, 10, outs, ins, "cross_layer_back", (1,), specs,
        tuple(whole(o.shape) for o in outs),
        (pltpu.VMEM((tokens, 2 * each), BF16), pltpu.SemaphoreType.DMA((many,))),
    )


def feed_forward(parts, cot, fc1_w, fc2_w, pack):
    rows, width = parts[0].shape
    tokens = rows * len(parts)
    hidden = fc2_w.shape[0]
    block = hidden // 2
    places = pack.shape[0]
    each = hidden // places
    both = 2 * each
    root = (2 / 3.141592653589793) ** 0.5
    many = len(parts)

    def kernel(*refs):
        cot_ref, w1_ref, w2_ref, pack_ref, x_ref, acts_ref, *out_refs, acc_ref, sum_ref, sems = refs[many:]
        step = pl.program_id(0)

        @pl.when(step == 0)
        def _():
            load_blocks(refs[:many], x_ref, sems)
            acc_ref[...] = jnp.zeros_like(acc_ref)
            sum_ref[...] = jnp.zeros_like(sum_ref)

        def work(pre, w2, back):
            square = pre * pre
            bent = jnp.tanh(root * pre * (1 + 0.044715 * square))
            part = 0.5 * (1 + bent)
            slope = part + 0.5 * pre * (1 - bent * bent) * root * (1 + 3 * 0.044715 * square)
            grad = (dot_t(cot_ref[...], w2) * slope).astype(BF16)
            acts_ref[0, 0] = grad
            active = (pre * part).astype(BF16)
            acts_ref[0, 1] = active
            acc_ref[...] += back(grad)
            sum_ref[...] += dot(active, w2)

        @pl.when(step < 2)
        def _():
            weight = w1_ref[...]
            work(dot(x_ref[...], weight), w2_ref[...], lambda grad: dot_t(grad, weight))

        @pl.when(step >= 2)
        def _():
            weight = pack_ref[:, :each].reshape(block, width)
            second = pack_ref[:, each:].reshape(block, width)
            work(dot_t(x_ref[...], weight), second, lambda grad: dot(grad, weight))

        @pl.when(step == 3)
        def _():
            put_blocks(out_refs[:many], acc_ref[...])
            put_blocks(out_refs[many:], sum_ref[...])

    low = lambda i: jnp.minimum(i, 1)
    high = lambda i: jnp.maximum(i - 2, 0)
    outs = (
        struct((tokens, width), BF16),
        struct((2, 2, tokens, hidden), BF16),
    ) + (struct((rows, width), BF16),) * (2 * many)
    out_specs = (
        whole((tokens, width)),
        pl.BlockSpec((1, 2, tokens, block), lambda i: (i // 2, 0, 0, i % 2)),
    ) + (whole((rows, width)),) * (2 * many)
    in_specs = [HBM] * many + [
        whole(cot.shape),
        pl.BlockSpec((width, block), lambda i: (0, low(i))),
        pl.BlockSpec((block, width), lambda i: (low(i), 0)),
        pl.BlockSpec((places // 2, both, width), lambda i: (high(i), 0, 0)),
    ]
    return call(
        kernel, 9, outs, (*parts, cot, fc1_w, fc2_w, pack), "feed_forward", (4,), in_specs, out_specs,
        (
            pltpu.VMEM((tokens, width), F32),
            pltpu.VMEM((tokens, width), F32),
            pltpu.SemaphoreType.DMA((many,)),
        ),
    )


def feed_forward_grads(acts, rows_in, cot, places):
    _, _, tokens, hidden = acts.shape
    width = cot.shape[1]
    share = 2 * hidden // places

    def kernel(acts_ref, x_ref, cot_ref, out_ref):
        which = pl.program_id(1)

        def put(right_ref):
            grads = t_dot(acts_ref[0, 0], right_ref[...]).astype(BF16)
            out_ref[...] = grads.reshape(out_ref.shape)

        pl.when(which == 0)(lambda: put(x_ref))
        pl.when(which == 1)(lambda: put(cot_ref))

    return call(
        kernel,
        7,
        struct((places, 2, share, width), BF16),
        (acts, rows_in, cot),
        "feed_forward_grads",
        (2, 2),
        [
            pl.BlockSpec((1, 1, tokens, hidden), lambda s, w: (s, w, 0, 0)),
            whole(rows_in.shape),
            whole(cot.shape),
        ],
        pl.BlockSpec((places // 2, 1, share, width), lambda s, w: (w, s, 0, 0)),
    )


def late_grads(draw, mixed_two, rows_two, grad_two, mine, other, mixed_one, rows_one, grad_one, texts):
    each = draw.shape[1] // 2
    width = rows_two.shape[1]
    wide = mine.shape[1]
    places, _, more, _ = texts.shape
    first, second = 48, 96

    def kernel(draw_ref, mixed_ref, x_ref, d_ref, mine_ref, other_ref, one_ref, y_ref, e_ref, text_ref, out_ref, hold_ref):
        step = pl.program_id(0)
        for s, grad_ref in ((0, mine_ref), (1, other_ref)):

            @pl.when(step == s)
            def _(s=s, grad_ref=grad_ref):
                cut = slice(s * each, (s + 1) * each)
                hold_ref[:each] = t_dot(draw_ref[:, cut], x_ref[...]).astype(BF16)
                hold_ref[each : 2 * each] = t_dot(mixed_ref[:, cut], d_ref[...]).astype(BF16)
                hold_ref[2 * each : 2 * each + wide] = t_dot(grad_ref[...], y_ref[...]).astype(BF16)
                hold_ref[2 * each + wide :] = t_dot(one_ref[:, cut], e_ref[...]).astype(BF16)

        for place in range(places):
            for share, start, stop, to in (
                (first, 0, 2 * each, 0),
                (second, 2 * each, 3 * each + wide, first),
            ):
                begin = min(start + place * share, stop)
                count = min(share, stop - begin)
                out_ref[place, 0, to : to + count] = hold_ref[begin : begin + count]
                if count < share:
                    blank = jnp.zeros((share - count, width), BF16)
                    out_ref[place, 0, to + count : to + share] = blank
            out_ref[place, 0, first + second :] = text_ref[place, 0]

    ins = (draw, mixed_two, rows_two, grad_two, mine, other, mixed_one, rows_one, grad_one, texts)
    rows = first + second + more
    return call(
        kernel, 9, struct((places, 2, rows, width), BF16), ins, "late_grads", (2,),
        [whole(item.shape) for item in ins[:-1]]
        + [pl.BlockSpec((places, 1, more, width), lambda s: (0, s, 0, 0))],
        pl.BlockSpec((places, 1, rows, width), lambda s: (0, s, 0, 0)),
        (pltpu.VMEM((3 * each + wide, width), BF16),),
    )


def skip_grads(parts, joined_own, joined_other, long):
    rows, width = parts[0].shape
    small = 16
    rows -= small
    tokens, slab = joined_own.shape
    many = len(parts)

    def kernel(*refs):
        own_ref, other_ref, x_ref, out_ref, all_ref, sems = refs[many:]
        load_blocks(refs[:many], all_ref, sems)
        total = jnp.zeros((small, width), F32)
        for i in range(many):
            start = i * (rows + small)
            x_ref[i * rows : (i + 1) * rows] = all_ref[start : start + rows]
            total = total + all_ref[start + rows : start + rows + small].astype(F32)
        for s, left_ref in ((0, own_ref), (1, other_ref)):
            out_ref[s, :slab] = t_dot(left_ref[...], x_ref[...])
            out_ref[s, slab : slab + small] = total
            out_ref[s, slab + small :] = jnp.zeros((long - slab - small, width), F32)

    outs = (struct((tokens, width), BF16), struct((2, long, width), F32))
    ins = (*parts, joined_own, joined_other)
    return call(
        kernel, 4, outs, ins, "skip_grads", (1,),
        [HBM] * many + [whole(joined_own.shape), whole(joined_other.shape)],
        tuple(whole(o.shape) for o in outs),
        (pltpu.VMEM((many * (rows + small), width), BF16), pltpu.SemaphoreType.DMA((many,))),
    )


def joined_grads(rows_in, pack, slab):
    tokens, width = rows_in.shape
    _, count, deep, _ = pack.shape
    held = slab // deep
    half = count // 2

    def kernel(x_ref, pack_ref, one_ref, two_ref):
        for step, out_ref in ((0, one_ref), (1, two_ref)):

            @pl.when(pl.program_id(0) == step)
            def _(out_ref=out_ref):
                for j in range(half):
                    weight = pack_ref[:, j].reshape(slab, width)
                    out_ref[:, j * slab : (j + 1) * slab] = dot_t(x_ref[...], weight)

    outs = (struct((tokens, width), F32), struct((tokens, width), F32))
    return call(
        kernel, 9, outs, (rows_in, pack), "joined_grads", (2,),
        [
            whole(rows_in.shape),
            pl.BlockSpec((held, half, deep, width), lambda i: (0, i, 0, 0)),
        ],
        (whole((tokens, width)), whole((tokens, width))),
    )


def feed_forward_out(sums):
    places, share, width = sums.shape
    half = places // 2
    hidden = half * share

    def kernel(sum_ref, one_ref, two_ref):
        @pl.when(pl.program_id(0) == 0)
        def _():
            one_ref[...] = sum_ref[...].reshape(hidden, width).astype(F32).T

        @pl.when(pl.program_id(0) == 1)
        def _():
            two_ref[...] = sum_ref[...].reshape(hidden, width).astype(F32)

    outs = (struct((width, hidden), F32), struct((hidden, width), F32))
    return call(
        kernel, 6, outs, (sums,), "feed_forward_out", (2,),
        [pl.BlockSpec((half, share, width), lambda i: (i, 0, 0))],
        (whole((width, hidden)), whole((hidden, width))),
    )


def text_layer(tokens, ckv, gain, rows):
    count, width = tokens.shape
    packed = ckv.ndim == 3
    both = ckv.shape[2] // 4 if packed else ckv.shape[1]
    each = both // 2
    head = gain.shape[0]
    heads = each // head

    def kernel(x_ref, w_ref, gain_ref, pair_ref, unit_ref, scale_ref, *more):
        if packed:
            weight_ref = more[0]
            deep = w_ref.shape[1]
            for place in range(w_ref.shape[0]):
                for k in range(4):
                    start = (place * 4 + k) * deep
                    weight_ref[start : start + deep] = w_ref[place, :, k * both : (k + 1) * both]
        else:
            weight_ref = w_ref
        out = dot(x_ref[...], weight_ref[...])
        pair_ref[...] = jnp.zeros_like(pair_ref)
        pair_ref[:count, each:] = out[:, each:].astype(BF16)
        for h in range(heads):
            cut = slice(h * head, (h + 1) * head)
            unit, scale = norm_parts(out[:, cut])
            unit_ref[:, cut] = unit
            scale_ref[:, h : h + 1] = scale
            pair_ref[:count, cut] = (unit * gain_ref[...]).astype(BF16)

    outs = (
        struct((rows, both), BF16),
        struct((count, each), F32),
        struct((count, heads), F32),
    )
    specs = [whole(tokens.shape), whole(ckv.shape), whole((1, head))]
    if packed:
        outs += (struct((width, both), BF16),)
        deep = width // ckv.shape[0] // 4
        place = ckv.shape[1] // deep - 1
        specs[1] = pl.BlockSpec((ckv.shape[0], deep, ckv.shape[2]), lambda *step: (0, place, 0))
    return call(
        kernel, 4, outs, (tokens, ckv, gain[None]), "text_layer", (1,), specs,
        tuple(whole(o.shape) for o in outs),
    )


def text_layer_back(pairs, units, scales, tokens, ckvs, gain, places):
    count, width = tokens.shape
    both = ckvs[0].shape[1]
    each = both // 2
    head = gain.shape[0]
    heads = each // head
    wide = 4 * both
    deep = 48
    more = 48
    long = more * places

    def kernel(a_ref, b_ref, ua_ref, ub_ref, sa_ref, sb_ref, x_ref, wa_ref, wb_ref, gain_ref, out_ref, dw_ref, grad_ref, part_ref):
        dgain = jnp.zeros((1, head), F32)
        part = jnp.zeros((count, width), F32)
        for s, (pair_ref, unit_ref, scale_ref, w_ref) in enumerate(
            ((a_ref, ua_ref, sa_ref, wa_ref), (b_ref, ub_ref, sb_ref, wb_ref))
        ):
            grad_ref[:, each:] = pair_ref[:count, each:]
            for h in range(heads):
                cut = slice(h * head, (h + 1) * head)
                grad, step = norm_back(
                    unit_ref[:, cut], scale_ref[:, h : h + 1], gain_ref[...], pair_ref[:count, cut].astype(F32)
                )
                dgain = dgain + step
                grad_ref[:, cut] = grad.astype(BF16)
            dw_ref[...] = t_dot(grad_ref[...], x_ref[...]).astype(BF16)
            part = part + dot_t(grad_ref[...], w_ref[...])
            for place in range(places):
                begin = min(place * deep, both)
                held = min(deep, both - begin)
                out_ref[place, s, :deep] = jnp.zeros((deep, wide), BF16)
                out_ref[place, s, :held, :width] = dw_ref[begin : begin + held]
        part_ref[...] = jnp.zeros_like(part_ref)
        part_ref[:count, :width] = part
        part_ref[long - 1 :, :head] = dgain
        for place in range(places):
            rows = part_ref[place * more : (place + 1) * more].astype(BF16)
            for s in range(2):
                out_ref[place, s, deep : deep + more] = rows

    ins = (*pairs, *units, *scales, tokens, *ckvs, gain[None])
    scratch = (
        pltpu.VMEM((both, width), BF16),
        pltpu.VMEM((count, both), BF16),
        pltpu.VMEM((long, wide), F32),
    )
    return call(
        kernel, 9, struct((places, 2, deep + more, wide), BF16), ins, "text_layer_back", scratch=scratch
    )


def local(
    latent,
    skip_input,
    text_tokens,
    condition,
    positions,
    cotangent,
    skip_w,
    skip_gain,
    norm1_gain,
    mod_w,
    qkv_w,
    qnorm_gain,
    knorm_gain,
    attn_out_w,
    norm2_gain,
    cq_w,
    ckv_w,
    cqnorm_gain,
    cknorm_gain,
    cross_out_w,
    norm3_gain,
    fc1_w,
    fc2_w,
):
    token_count, model_width = latent.shape
    head_dim = qnorm_gain.shape[0]
    local_width = cq_w.shape[1]
    local_heads = local_width // head_dim
    slab_width = skip_w.shape[0]
    hidden_width = fc1_w.shape[1]
    text_count, text_width = text_tokens.shape
    tensor_place = lax.axis_index("tensor")
    tensor_count = lax.axis_size("tensor")
    dp_count = lax.axis_size("dp")
    low_count = len(low_groups()[0])
    part_count = token_count // tensor_count
    ring = tensor_count // 2
    ring_place, half = tensor_place % ring, tensor_place // ring
    qkv_rows = 3 * local_width

    def own_rows(rows):
        return lax.dynamic_slice_in_dim(rows, tensor_place * part_count, part_count, 0)

    def ring_rows(rows, which):
        first = which * ring
        return jnp.concatenate(
            [
                lax.dynamic_slice_in_dim(
                    rows, (first + (ring_place - k) % ring) * part_count, part_count, 0
                )
                for k in range(ring)
            ],
            0,
        )

    joined = jnp.concatenate([latent, skip_input], 1)
    joined_part = lax.dynamic_slice_in_dim(joined, tensor_place * slab_width, slab_width, 1)
    partial = jnp.dot(joined_part, skip_w, preferred_element_type=F32).astype(BF16)
    got = exchange(partial.reshape(tensor_count, part_count, model_width))

    dp_place = lax.axis_index("dp")
    qkv_flat = qkv_w.transpose(1, 2, 0).reshape(qkv_rows, model_width)
    cq_turned = cq_w.T
    shares = [dp_slice(qkv_flat, 48)]
    shares += [dp_slice(rows, 16) for rows in (attn_out_w, cq_turned, cross_out_w)]
    pack = lax.all_gather(half_swap(jnp.concatenate(shares, 0)), "dp", axis=0, tiled=False)
    ckv_flat = ckv_w.reshape(text_width, 2 * local_width)
    text_pair, text_units, text_scales = text_layer(
        text_tokens, ckv_flat, cknorm_gain, model_width // 4
    )
    share = hidden_width // dp_count
    deep = text_width // dp_count // 4
    ff_share = [
        lax.dynamic_slice_in_dim(fc1_w, dp_place * share, share, 1).T,
        lax.dynamic_slice_in_dim(fc2_w, dp_place * share, share, 0),
    ]
    ckv_share = lax.dynamic_slice_in_dim(ckv_flat, dp_place * 4 * deep, 4 * deep, 0)
    ff_share.append(jnp.concatenate(jnp.split(ckv_share, 4), 1))
    ff_share = half_swap(jnp.concatenate(ff_share, 0))
    silu_cond = jax.nn.silu(condition.astype(F32)).astype(BF16)
    shift = jnp.dot(silu_cond[None], mod_w, preferred_element_type=F32)[0]
    cos_wide, sin_wide = rotary_tables(ring_rows(positions, half), head_dim)
    cot_rows = ring_rows(cotangent, half)
    got, qkv_flat, cos_wide, sin_wide, shift, text_pair, cot_rows, ff_share = join(
        got, qkv_flat, cos_wide, sin_wide, shift, text_pair, cot_rows, ff_share
    )
    skip_share = dp_slice(skip_w, 32)
    merged, hidden_zero, normed = first_norms(got, skip_gain, norm1_gain, shift, skip_share)
    normed_parts = ring_gather(normed)
    rows_one, units, scales, queries, own_pair = project(
        normed_parts, qkv_flat, pack, cos_wide, sin_wide, qnorm_gain, knorm_gain
    )
    ff_pack = lax.all_gather(after(ff_share, rows_one), "dp", axis=0, tiled=False)
    core_pair = core_swap(own_pair)
    half_pair = half_swap(own_pair)
    pairs = (own_pair, core_pair, half_pair, core_swap(half_pair))
    mixed_one, totals, *partial = self_attention(
        queries, pairs, attn_out_w, pack, head_dim
    )
    hidden_one, normed = mid_norm(ring_scatter(partial), hidden_zero, norm2_gain)
    skip_rows = jnp.concatenate([part[part_count:] for part in normed_parts], 0)
    skip_half = half_swap(after(skip_rows, normed))
    other_text, other_units, other_scales, other_ckv = text_layer(
        text_tokens, after(ff_pack, normed), cknorm_gain, model_width // 4
    )
    *normed_parts, skip_half, other_text = join(*ring_gather(normed), skip_half, other_text)
    skip_rows = place_blocks(jnp.split(skip_rows, ring), jnp.split(skip_half, ring))
    skip_pack = lax.all_gather(
        skip_rows.reshape(tensor_count, -1, model_width), "dp", axis=0, tiled=False
    )
    rows_two, cross_raw, mixed_two, *partial = cross_layer(
        normed_parts,
        cq_turned,
        cross_out_w,
        pack,
        text_pair,
        other_text,
        cqnorm_gain,
        text_count,
    )
    hidden_two, normed = mid_norm(ring_scatter(partial), hidden_one, norm3_gain)
    rows_three, acts, *partial = feed_forward(
        ring_gather(normed), cot_rows, fc1_w, fc2_w, ff_pack
    )
    partial, last_partial = partial[:ring], partial[ring:]

    fc_grads = feed_forward_grads(acts, rows_three, cot_rows, low_count)
    *pieces, fc_grads = join(*ring_scatter(partial), fc_grads.reshape(-1, model_width))
    fc_grads = scatter_low(after(fc_grads, skip_pack))
    residual, out_grad, norm3_grad = mid_norm_back(
        pieces, own_rows(cotangent), hidden_two, norm3_gain
    )
    out_parts = ring_gather(out_grad)
    grad_rows_two, cross_raw_grad, text_own, text_other, cqnorm_grad, *partial = cross_layer_back(
        out_parts,
        cross_raw,
        cq_turned,
        cross_out_w,
        pack,
        text_pair,
        other_text,
        cqnorm_gain,
        text_count,
    )
    residual, out_grad, norm2_grad = mid_norm_back(
        ring_scatter(partial), residual, hidden_one, norm2_gain
    )
    text_sums = text_layer_back(
        (text_own, text_other),
        (text_units, other_units),
        (text_scales, other_scales),
        after(text_tokens, out_grad),
        (ckv_flat, other_ckv),
        cknorm_gain,
        low_count,
    )
    *out_parts, text_sums = join(*ring_gather(out_grad), text_sums)
    grad_rows_one, query_grad, pair_grad, half_grad, core_grad, far_grad = self_attention_back(
        queries,
        pairs,
        totals,
        out_parts,
        attn_out_w,
        pack,
        head_dim,
    )
    core_grad = core_swap(core_grad)
    half_grad = half_swap(half_grad)
    far_grad = far_swap(far_grad)
    core_grad, half_grad, far_grad = join(core_grad, half_grad, far_grad)
    fc_grads = after(fc_grads, half_grad)
    share = fc_grads.shape[0] // 2
    fc_grads = half_sum(fc_grads[:share], fc_grads[share:])
    output = hidden_two
    for piece in ring_scatter(after_all(last_partial, half_grad)):
        output = output + piece.astype(F32)
    projected_grad, projected_other, qnorm_grad, knorm_grad, *partial = project_back(
        units,
        scales,
        cos_wide,
        sin_wide,
        qnorm_gain,
        knorm_gain,
        query_grad,
        pair_grad,
        core_grad,
        half_grad,
        far_grad,
        qkv_flat,
        pack,
    )
    *partial, fc_grads, output = join(*partial, fc_grads, output)
    fc_grads = fc_grads + low_swap(fc_grads.astype(BF16)).astype(F32)
    late_sums = late_grads(
        cross_raw_grad,
        mixed_two,
        rows_two,
        grad_rows_two,
        projected_grad,
        projected_other,
        mixed_one,
        rows_one,
        grad_rows_one,
        text_sums,
    )
    late_sums = late_sums.reshape(-1, model_width)
    *pieces, late_sums, fc_grads = join(*ring_scatter(partial), late_sums, fc_grads)
    late_sums = scatter_low(late_sums)
    misc = jnp.concatenate([qnorm_grad, knorm_grad, cqnorm_grad], 1)
    misc = jnp.pad(misc, ((0, 0), (0, model_width - misc.shape[1])))
    merged_out = last_norms(
        pieces,
        hidden_zero,
        merged,
        residual,
        (norm1_gain, skip_gain),
        norm2_grad,
        norm3_grad,
        misc,
    )
    joined_rows = ring_rows(joined, half)
    joined_own = lax.dynamic_slice_in_dim(joined_rows, tensor_place * slab_width, slab_width, 1)
    joined_other = lax.dynamic_slice_in_dim(
        joined_rows, (tensor_place + ring) % tensor_count * slab_width, slab_width, 1
    )
    *merged_parts, joined_own, joined_other = join(
        *ring_gather(merged_out), joined_own, joined_other
    )

    last_rows = -(-(slab_width + 16) // (8 * dp_count)) * 8 * dp_count
    merged_rows, last_sums = skip_grads(merged_parts, joined_own, joined_other, last_rows)
    merged_half = half_swap(merged_rows)
    last_sums = scatter_stage(0, last_sums)
    output = jnp.concatenate(ring_gather(after(output.astype(BF16), merged_rows)), 0)
    last_sums, output = join(last_sums, output)
    last_sums = scatter_stage(1, last_sums)
    output_half = half_swap(output)
    last_sums, merged_half, late_sums = join(last_sums, merged_half, late_sums)
    fc_grads = gather_low(after(fc_grads.astype(BF16), late_sums))
    share = late_sums.shape[0] // 2
    own_sums = jnp.concatenate([late_sums[:share].astype(F32), last_sums[0]], 0)
    other_sums = jnp.concatenate([late_sums[share:], last_sums[1].astype(BF16)], 0)
    last_sums = half_sum(own_sums, other_sums)
    merged_grad = place_blocks(jnp.split(merged_rows, ring), jnp.split(merged_half, ring))
    latent_grad, skip_grad = joined_grads(merged_grad, skip_pack, slab_width)
    last_sums, latent_grad, skip_grad = join(last_sums, latent_grad, skip_grad)
    last_sums = last_sums + low_swap(last_sums.astype(BF16)).astype(F32)
    text_share = slice(share - 48, share)
    text_parts = ring_gather(last_sums[text_share].astype(BF16))
    text_rows = last_sums[text_share]
    for part in text_parts[1:]:
        text_rows = text_rows + part.astype(F32)
    last_sums = jnp.concatenate([last_sums[: share - 48], text_rows, last_sums[share:]], 0)
    last_sums, fc_grads = join(last_sums, fc_grads)
    last_sums = gather_low(last_sums.astype(BF16))
    fc1_grad, fc2_grad = feed_forward_out(fc_grads)
    output = place_blocks(jnp.split(output, ring), jnp.split(output_half, ring))
    last_sums, output, fc1_grad, fc2_grad = join(last_sums, output, fc1_grad, fc2_grad)
    cross_sums = last_sums[:, :48].reshape(-1, model_width)
    cq_grad = cross_sums[:local_width].T.astype(F32)
    cross_out_grad = cross_sums[local_width : 2 * local_width].astype(F32)
    self_sums = last_sums[:, 48:144].reshape(-1, model_width)
    qkv_grad = self_sums[:qkv_rows].T.astype(F32).reshape(model_width, 3, local_width)
    attn_out_grad = self_sums[qkv_rows : qkv_rows + local_width].astype(F32)
    ckv_grad = last_sums[:, 144:192].reshape(-1, model_width)[: 2 * local_width, :text_width]
    ckv_grad = ckv_grad.astype(F32).T.reshape(text_width, 2, local_width)
    text_rows = last_sums[:, text_share].reshape(-1, model_width).astype(F32)
    text_grad = text_rows[:text_count, :text_width]
    cknorm_grad = text_rows[-1, :head_dim]
    last_sums = last_sums[:, share:].reshape(4, 2, -1, model_width).transpose(1, 0, 2, 3)
    last_sums = last_sums.reshape(-1, model_width)
    skip_w_grad = last_sums[:slab_width].astype(F32)
    small = last_sums[slab_width:].astype(F32)
    skip_gain_grad, norm1_grad, norm2_grad, norm3_grad, mod_vector = [small[i] for i in range(5)]
    qnorm_grad, knorm_grad, cqnorm_grad = [
        small[5, i * head_dim : (i + 1) * head_dim] for i in range(3)
    ]
    mod_grad = silu_cond.astype(F32)[:, None] * mod_vector[None, :]
    return (
        output,
        latent_grad,
        skip_grad,
        text_grad,
        skip_w_grad,
        skip_gain_grad,
        norm1_grad,
        mod_grad,
        qkv_grad,
        qnorm_grad,
        knorm_grad,
        attn_out_grad,
        norm2_grad,
        cq_grad,
        ckv_grad,
        cqnorm_grad,
        cknorm_grad,
        cross_out_grad,
        norm3_grad,
        fc1_grad,
        fc2_grad,
    )


def solution(mesh):
    placed = (
        P("dp", None),
        P("dp", None),
        P(),
        P(),
        P("dp", None),
        P("dp", None),
        P("tensor", None),
        P(),
        P(),
        P(),
        P(None, None, "tensor"),
        P(),
        P(),
        P("tensor", None),
        P(),
        P(None, "tensor"),
        P(None, None, "tensor"),
        P(),
        P(),
        P("tensor", None),
        P(),
        P(None, "tensor"),
        P("tensor", None),
    )
    return jax.shard_map(
        local,
        mesh=mesh,
        in_specs=placed,
        out_specs=(
            P("dp", None),
            P("dp", None),
            P("dp", None),
            P(),
            P("tensor", None),
            P(),
            P(),
            P(),
            P(None, None, "tensor"),
            P(),
            P(),
            P("tensor", None),
            P(),
            P(None, "tensor"),
            P(None, None, "tensor"),
            P(),
            P(),
            P("tensor", None),
            P(),
            P(None, "tensor"),
            P("tensor", None),
        ),
        check_vma=False,
    )
```

```python
import jax
import jax.numpy as jnp
from jax import lax
from jax.experimental import pallas as pl
from jax.experimental.pallas import tpu as pltpu
from jax.sharding import PartitionSpec as P

BF16 = jnp.bfloat16
F32 = jnp.float32


def layer_norm(inputs, norm_gain):
    centered = inputs - jnp.mean(inputs, -1, keepdims=True)
    variance = jnp.mean(centered * centered, -1, keepdims=True)
    return centered * lax.rsqrt(variance + 1e-06) * norm_gain


def rotary_tables(positions, head_dim):
    quarter = head_dim // 4
    frequency = 10000.0 ** (-jnp.arange(quarter).astype(F32) / quarter)
    angles = positions.astype(F32)[:, :, None] * frequency
    cosine, sine = jnp.cos(angles), jnp.sin(angles)
    cos_wide = jnp.stack([cosine, cosine], 2).reshape(positions.shape[0], head_dim)
    sin_wide = jnp.stack([-sine, sine], 2).reshape(positions.shape[0], head_dim)
    return cos_wide, sin_wide


def left_product(inputs, grads):
    return lax.dot_general(
        inputs, grads, (((0,), (0,)), ((), ())), preferred_element_type=jnp.float32
    )


def right_product(grads, weight):
    return lax.dot_general(
        grads, weight, (((1,), (1,)), ((), ())), preferred_element_type=jnp.float32
    )


def exchange(blocks, axis="tensor"):
    return lax.all_to_all(blocks, axis, 0, 0, tiled=True)


def spread(block, axis="tensor"):
    count = lax.axis_size(axis)
    return jnp.broadcast_to(block[None], (count,) + block.shape)


def after(value, *earlier):
    return lax.optimization_barrier((value,) + earlier)[0]


def after_all(values, *earlier):
    return lax.optimization_barrier((tuple(values),) + earlier)[0]


def pad_rows(rows, multiple):
    extra = -rows.shape[0] % multiple
    return jnp.pad(rows, ((0, extra),) + ((0, 0),) * (rows.ndim - 1))


def ring_route(step):
    count = lax.axis_size("tensor")
    ring = count // 2
    return [(i, i // ring * ring + (i + step) % ring) for i in range(count)]


def ring_gather(block):
    ring = lax.axis_size("tensor") // 2
    got = {k: lax.ppermute(block, "tensor", ring_route(k)) for k in (1, 3, 2)}
    return [block] + [got[k] for k in range(1, ring)]


def ring_scatter(blocks):
    got = {k: lax.ppermute(blocks[k], "tensor", ring_route(-k)) for k in (1, 3, 2)}
    return [blocks[0]] + [got[k] for k in range(1, len(blocks))]


def place_blocks(blocks, half_blocks):
    ring = len(blocks)
    place = lax.axis_index("tensor")
    ring_place, half = place % ring, place // ring
    rows = blocks[0].shape[0]
    out = jnp.zeros((2 * ring * rows,) + blocks[0].shape[1:], blocks[0].dtype)
    for k in range(ring):
        at_ring = (ring_place - k) % ring
        for which, block in ((half, blocks[k]), (1 - half, half_blocks[k])):
            out = lax.dynamic_update_slice_in_dim(out, block, (which * ring + at_ring) * rows, 0)
    return out


def half_swap(block):
    count = lax.axis_size("tensor")
    return lax.ppermute(block, "tensor", [(i, (i + count // 2) % count) for i in range(count)])


def core_swap(block):
    count = lax.axis_size("dp")
    return lax.ppermute(block, "dp", [(i, i ^ 1) for i in range(count)])


def dp_slice(rows, unit):
    places = lax.axis_size("dp")
    each = -(-rows.shape[0] // (places * unit)) * unit
    rows = pad_rows(rows, each * places)
    return lax.dynamic_slice_in_dim(rows, lax.axis_index("dp") * each, each, 0)


def dp_routes():
    count = lax.axis_size("dp")
    place = lax.axis_index("dp")
    stages = []
    for low, size in ((0, 2), (1, 4), (3, 2)):
        part = place // (1 << low) % size
        routes = []
        for step in range(1, size):
            route = []
            for source in range(count):
                here = source // (1 << low) % size
                there = (here + step) % size
                route.append((source, source + ((there - here) << low)))
            routes.append(route)
        stages.append((size, part, routes))
    return stages


def join(*values):
    return lax.optimization_barrier(values)


def low_slice(rows, unit):
    places = len(low_groups()[0])
    each = -(-rows.shape[0] // (places * unit)) * unit
    rows = pad_rows(rows, each * places)
    return lax.dynamic_slice_in_dim(rows, lax.axis_index("dp") % places * each, each, 0)


def far_swap(block):
    dp_count, count = lax.axis_size("dp"), lax.axis_size("tensor")
    route = [
        (d * count + t, (d ^ 1) * count + (t + count // 2) % count)
        for d in range(dp_count)
        for t in range(count)
    ]
    return lax.ppermute(block, ("dp", "tensor"), route)


def low_swap(block):
    count = lax.axis_size("dp")
    return lax.ppermute(block, "dp", [(i, i ^ 8) for i in range(count)])


def low_groups():
    return [list(range(8)), list(range(8, 16))]


def scatter_low(rows):
    return lax.psum_scatter(
        rows, "dp", scatter_dimension=0, tiled=True, axis_index_groups=low_groups()
    )


def gather_low(rows):
    return lax.all_gather(rows, "dp", axis=0, tiled=False, axis_index_groups=low_groups())


def scatter_stage(stage, grads):
    size, part, routes = dp_routes()[stage]
    rows = grads.shape[1] // size
    cut = lambda place: lax.dynamic_slice_in_dim(grads, place * rows, rows, 1)
    total = cut(part).astype(F32)
    for step, route in enumerate(routes, 1):
        send = cut((part + step) % size).astype(BF16)
        total = total + lax.ppermute(send, "dp", route).astype(F32)
    return total


def half_sum(own, other):
    return own.astype(F32) + half_swap(other.astype(BF16)).astype(F32)


VMEM_LIMIT = 60 * 1024 * 1024


def cost(micros):
    return pl.CostEstimate(flops=0, transcendentals=0, bytes_accessed=int(micros * 3.3e6))


def call(kernel, micros, outs, ins, name, grid=None, in_specs=None, out_specs=None, scratch=()):
    extra = {}
    if grid:
        extra = {"grid": grid, "in_specs": in_specs, "out_specs": out_specs}
    return pl.pallas_call(
        kernel,
        out_shape=outs,
        scratch_shapes=scratch,
        compiler_params=pltpu.CompilerParams(
            vmem_limit_bytes=VMEM_LIMIT,
            dimension_semantics=("arbitrary",) * len(grid) if grid else None,
        ),
        cost_estimate=cost(micros),
        name=name,
        **extra,
    )(*ins)


def dot(left, right):
    return lax.dot_general(left, right, (((1,), (0,)), ((), ())), preferred_element_type=F32)


def dot_t(left, right):
    return lax.dot_general(left, right, (((1,), (1,)), ((), ())), preferred_element_type=F32)


def t_dot(left, right):
    return lax.dot_general(left, right, (((0,), (0,)), ((), ())), preferred_element_type=F32)


def norm_parts(rows):
    centered = rows - jnp.mean(rows, -1, keepdims=True)
    scale = lax.rsqrt(jnp.mean(centered * centered, -1, keepdims=True) + 1e-06)
    return centered * scale, scale


def norm_back(unit, scale, gain, grad):
    weighted = grad * gain
    rows = scale * (
        weighted
        - jnp.mean(weighted, -1, keepdims=True)
        - unit * jnp.mean(weighted * unit, -1, keepdims=True)
    )
    return rows, jnp.sum(grad * unit, 0, keepdims=True)


def add_all(refs):
    total = refs[0][...].astype(F32)
    for ref in refs[1:]:
        total = total + ref[...].astype(F32)
    return total


def stack(parts):
    return jnp.concatenate(parts, 0)


HBM = pl.BlockSpec(memory_space=pltpu.HBM)


def load_blocks(refs, x_ref, sems):
    rows = x_ref.shape[0] // len(refs)
    copies = [
        pltpu.make_async_copy(
            ref.at[pl.ds(0, rows)], x_ref.at[pl.ds(i * rows, rows)], sems.at[i]
        )
        for i, ref in enumerate(refs)
    ]
    for copy in copies:
        copy.start()
    for copy in copies:
        copy.wait()


def put_blocks(refs, value):
    rows = refs[0].shape[0]
    for i, ref in enumerate(refs):
        ref[...] = value[i * rows : (i + 1) * rows].astype(BF16)


def struct(shape, kind):
    return jax.ShapeDtypeStruct(shape, kind)


def whole(shape):
    return pl.BlockSpec(shape, lambda *place: (0,) * len(shape))


def at(shape, row):
    return pl.BlockSpec(shape, lambda *place: (row,) + (0,) * (len(shape) - 1))


def swap(rows):
    quarter = rows.shape[1] // 4
    cut = [rows[:, i * quarter : (i + 1) * quarter] for i in range(4)]
    return jnp.concatenate([cut[1], cut[0], cut[3], cut[2]], 1)


def pack_spec(rows, width, place, share=16):
    return pl.BlockSpec((rows // share, share, width), lambda *step: (0, place // share, 0))


def pack_rows(pack_ref):
    return pack_ref[...].reshape(-1, pack_ref.shape[2])


def first_norms(got, skip_gain, norm1_gain, shift, along):
    count, rows, width = got.shape

    def kernel(got_ref, skip_ref, gain_ref, shift_ref, along_ref, merged_ref, hidden_ref, out_ref):
        merged = add_all([got_ref.at[i] for i in range(count)])
        merged_ref[...] = merged
        hidden = norm_parts(merged)[0] * skip_ref[...]
        hidden_ref[...] = hidden
        out_ref[:rows] = (norm_parts(hidden)[0] * gain_ref[...] + shift_ref[...]).astype(BF16)
        out_ref[rows:] = along_ref[...]

    outs = (
        struct((rows, width), F32),
        struct((rows, width), F32),
        struct((rows + along.shape[0], width), BF16),
    )
    ins = (got, skip_gain[None], norm1_gain[None], shift[None], along)
    return call(kernel, 2.5, outs, ins, "first_norms")


def mid_norm(pieces, hidden, gain):
    def kernel(*refs):
        hidden_ref, gain_ref, new_ref, out_ref = refs[len(pieces) :]
        new = hidden_ref[...] + add_all(refs[: len(pieces)])
        new_ref[...] = new
        out_ref[...] = (norm_parts(new)[0] * gain_ref[...]).astype(BF16)

    outs = (struct(hidden.shape, F32), struct(hidden.shape, BF16))
    return call(kernel, 1.5, outs, (*pieces, hidden, gain[None]), "mid_norm")


def mid_norm_back(pieces, residual, hidden, gain):
    def kernel(*refs):
        res_ref, hidden_ref, gain_ref, new_ref, out_ref, dgain_ref = refs[len(pieces) :]
        unit, scale = norm_parts(hidden_ref[...])
        grad, dgain = norm_back(unit, scale, gain_ref[...], add_all(refs[: len(pieces)]))
        dgain_ref[...] = dgain
        new = res_ref[...].astype(F32) + grad
        new_ref[...] = new
        out_ref[...] = new.astype(BF16)

    width = hidden.shape[1]
    outs = (struct(hidden.shape, F32), struct(hidden.shape, BF16), struct((1, width), F32))
    return call(kernel, 2, outs, (*pieces, residual, hidden, gain[None]), "mid_norm_back")


def last_norms(pieces, hidden_zero, merged, residual, gains, rows_two, rows_three, misc):
    rows, width = merged.shape
    many = len(pieces)

    def kernel(*refs):
        h0_ref, merged_ref, res_ref, g1_ref, gs_ref, two_ref, three_ref, misc_ref, out_ref = refs[many:]
        grad = add_all(refs[:many])
        shift_grad = jnp.sum(grad, 0, keepdims=True)
        unit, scale = norm_parts(h0_ref[...])
        step, norm1_grad = norm_back(unit, scale, g1_ref[...], grad)
        residual = res_ref[...] + step
        unit, scale = norm_parts(merged_ref[...])
        step, skip_grad = norm_back(unit, scale, gs_ref[...], residual)
        small = [skip_grad, norm1_grad, two_ref[...], three_ref[...], shift_grad, misc_ref[...]]
        small = stack(small + [jnp.zeros((16 - len(small), width), F32)]).astype(BF16)
        out_ref[:rows] = step.astype(BF16)
        out_ref[rows:] = small

    ins = (*pieces, hidden_zero, merged, residual, gains[0][None], gains[1][None])
    ins += (rows_two, rows_three, misc)
    return call(kernel, 3, struct((rows + 16, width), BF16), ins, "last_norms")


def project(parts, weight, other, cos_wide, sin_wide, qgain, kgain):
    width = parts[0].shape[1]
    tokens = cos_wide.shape[0]
    wide = weight.shape[0]
    each = wide // 3
    head = qgain.shape[0]
    heads = each // head
    many = len(parts)

    def kernel(*refs):
        w_ref, o_ref, cos_ref, sin_ref, qg_ref, kg_ref = refs[many : many + 6]
        x_ref, unit_ref, scale_ref, q_ref, kv_ref, sems = refs[many + 6 :]
        load_blocks(refs[:many], x_ref, sems)
        cos, sin = cos_ref[...], sin_ref[...]
        for s in range(2):
            out = dot_t(x_ref[...], w_ref[...] if s == 0 else pack_rows(o_ref))
            base = 2 * each * s
            kv_ref[:, base + each : base + 2 * each] = out[:, 2 * each :].astype(BF16)
            for h in range(heads):
                cut = lambda start: slice(start + h * head, start + (h + 1) * head)
                turn = lambda v: (v * cos + swap(v) * sin).astype(BF16)
                for part, gain_ref in ((0, qg_ref), (1, kg_ref)):
                    unit, scale = norm_parts(out[:, cut(part * each)])
                    n = (s * 2 + part) * heads + h
                    unit_ref[:, cut(base + part * each)] = unit
                    scale_ref[:, n : n + 1] = scale
                    if part == 0:
                        q_ref[:, cut(each * s)] = turn(unit * gain_ref[...])
                    else:
                        kv_ref[:, cut(base)] = turn(unit * gain_ref[...])

    outs = (
        struct((tokens, width), BF16),
        struct((tokens, 4 * each), F32),
        struct((tokens, 4 * heads), F32),
        struct((tokens, 2 * each), BF16),
        struct((tokens, 4 * each), BF16),
    )
    ins = (*parts, weight, other, cos_wide, sin_wide, qgain[None], kgain[None])
    specs = [HBM] * many + [whole(item.shape) for item in ins[many:]]
    specs[many + 1] = pack_spec(wide, width, 0, 48)
    return call(
        kernel, 6, outs, ins, "project", (1,), specs, tuple(whole(o.shape) for o in outs),
        (pltpu.SemaphoreType.DMA((many,)),),
    )


def key_rows(refs, shard, start, size, each):
    first = 2 * each * shard + start
    second = 2 * each * (1 - shard) + start
    return stack(
        [
            ref[:, first : first + size] if i < 2 else ref[:, second : second + size]
            for i, ref in enumerate(refs)
        ]
    )


def self_attention(queries, pairs, out_w, pack, head):
    tokens, both = queries.shape
    each = both // 2
    heads = each // head
    width = out_w.shape[1]
    scaling = head ** (-0.5)

    def kernel(q_ref, a_ref, b_ref, c_ref, d_ref, w_ref, o_ref, mixed_ref, total_ref, *out_refs):
        refs = (a_ref, b_ref, c_ref, d_ref)
        for s in range(2):
            for h in range(heads):
                n = s * heads + h
                cut = slice(n * head, (n + 1) * head)
                scores = dot_t(q_ref[:, cut], key_rows(refs, s, h * head, head, each)) * scaling
                most = jnp.max(scores, -1, keepdims=True)
                total = most + jnp.log(jnp.sum(jnp.exp(scores - most), -1, keepdims=True))
                total_ref[:, n : n + 1] = total
                shares = jnp.exp(scores - total).astype(BF16)
                mixture = dot(shares, key_rows(refs, s, each + h * head, head, each))
                mixed_ref[:, cut] = mixture.astype(BF16)
        out = dot(mixed_ref[:, :each], w_ref[...])
        out = out + dot(mixed_ref[:, each:], pack_rows(o_ref))
        put_blocks(out_refs, out)

    outs = (
        struct((tokens, both), BF16),
        struct((tokens, 2 * heads), F32),
    ) + (struct((tokens // 4, width), BF16),) * 4
    ins = (queries, *pairs, out_w, pack)
    specs = [whole(item.shape) for item in ins]
    specs[-1] = pack_spec(each, width, 48)
    return call(
        kernel, 5, outs, ins, "self_attention", (1,), specs, tuple(whole(o.shape) for o in outs)
    )


def self_attention_back(queries, pairs, totals, parts, out_w, pack, head):
    tokens, both = queries.shape
    each = both // 2
    heads = each // head
    rows, width = parts[0].shape
    scaling = head ** (-0.5)
    many = len(parts)

    def kernel(*refs):
        q_ref, a_ref, b_ref, c_ref, d_ref, total_ref, w_ref, o_ref = refs[many : many + 8]
        x_ref, dq_ref, own_ref, half_ref, core_ref, far_ref, dm_ref, sems = refs[many + 8 :]
        pair_refs = (a_ref, b_ref, c_ref, d_ref)
        load_blocks(refs[:many], x_ref, sems)
        dm_ref[:, :each] = dot_t(x_ref[...], w_ref[...]).astype(BF16)
        dm_ref[:, each:] = dot_t(x_ref[...], pack_rows(o_ref)).astype(BF16)

        def put(grads, shard, start):
            first = 2 * each * shard + start
            second = 2 * each * (1 - shard) + start
            cut = lambda i: grads[i * tokens : (i + 1) * tokens]
            own_ref[:, first : first + head] = cut(0)
            core_ref[:, first : first + head] = cut(1).astype(BF16)
            half_ref[:, second : second + head] = cut(2).astype(BF16)
            far_ref[:, second : second + head] = cut(3).astype(BF16)

        for s in range(2):
            for h in range(heads):
                n = s * heads + h
                cut = slice(n * head, (n + 1) * head)
                mine, grads = q_ref[:, cut], dm_ref[:, cut]
                keys_h = key_rows(pair_refs, s, h * head, head, each)
                values_h = key_rows(pair_refs, s, each + h * head, head, each)
                shares = jnp.exp(dot_t(mine, keys_h) * scaling - total_ref[:, n : n + 1])
                dshares = dot_t(grads, values_h)
                put(t_dot(shares.astype(BF16), grads), s, each + h * head)
                weighted = jnp.sum(shares * dshares, -1, keepdims=True)
                dscores = (shares * (dshares - weighted) * scaling).astype(BF16)
                dq_ref[:, cut] = dot(dscores, keys_h)
                put(t_dot(dscores, mine), s, h * head)

    outs = (
        struct((tokens, width), BF16),
        struct((tokens, both), F32),
        struct((tokens, 4 * each), F32),
        struct((tokens, 4 * each), BF16),
        struct((tokens, 4 * each), BF16),
        struct((tokens, 4 * each), BF16),
    )
    ins = (*parts, queries, *pairs, totals, out_w, pack)
    specs = [HBM] * many + [whole(item.shape) for item in ins[many:]]
    specs[-1] = pack_spec(each, width, 48)
    return call(
        kernel, 9, outs, ins, "self_attention_back", (1,), specs,
        tuple(whole(o.shape) for o in outs),
        (pltpu.VMEM((tokens, both), BF16), pltpu.SemaphoreType.DMA((many,))),
    )


def project_back(units, scales, cos_wide, sin_wide, qgain, kgain, dq, own, core, half, far, weight, other):
    tokens = units.shape[0]
    wide, width = weight.shape
    each = wide // 3
    head = qgain.shape[0]
    heads = each // head

    def kernel(unit_ref, scale_ref, cos_ref, sin_ref, qg_ref, kg_ref, dq_ref, own_ref, core_ref, half_ref, far_ref, w_ref, o_ref,
               mine_ref, other_ref, dqg_ref, dkg_ref, *out_refs):
        cos, sin = cos_ref[...], sin_ref[...]
        dkv = own_ref[...] + core_ref[...].astype(F32)
        dkv = dkv + half_ref[...].astype(F32) + far_ref[...].astype(F32)
        dgains = [jnp.zeros((1, head), F32), jnp.zeros((1, head), F32)]
        for s, to_ref in ((0, mine_ref), (1, other_ref)):
            base = 2 * each * s
            to_ref[:, 2 * each : 3 * each] = dkv[:, base + each : base + 2 * each].astype(BF16)
            for h in range(heads):
                cut = lambda start: slice(start + h * head, start + (h + 1) * head)
                for part, gain_ref in ((0, qg_ref), (1, kg_ref)):
                    turned = dq_ref[:, cut(each * s)] if part == 0 else dkv[:, cut(base)]
                    grad = turned * cos - swap(turned) * sin
                    n = (s * 2 + part) * heads + h
                    unit = unit_ref[:, cut(base + part * each)]
                    grad, dgain = norm_back(unit, scale_ref[:, n : n + 1], gain_ref[...], grad)
                    dgains[part] = dgains[part] + dgain
                    to_ref[:, cut(part * each)] = grad.astype(BF16)
        dqg_ref[...], dkg_ref[...] = dgains
        out = dot(mine_ref[...], w_ref[...])
        put_blocks(out_refs, out + dot(other_ref[...], pack_rows(o_ref)))

    outs = (
        struct((tokens, wide), BF16),
        struct((tokens, wide), BF16),
        struct((1, head), F32),
        struct((1, head), F32),
    ) + (struct((tokens // 4, width), BF16),) * 4
    ins = (units, scales, cos_wide, sin_wide, qgain[None], kgain[None], dq, own, core, half, far, weight, other)
    specs = [whole(item.shape) for item in ins]
    specs[-1] = pack_spec(wide, width, 0, 48)
    return call(
        kernel, 8, outs, ins, "project_back", (1,), specs, tuple(whole(o.shape) for o in outs)
    )


def text_shares(scores, scaling, count):
    place = lax.broadcasted_iota(jnp.int32, scores.shape, 1)
    scores = jnp.where(place < count, scores * scaling, -1e30)
    most = jnp.max(scores, -1, keepdims=True)
    total = most + jnp.log(jnp.sum(jnp.exp(scores - most), -1, keepdims=True))
    return jnp.exp(scores - total)


def cross_layer(parts, cq_w, out_w, pack, text, other_text, gain, text_count):
    rows, width = parts[0].shape
    tokens = rows * len(parts)
    each = cq_w.shape[0]
    head = gain.shape[0]
    heads = each // head
    scaling = head ** (-0.5)
    many = len(parts)

    def kernel(*refs):
        cq_ref, w_ref, ocq_ref, ow_ref, text_ref, otext_ref, gain_ref = refs[many : many + 7]
        x_ref, raw_ref, mixed_ref, *out_refs, sems = refs[many + 7 :]
        load_blocks(refs[:many], x_ref, sems)
        raw_ref[:, :each] = dot_t(x_ref[...], cq_ref[...])
        raw_ref[:, each:] = dot_t(x_ref[...], pack_rows(ocq_ref))
        for s, keys_ref in ((0, text_ref), (1, otext_ref)):
            for h in range(heads):
                n = s * heads + h
                cut = slice(n * head, (n + 1) * head)
                mine = (norm_parts(raw_ref[:, cut])[0] * gain_ref[...]).astype(BF16)
                scores = dot_t(mine, keys_ref[:, h * head : (h + 1) * head])
                shares = text_shares(scores, scaling, text_count).astype(BF16)
                values = keys_ref[:, each + h * head : each + (h + 1) * head]
                mixed_ref[:, cut] = dot(shares, values).astype(BF16)
        out = dot(mixed_ref[:, :each], w_ref[...])
        out = out + dot(mixed_ref[:, each:], pack_rows(ow_ref))
        put_blocks(out_refs, out)

    outs = (
        struct((tokens, width), BF16),
        struct((tokens, 2 * each), F32),
        struct((tokens, 2 * each), BF16),
    ) + (struct((rows, width), BF16),) * many
    ins = (*parts, cq_w, out_w, pack, pack, text, other_text, gain[None])
    specs = [HBM] * many + [whole(item.shape) for item in ins[many:]]
    specs[many + 2] = pack_spec(each, width, 0)
    specs[many + 3] = pack_spec(each, width, 16)
    return call(
        kernel, 7, outs, ins, "cross_layer", (1,), specs, tuple(whole(o.shape) for o in outs),
        (pltpu.SemaphoreType.DMA((many,)),),
    )


def cross_layer_back(parts, raw, cq_w, out_w, pack, text, other_text, gain, text_count):
    rows, width = parts[0].shape
    tokens = rows * len(parts)
    each = cq_w.shape[0]
    head = gain.shape[0]
    heads = each // head
    scaling = head ** (-0.5)
    many = len(parts)

    def kernel(*refs):
        raw_ref, cq_ref, w_ref, ocq_ref, ow_ref, text_ref, otext_ref, gain_ref = refs[many : many + 8]
        x_ref, draw_ref, dtext_ref, dother_ref, dgain_ref, *out_refs, dm_ref, sems = refs[many + 8 :]
        load_blocks(refs[:many], x_ref, sems)
        dm_ref[:, :each] = dot_t(x_ref[...], w_ref[...]).astype(BF16)
        dm_ref[:, each:] = dot_t(x_ref[...], pack_rows(ow_ref)).astype(BF16)
        dgain = jnp.zeros((1, head), F32)
        for s, keys_ref, to_ref in ((0, text_ref, dtext_ref), (1, otext_ref, dother_ref)):
            for h in range(heads):
                n = s * heads + h
                cut = slice(n * head, (n + 1) * head)
                kcut = slice(h * head, (h + 1) * head)
                vcut = slice(each + h * head, each + (h + 1) * head)
                unit, scale = norm_parts(raw_ref[:, cut])
                mine = (unit * gain_ref[...]).astype(BF16)
                shares = text_shares(dot_t(mine, keys_ref[:, kcut]), scaling, text_count)
                dshares = dot_t(dm_ref[:, cut], keys_ref[:, vcut])
                to_ref[:, vcut] = t_dot(shares.astype(BF16), dm_ref[:, cut]).astype(BF16)
                weighted = jnp.sum(shares * dshares, -1, keepdims=True)
                dscores = (shares * (dshares - weighted) * scaling).astype(BF16)
                to_ref[:, kcut] = t_dot(dscores, mine).astype(BF16)
                grad, step = norm_back(unit, scale, gain_ref[...], dot(dscores, keys_ref[:, kcut]))
                dgain = dgain + step
                draw_ref[:, cut] = grad.astype(BF16)
        dgain_ref[...] = dgain
        out = dot(draw_ref[:, :each], cq_ref[...])
        out = out + dot(draw_ref[:, each:], pack_rows(ocq_ref))
        put_blocks(out_refs, out)

    outs = (
        struct((tokens, width), BF16),
        struct((tokens, 2 * each), BF16),
        struct(text.shape, BF16),
        struct(text.shape, BF16),
        struct((1, head), F32),
    ) + (struct((rows, width), BF16),) * many
    ins = (*parts, raw, cq_w, out_w, pack, pack, text, other_text, gain[None])
    specs = [HBM] * many + [whole(item.shape) for item in ins[many:]]
    specs[many + 3] = pack_spec(each, width, 0)
    specs[many + 4] = pack_spec(each, width, 16)
    return call(
        kernel, 10, outs, ins, "cross_layer_back", (1,), specs,
        tuple(whole(o.shape) for o in outs),
        (pltpu.VMEM((tokens, 2 * each), BF16), pltpu.SemaphoreType.DMA((many,))),
    )


def feed_forward(parts, cot, fc1_w, fc2_w, pack):
    rows, width = parts[0].shape
    tokens = rows * len(parts)
    hidden = fc2_w.shape[0]
    block = hidden // 2
    places = pack.shape[0]
    each = hidden // places
    both = 2 * each
    root = (2 / 3.141592653589793) ** 0.5
    many = len(parts)

    def kernel(*refs):
        cot_ref, w1_ref, w2_ref, pack_ref, x_ref, acts_ref, *out_refs, acc_ref, sum_ref, sems = refs[many:]
        step = pl.program_id(0)

        @pl.when(step == 0)
        def _():
            load_blocks(refs[:many], x_ref, sems)
            acc_ref[...] = jnp.zeros_like(acc_ref)
            sum_ref[...] = jnp.zeros_like(sum_ref)

        def work(pre, w2, back):
            square = pre * pre
            bent = jnp.tanh(root * pre * (1 + 0.044715 * square))
            part = 0.5 * (1 + bent)
            slope = part + 0.5 * pre * (1 - bent * bent) * root * (1 + 3 * 0.044715 * square)
            grad = (dot_t(cot_ref[...], w2) * slope).astype(BF16)
            acts_ref[0, 0] = grad
            active = (pre * part).astype(BF16)
            acts_ref[0, 1] = active
            acc_ref[...] += back(grad)
            sum_ref[...] += dot(active, w2)

        @pl.when(step < 2)
        def _():
            weight = w1_ref[...]
            work(dot(x_ref[...], weight), w2_ref[...], lambda grad: dot_t(grad, weight))

        @pl.when(step >= 2)
        def _():
            weight = pack_ref[:, :each].reshape(block, width)
            second = pack_ref[:, each:].reshape(block, width)
            work(dot_t(x_ref[...], weight), second, lambda grad: dot(grad, weight))

        @pl.when(step == 3)
        def _():
            put_blocks(out_refs[:many], acc_ref[...])
            put_blocks(out_refs[many:], sum_ref[...])

    low = lambda i: jnp.minimum(i, 1)
    high = lambda i: jnp.maximum(i - 2, 0)
    outs = (
        struct((tokens, width), BF16),
        struct((2, 2, tokens, hidden), BF16),
    ) + (struct((rows, width), BF16),) * (2 * many)
    out_specs = (
        whole((tokens, width)),
        pl.BlockSpec((1, 2, tokens, block), lambda i: (i // 2, 0, 0, i % 2)),
    ) + (whole((rows, width)),) * (2 * many)
    in_specs = [HBM] * many + [
        whole(cot.shape),
        pl.BlockSpec((width, block), lambda i: (0, low(i))),
        pl.BlockSpec((block, width), lambda i: (low(i), 0)),
        pl.BlockSpec((places // 2, both, width), lambda i: (high(i), 0, 0)),
    ]
    return call(
        kernel, 9, outs, (*parts, cot, fc1_w, fc2_w, pack), "feed_forward", (4,), in_specs, out_specs,
        (
            pltpu.VMEM((tokens, width), F32),
            pltpu.VMEM((tokens, width), F32),
            pltpu.SemaphoreType.DMA((many,)),
        ),
    )


def feed_forward_grads(acts, rows_in, cot, places):
    _, _, tokens, hidden = acts.shape
    width = cot.shape[1]
    share = 2 * hidden // places

    def kernel(acts_ref, x_ref, cot_ref, out_ref):
        which = pl.program_id(1)

        def put(right_ref):
            grads = t_dot(acts_ref[0, 0], right_ref[...]).astype(BF16)
            out_ref[...] = grads.reshape(out_ref.shape)

        pl.when(which == 0)(lambda: put(x_ref))
        pl.when(which == 1)(lambda: put(cot_ref))

    return call(
        kernel,
        7,
        struct((places, 2, share, width), BF16),
        (acts, rows_in, cot),
        "feed_forward_grads",
        (2, 2),
        [
            pl.BlockSpec((1, 1, tokens, hidden), lambda s, w: (s, w, 0, 0)),
            whole(rows_in.shape),
            whole(cot.shape),
        ],
        pl.BlockSpec((places // 2, 1, share, width), lambda s, w: (w, s, 0, 0)),
    )


def put_shares(out_ref, shard, to, share, rows_ref):
    stop, width = rows_ref.shape
    for place in range(out_ref.shape[0]):
        begin = min(place * share, stop)
        count = min(share, stop - begin)
        if count:
            out_ref[place, shard, to : to + count] = rows_ref[begin : begin + count]
        if count < share:
            out_ref[place, shard, to + count : to + share] = jnp.zeros((share - count, width), BF16)


def cross_grads(draw, mixed, rows_in, grad_rows, places, share):
    each = draw.shape[1] // 2
    width = rows_in.shape[1]

    def kernel(draw_ref, mixed_ref, x_ref, d_ref, out_ref, hold_ref):
        for s in range(2):
            cut = slice(s * each, (s + 1) * each)
            hold_ref[:each] = t_dot(draw_ref[:, cut], x_ref[...]).astype(BF16)
            hold_ref[each:] = t_dot(mixed_ref[:, cut], d_ref[...]).astype(BF16)
            put_shares(out_ref, s, 0, share, hold_ref)

    ins = (draw, mixed, rows_in, grad_rows)
    scratch = (pltpu.VMEM((2 * each, width), BF16),)
    return call(kernel, 4, struct((places, 2, share, width), BF16), ins, "cross_grads", scratch=scratch)


def self_grads(mine, other, mixed, rows_in, grad_rows, places, share):
    wide = mine.shape[1]
    each = wide // 3
    width = rows_in.shape[1]

    def kernel(mine_ref, other_ref, mixed_ref, x_ref, d_ref, out_ref, hold_ref):
        for s, grad_ref in ((0, mine_ref), (1, other_ref)):
            cut = slice(s * each, (s + 1) * each)
            hold_ref[:wide] = t_dot(grad_ref[...], x_ref[...]).astype(BF16)
            hold_ref[wide:] = t_dot(mixed_ref[:, cut], d_ref[...]).astype(BF16)
            put_shares(out_ref, s, 0, share, hold_ref)

    ins = (mine, other, mixed, rows_in, grad_rows)
    scratch = (pltpu.VMEM((wide + each, width), BF16),)
    return call(kernel, 5, struct((places, 2, share, width), BF16), ins, "self_grads", scratch=scratch)


def skip_grads(parts, joined_own, joined_other, long):
    rows, width = parts[0].shape
    small = 16
    rows -= small
    tokens, slab = joined_own.shape
    many = len(parts)

    def kernel(*refs):
        own_ref, other_ref, x_ref, out_ref, all_ref, sems = refs[many:]
        load_blocks(refs[:many], all_ref, sems)
        total = jnp.zeros((small, width), F32)
        for i in range(many):
            start = i * (rows + small)
            x_ref[i * rows : (i + 1) * rows] = all_ref[start : start + rows]
            total = total + all_ref[start + rows : start + rows + small].astype(F32)
        for s, left_ref in ((0, own_ref), (1, other_ref)):
            out_ref[s, :slab] = t_dot(left_ref[...], x_ref[...])
            out_ref[s, slab : slab + small] = total
            out_ref[s, slab + small :] = jnp.zeros((long - slab - small, width), F32)

    outs = (struct((tokens, width), BF16), struct((2, long, width), F32))
    ins = (*parts, joined_own, joined_other)
    return call(
        kernel, 4, outs, ins, "skip_grads", (1,),
        [HBM] * many + [whole(joined_own.shape), whole(joined_other.shape)],
        tuple(whole(o.shape) for o in outs),
        (pltpu.VMEM((many * (rows + small), width), BF16), pltpu.SemaphoreType.DMA((many,))),
    )


def joined_grads(rows_in, pack, slab):
    tokens, width = rows_in.shape
    held, count, deep, _ = pack.shape
    half = count // 2

    def kernel(x_ref, pack_ref, one_ref, two_ref):
        for step, out_ref in ((0, one_ref), (1, two_ref)):

            @pl.when(pl.program_id(0) == step)
            def _(out_ref=out_ref):
                for j in range(half):
                    weight = pack_ref[:, j].reshape(held * deep, width)[:slab]
                    out_ref[:, j * slab : (j + 1) * slab] = dot_t(x_ref[...], weight)

    outs = (struct((tokens, width), F32), struct((tokens, width), F32))
    return call(
        kernel, 9, outs, (rows_in, pack), "joined_grads", (2,),
        [
            whole(rows_in.shape),
            pl.BlockSpec((held, half, deep, width), lambda i: (0, i, 0, 0)),
        ],
        (whole((tokens, width)), whole((tokens, width))),
    )


def feed_forward_out(sums, share):
    places, _, width = sums.shape
    half = places // 2
    hidden = half * share

    def kernel(sum_ref, one_ref, two_ref):
        @pl.when(pl.program_id(0) == 0)
        def _():
            one_ref[...] = sum_ref[...].reshape(hidden, width).astype(F32).T

        @pl.when(pl.program_id(0) == 1)
        def _():
            two_ref[...] = sum_ref[...].reshape(hidden, width).astype(F32)

    outs = (struct((width, hidden), F32), struct((hidden, width), F32))
    return call(
        kernel, 6, outs, (sums,), "feed_forward_out", (2,),
        [pl.BlockSpec((half, share, width), lambda i: (i, 0, 0))],
        (whole((width, hidden)), whole((hidden, width))),
    )


def text_layer(tokens, ckv, gain, rows):
    count, width = tokens.shape
    packed = ckv.ndim == 3
    both = ckv.shape[2] // 4 if packed else ckv.shape[1]
    each = both // 2
    head = gain.shape[0]
    heads = each // head

    def kernel(x_ref, w_ref, gain_ref, pair_ref, unit_ref, scale_ref, *more):
        if packed:
            weight_ref = more[0]
            deep = w_ref.shape[1]
            for place in range(w_ref.shape[0]):
                for k in range(4):
                    start = (place * 4 + k) * deep
                    weight_ref[start : start + deep] = w_ref[place, :, k * both : (k + 1) * both]
        else:
            weight_ref = w_ref
        out = dot(x_ref[...], weight_ref[...])
        pair_ref[...] = jnp.zeros_like(pair_ref)
        pair_ref[:count, each:] = out[:, each:].astype(BF16)
        for h in range(heads):
            cut = slice(h * head, (h + 1) * head)
            unit, scale = norm_parts(out[:, cut])
            unit_ref[:, cut] = unit
            scale_ref[:, h : h + 1] = scale
            pair_ref[:count, cut] = (unit * gain_ref[...]).astype(BF16)

    outs = (
        struct((rows, both), BF16),
        struct((count, each), F32),
        struct((count, heads), F32),
    )
    specs = [whole(tokens.shape), whole(ckv.shape), whole((1, head))]
    if packed:
        outs += (struct((width, both), BF16),)
        deep = width // ckv.shape[0] // 4
        place = ckv.shape[1] // deep - 1
        specs[1] = pl.BlockSpec((ckv.shape[0], deep, ckv.shape[2]), lambda *step: (0, place, 0))
    return call(
        kernel, 4, outs, (tokens, ckv, gain[None]), "text_layer", (1,), specs,
        tuple(whole(o.shape) for o in outs),
    )


def text_layer_back(crosses, pairs, units, scales, tokens, ckvs, gain):
    count, width = tokens.shape
    both = ckvs[0].shape[1]
    each = both // 2
    head = gain.shape[0]
    heads = each // head
    places, _, first, wide = crosses.shape
    deep = 48
    more = 48
    long = more * places

    def kernel(first_ref, a_ref, b_ref, ua_ref, ub_ref, sa_ref, sb_ref, x_ref, wa_ref, wb_ref, gain_ref, out_ref, dw_ref, grad_ref, part_ref):
        dgain = jnp.zeros((1, head), F32)
        part = jnp.zeros((count, width), F32)
        for s, (pair_ref, unit_ref, scale_ref, w_ref) in enumerate(
            ((a_ref, ua_ref, sa_ref, wa_ref), (b_ref, ub_ref, sb_ref, wb_ref))
        ):
            grad_ref[:, each:] = pair_ref[:count, each:]
            for h in range(heads):
                cut = slice(h * head, (h + 1) * head)
                grad, step = norm_back(
                    unit_ref[:, cut], scale_ref[:, h : h + 1], gain_ref[...], pair_ref[:count, cut].astype(F32)
                )
                dgain = dgain + step
                grad_ref[:, cut] = grad.astype(BF16)
            dw_ref[...] = t_dot(grad_ref[...], x_ref[...]).astype(BF16)
            part = part + dot_t(grad_ref[...], w_ref[...])
            for place in range(places):
                begin = min(place * deep, both)
                held = min(deep, both - begin)
                out_ref[place, s, :first] = first_ref[place, s]
                out_ref[place, s, first : first + deep] = jnp.zeros((deep, wide), BF16)
                out_ref[place, s, first : first + held, :width] = dw_ref[begin : begin + held]
        part_ref[...] = jnp.zeros_like(part_ref)
        part_ref[:count, :width] = part
        part_ref[long - 1 :, :head] = dgain
        for place in range(places):
            rows = part_ref[place * more : (place + 1) * more].astype(BF16)
            for s in range(2):
                out_ref[place, s, first + deep :] = rows

    ins = (crosses, *pairs, *units, *scales, tokens, *ckvs, gain[None])
    scratch = (
        pltpu.VMEM((both, width), BF16),
        pltpu.VMEM((count, both), BF16),
        pltpu.VMEM((long, wide), F32),
    )
    return call(
        kernel, 9, struct((places, 2, first + deep + more, wide), BF16), ins, "text_layer_back", scratch=scratch
    )


def local(
    latent,
    skip_input,
    text_tokens,
    condition,
    positions,
    cotangent,
    skip_w,
    skip_gain,
    norm1_gain,
    mod_w,
    qkv_w,
    qnorm_gain,
    knorm_gain,
    attn_out_w,
    norm2_gain,
    cq_w,
    ckv_w,
    cqnorm_gain,
    cknorm_gain,
    cross_out_w,
    norm3_gain,
    fc1_w,
    fc2_w,
):
    token_count, model_width = latent.shape
    head_dim = qnorm_gain.shape[0]
    local_width = cq_w.shape[1]
    local_heads = local_width // head_dim
    slab_width = skip_w.shape[0]
    hidden_width = fc1_w.shape[1]
    text_count, text_width = text_tokens.shape
    tensor_place = lax.axis_index("tensor")
    tensor_count = lax.axis_size("tensor")
    dp_count = lax.axis_size("dp")
    low_count = len(low_groups()[0])
    part_count = token_count // tensor_count
    ring = tensor_count // 2
    ring_place, half = tensor_place % ring, tensor_place // ring
    qkv_rows = 3 * local_width

    def own_rows(rows):
        return lax.dynamic_slice_in_dim(rows, tensor_place * part_count, part_count, 0)

    def ring_rows(rows, which):
        first = which * ring
        return jnp.concatenate(
            [
                lax.dynamic_slice_in_dim(
                    rows, (first + (ring_place - k) % ring) * part_count, part_count, 0
                )
                for k in range(ring)
            ],
            0,
        )

    joined = jnp.concatenate([latent, skip_input], 1)
    joined_part = lax.dynamic_slice_in_dim(joined, tensor_place * slab_width, slab_width, 1)
    partial = jnp.dot(joined_part, skip_w, preferred_element_type=F32).astype(BF16)
    got = exchange(partial.reshape(tensor_count, part_count, model_width))

    dp_place = lax.axis_index("dp")
    qkv_flat = qkv_w.transpose(1, 2, 0).reshape(qkv_rows, model_width)
    cq_turned = cq_w.T
    shares = [dp_slice(qkv_flat, 48), dp_slice(attn_out_w, 16)]
    pack = lax.all_gather(half_swap(jnp.concatenate(shares, 0)), "dp", axis=0, tiled=False)
    ckv_flat = ckv_w.reshape(text_width, 2 * local_width)
    text_pair, text_units, text_scales = text_layer(
        text_tokens, ckv_flat, cknorm_gain, model_width // 4
    )
    share = hidden_width // dp_count
    deep = text_width // dp_count // 4
    share = hidden_width // low_count
    low_place = dp_place % low_count
    ff_share = [
        lax.dynamic_slice_in_dim(fc1_w, low_place * share, share, 1).T,
        lax.dynamic_slice_in_dim(fc2_w, low_place * share, share, 0),
    ]
    ff_share = jnp.concatenate(ff_share, 0)
    ckv_share = lax.dynamic_slice_in_dim(ckv_flat, dp_place * 4 * deep, 4 * deep, 0)
    cross_share = [dp_slice(rows, 16) for rows in (cq_turned, cross_out_w)]
    cross_share.append(jnp.concatenate(jnp.split(ckv_share, 4), 1))
    cross_share = jnp.concatenate(cross_share, 0)
    silu_cond = jax.nn.silu(condition.astype(F32)).astype(BF16)
    shift = jnp.dot(silu_cond[None], mod_w, preferred_element_type=F32)[0]
    cos_wide, sin_wide = rotary_tables(ring_rows(positions, half), head_dim)
    cot_rows = ring_rows(cotangent, half)
    got, cos_wide, sin_wide, shift, text_pair, cot_rows, ff_share, cross_share = join(
        got, cos_wide, sin_wide, shift, text_pair, cot_rows, ff_share, cross_share
    )
    skip_share = low_slice(skip_w, 16)
    merged, hidden_zero, normed = first_norms(got, skip_gain, norm1_gain, shift, skip_share)
    normed_parts = ring_gather(normed)
    cross_share = half_swap(after(cross_share, normed))
    rows_one, units, scales, queries, own_pair = project(
        normed_parts, qkv_flat, pack, cos_wide, sin_wide, qnorm_gain, knorm_gain
    )
    own_pair, cross_share = join(own_pair, cross_share)
    cross_pack = lax.all_gather(cross_share, "dp", axis=0, tiled=False)
    core_pair = core_swap(own_pair)
    half_pair = half_swap(own_pair)
    pairs = (own_pair, core_pair, half_pair, core_swap(half_pair))
    mixed_one, totals, *partial = self_attention(
        queries, pairs, attn_out_w, pack, head_dim
    )
    ff_share = half_swap(after(ff_share, half_pair))
    hidden_one, normed = mid_norm(ring_scatter(partial), hidden_zero, norm2_gain)
    ff_pack = gather_low(after(ff_share, normed))
    skip_rows = jnp.concatenate([part[part_count:] for part in normed_parts], 0)
    skip_half = half_swap(after(skip_rows, normed))
    other_text, other_units, other_scales, other_ckv = text_layer(
        text_tokens, after(cross_pack, normed), cknorm_gain, model_width // 4
    )
    *normed_parts, other_text = join(*ring_gather(normed), other_text)
    rows_two, cross_raw, mixed_two, *partial = cross_layer(
        normed_parts,
        cq_turned,
        cross_out_w,
        cross_pack,
        text_pair,
        other_text,
        cqnorm_gain,
        text_count,
    )
    *partial, skip_half = join(*partial, skip_half)
    skip_rows = place_blocks(jnp.split(skip_rows, ring), jnp.split(skip_half, ring))
    *pieces, skip_rows = join(*ring_scatter(partial), skip_rows)
    hidden_two, normed = mid_norm(pieces, hidden_one, norm3_gain)
    skip_pack = gather_low(
        skip_rows.reshape(tensor_count, -1, model_width)
    )
    rows_three, acts, *partial = feed_forward(
        ring_gather(normed), cot_rows, fc1_w, fc2_w, ff_pack
    )
    partial, last_partial = partial[:ring], partial[ring:]

    fc_grads = feed_forward_grads(acts, rows_three, cot_rows, low_count)
    *pieces, fc_grads = join(*ring_scatter(partial), fc_grads.reshape(-1, model_width))
    fc_grads = scatter_low(after(fc_grads, skip_pack))
    residual, out_grad, norm3_grad = mid_norm_back(
        pieces, own_rows(cotangent), hidden_two, norm3_gain
    )
    out_parts = ring_gather(out_grad)
    grad_rows_two, cross_raw_grad, text_own, text_other, cqnorm_grad, *partial = cross_layer_back(
        out_parts,
        cross_raw,
        cq_turned,
        cross_out_w,
        cross_pack,
        text_pair,
        other_text,
        cqnorm_gain,
        text_count,
    )
    crosses = cross_grads(
        cross_raw_grad, mixed_two, rows_two, grad_rows_two, low_count, 48
    )
    *pieces, crosses = join(*ring_scatter(partial), crosses)
    residual, out_grad, norm2_grad = mid_norm_back(pieces, residual, hidden_one, norm2_gain)
    early_sums = text_layer_back(
        crosses,
        (text_own, text_other),
        (text_units, other_units),
        (text_scales, other_scales),
        after(text_tokens, out_grad),
        (ckv_flat, other_ckv),
        cknorm_gain,
    )
    *out_parts, early_sums, fc_grads = join(*ring_gather(out_grad), early_sums, fc_grads)
    early_sums = scatter_low(early_sums.reshape(-1, model_width))
    grad_rows_one, query_grad, pair_grad, half_grad, core_grad, far_grad = self_attention_back(
        queries,
        pairs,
        totals,
        out_parts,
        attn_out_w,
        pack,
        head_dim,
    )
    core_grad = core_swap(core_grad)
    half_grad = half_swap(half_grad)
    far_grad = far_swap(far_grad)
    core_grad, half_grad, far_grad = join(core_grad, half_grad, far_grad)
    fc_grads = after(fc_grads, half_grad)
    share = fc_grads.shape[0] // 2
    fc_grads = half_sum(fc_grads[:share], fc_grads[share:])
    projected_grad, projected_other, qnorm_grad, knorm_grad, *partial = project_back(
        units,
        scales,
        cos_wide,
        sin_wide,
        qnorm_gain,
        knorm_gain,
        query_grad,
        pair_grad,
        core_grad,
        half_grad,
        far_grad,
        qkv_flat,
        pack,
    )
    *partial, fc_grads = join(*partial, fc_grads)
    fc_grads = fc_grads + low_swap(fc_grads.astype(BF16)).astype(F32)
    late_sums = self_grads(
        projected_grad, projected_other, mixed_one, rows_one, grad_rows_one, low_count, 96
    )
    early_sums = after(early_sums, qnorm_grad)
    early_share = early_sums.shape[0] // 2
    early_sums = half_sum(early_sums[:early_share], early_sums[early_share:])
    *pieces, late_sums, fc_grads, early_sums = join(
        *ring_scatter(partial), late_sums, fc_grads, early_sums
    )
    late_sums = scatter_low(late_sums.reshape(-1, model_width))
    misc = jnp.concatenate([qnorm_grad, knorm_grad, cqnorm_grad], 1)
    misc = jnp.pad(misc, ((0, 0), (0, model_width - misc.shape[1])))
    merged_out = last_norms(
        pieces,
        hidden_zero,
        merged,
        residual,
        (norm1_gain, skip_gain),
        norm2_grad,
        norm3_grad,
        misc,
    )
    joined_rows = ring_rows(joined, half)
    joined_own = lax.dynamic_slice_in_dim(joined_rows, tensor_place * slab_width, slab_width, 1)
    joined_other = lax.dynamic_slice_in_dim(
        joined_rows, (tensor_place + ring) % tensor_count * slab_width, slab_width, 1
    )
    merged_out, early_sums = join(merged_out, early_sums)
    early_sums = early_sums + low_swap(early_sums.astype(BF16)).astype(F32)
    *merged_parts, joined_own, joined_other, early_sums = join(
        *ring_gather(merged_out), joined_own, joined_other, early_sums
    )

    text_rows = early_sums[-48:]
    for part in ring_gather(text_rows.astype(BF16))[1:]:
        text_rows = text_rows + part.astype(F32)

    last_rows = -(-(slab_width + 16) // (8 * dp_count)) * 8 * dp_count
    merged_rows, last_sums = skip_grads(merged_parts, joined_own, joined_other, last_rows)
    merged_rows, last_sums, text_rows = join(merged_rows, last_sums, text_rows)
    early_sums = jnp.concatenate([fc_grads, early_sums[:-48], text_rows], 0).astype(BF16)
    early_sums = gather_low(after(early_sums, late_sums))
    merged_half = half_swap(merged_rows)
    last_sums = scatter_stage(0, last_sums)
    last_sums, merged_half = join(last_sums, merged_half)
    last_sums = scatter_stage(1, last_sums)
    output = hidden_two
    for piece in ring_scatter(after_all(last_partial, merged_half)):
        output = output + piece.astype(F32)
    last_sums, output = join(last_sums, output)
    share = late_sums.shape[0] // 2
    own_sums = jnp.concatenate([late_sums[:share].astype(F32), last_sums[0]], 0)
    other_sums = jnp.concatenate([late_sums[share:], last_sums[1].astype(BF16)], 0)
    last_sums = half_sum(own_sums, other_sums)
    output = jnp.concatenate(ring_gather(output.astype(BF16)), 0)
    last_sums, output = join(last_sums, output)
    last_sums = last_sums + low_swap(last_sums.astype(BF16)).astype(F32)
    merged_grad = place_blocks(jnp.split(merged_rows, ring), jnp.split(merged_half, ring))
    latent_grad, skip_grad = joined_grads(merged_grad, skip_pack, slab_width)
    last_sums = gather_low(after(last_sums, early_sums).astype(BF16))
    output_half = half_swap(after(output, early_sums))
    fc_share = fc_grads.shape[0]
    fc1_grad, fc2_grad = feed_forward_out(early_sums, fc_share)
    output = place_blocks(jnp.split(output, ring), jnp.split(output_half, ring))
    cross_sums = early_sums[:, fc_share : fc_share + 48].reshape(-1, model_width)
    cq_grad = cross_sums[:local_width].T.astype(F32)
    cross_out_grad = cross_sums[local_width : 2 * local_width].astype(F32)
    ckv_grad = early_sums[:, fc_share + 48 : fc_share + 96].reshape(-1, model_width)
    ckv_grad = ckv_grad[: 2 * local_width, :text_width].astype(F32)
    ckv_grad = ckv_grad.T.reshape(text_width, 2, local_width)
    text_rows = early_sums[:, fc_share + 96 :].reshape(-1, model_width).astype(F32)
    text_grad = text_rows[:text_count, :text_width]
    cknorm_grad = text_rows[-1, :head_dim]
    (
        last_sums,
        latent_grad,
        skip_grad,
        output,
        fc1_grad,
        fc2_grad,
        cq_grad,
        cross_out_grad,
        ckv_grad,
        text_grad,
        cknorm_grad,
    ) = join(
        last_sums,
        latent_grad,
        skip_grad,
        output,
        fc1_grad,
        fc2_grad,
        cq_grad,
        cross_out_grad,
        ckv_grad,
        text_grad,
        cknorm_grad,
    )
    self_sums = last_sums[:, :share].reshape(-1, model_width)
    qkv_grad = self_sums[:qkv_rows].T.astype(F32).reshape(model_width, 3, local_width)
    attn_out_grad = self_sums[qkv_rows : qkv_rows + local_width].astype(F32)
    last_sums = last_sums[:, share:].reshape(4, 2, -1, model_width).transpose(1, 0, 2, 3)
    last_sums = last_sums.reshape(-1, model_width)
    skip_w_grad = last_sums[:slab_width].astype(F32)
    small = last_sums[slab_width:].astype(F32)
    skip_gain_grad, norm1_grad, norm2_grad, norm3_grad, mod_vector = [small[i] for i in range(5)]
    qnorm_grad, knorm_grad, cqnorm_grad = [
        small[5, i * head_dim : (i + 1) * head_dim] for i in range(3)
    ]
    mod_grad = silu_cond.astype(F32)[:, None] * mod_vector[None, :]
    return (
        output,
        latent_grad,
        skip_grad,
        text_grad,
        skip_w_grad,
        skip_gain_grad,
        norm1_grad,
        mod_grad,
        qkv_grad,
        qnorm_grad,
        knorm_grad,
        attn_out_grad,
        norm2_grad,
        cq_grad,
        ckv_grad,
        cqnorm_grad,
        cknorm_grad,
        cross_out_grad,
        norm3_grad,
        fc1_grad,
        fc2_grad,
    )


def solution(mesh):
    placed = (
        P("dp", None),
        P("dp", None),
        P(),
        P(),
        P("dp", None),
        P("dp", None),
        P("tensor", None),
        P(),
        P(),
        P(),
        P(None, None, "tensor"),
        P(),
        P(),
        P("tensor", None),
        P(),
        P(None, "tensor"),
        P(None, None, "tensor"),
        P(),
        P(),
        P("tensor", None),
        P(),
        P(None, "tensor"),
        P("tensor", None),
    )
    return jax.shard_map(
        local,
        mesh=mesh,
        in_specs=placed,
        out_specs=(
            P("dp", None),
            P("dp", None),
            P("dp", None),
            P(),
            P("tensor", None),
            P(),
            P(),
            P(),
            P(None, None, "tensor"),
            P(),
            P(),
            P("tensor", None),
            P(),
            P(None, "tensor"),
            P(None, None, "tensor"),
            P(),
            P(),
            P("tensor", None),
            P(),
            P(None, "tensor"),
            P("tensor", None),
        ),
        check_vma=False,
    )
```

```python
import jax
import jax.numpy as jnp
from jax import lax
from jax.experimental import pallas as pl
from jax.experimental.pallas import tpu as pltpu
from jax.sharding import PartitionSpec as P

BF16 = jnp.bfloat16
F32 = jnp.float32


def layer_norm(inputs, norm_gain):
    centered = inputs - jnp.mean(inputs, -1, keepdims=True)
    variance = jnp.mean(centered * centered, -1, keepdims=True)
    return centered * lax.rsqrt(variance + 1e-06) * norm_gain


def rotary_tables(positions, head_dim):
    quarter = head_dim // 4
    frequency = 10000.0 ** (-jnp.arange(quarter).astype(F32) / quarter)
    angles = positions.astype(F32)[:, :, None] * frequency
    cosine, sine = jnp.cos(angles), jnp.sin(angles)
    cos_wide = jnp.stack([cosine, cosine], 2).reshape(positions.shape[0], head_dim)
    sin_wide = jnp.stack([-sine, sine], 2).reshape(positions.shape[0], head_dim)
    return cos_wide, sin_wide


def left_product(inputs, grads):
    return lax.dot_general(
        inputs, grads, (((0,), (0,)), ((), ())), preferred_element_type=jnp.float32
    )


def right_product(grads, weight):
    return lax.dot_general(
        grads, weight, (((1,), (1,)), ((), ())), preferred_element_type=jnp.float32
    )


def exchange(blocks, axis="tensor"):
    return lax.all_to_all(blocks, axis, 0, 0, tiled=True)


def spread(block, axis="tensor"):
    count = lax.axis_size(axis)
    return jnp.broadcast_to(block[None], (count,) + block.shape)


def after(value, *earlier):
    return lax.optimization_barrier((value,) + earlier)[0]


def after_all(values, *earlier):
    return lax.optimization_barrier((tuple(values),) + earlier)[0]


def pad_rows(rows, multiple):
    extra = -rows.shape[0] % multiple
    return jnp.pad(rows, ((0, extra),) + ((0, 0),) * (rows.ndim - 1))


def ring_route(step):
    count = lax.axis_size("tensor")
    ring = count // 2
    return [(i, i // ring * ring + (i + step) % ring) for i in range(count)]


def ring_gather(block):
    ring = lax.axis_size("tensor") // 2
    got = {k: lax.ppermute(block, "tensor", ring_route(k)) for k in (1, 3, 2)}
    return [block] + [got[k] for k in range(1, ring)]


def ring_scatter(blocks):
    got = {k: lax.ppermute(blocks[k], "tensor", ring_route(-k)) for k in (1, 3, 2)}
    return [blocks[0]] + [got[k] for k in range(1, len(blocks))]


def place_blocks(blocks, half_blocks):
    ring = len(blocks)
    place = lax.axis_index("tensor")
    ring_place, half = place % ring, place // ring
    rows = blocks[0].shape[0]
    out = jnp.zeros((2 * ring * rows,) + blocks[0].shape[1:], blocks[0].dtype)
    for k in range(ring):
        at_ring = (ring_place - k) % ring
        for which, block in ((half, blocks[k]), (1 - half, half_blocks[k])):
            out = lax.dynamic_update_slice_in_dim(out, block, (which * ring + at_ring) * rows, 0)
    return out


def half_swap(block):
    count = lax.axis_size("tensor")
    return lax.ppermute(block, "tensor", [(i, (i + count // 2) % count) for i in range(count)])


def core_swap(block):
    count = lax.axis_size("dp")
    return lax.ppermute(block, "dp", [(i, i ^ 1) for i in range(count)])


def dp_slice(rows, unit):
    places = lax.axis_size("dp")
    each = -(-rows.shape[0] // (places * unit)) * unit
    rows = pad_rows(rows, each * places)
    return lax.dynamic_slice_in_dim(rows, lax.axis_index("dp") * each, each, 0)


def dp_routes():
    count = lax.axis_size("dp")
    place = lax.axis_index("dp")
    stages = []
    for low, size in ((0, 2), (1, 4), (3, 2)):
        part = place // (1 << low) % size
        routes = []
        for step in range(1, size):
            route = []
            for source in range(count):
                here = source // (1 << low) % size
                there = (here + step) % size
                route.append((source, source + ((there - here) << low)))
            routes.append(route)
        stages.append((size, part, routes))
    return stages


def join(*values):
    return lax.optimization_barrier(values)


def low_slice(rows, unit):
    places = len(low_groups()[0])
    each = -(-rows.shape[0] // (places * unit)) * unit
    rows = pad_rows(rows, each * places)
    return lax.dynamic_slice_in_dim(rows, lax.axis_index("dp") % places * each, each, 0)


def far_swap(block):
    dp_count, count = lax.axis_size("dp"), lax.axis_size("tensor")
    route = [
        (d * count + t, (d ^ 1) * count + (t + count // 2) % count)
        for d in range(dp_count)
        for t in range(count)
    ]
    return lax.ppermute(block, ("dp", "tensor"), route)


def low_swap(block):
    count = lax.axis_size("dp")
    return lax.ppermute(block, "dp", [(i, i ^ 8) for i in range(count)])


def low_groups():
    return [list(range(8)), list(range(8, 16))]


def scatter_low(rows):
    return lax.psum_scatter(
        rows, "dp", scatter_dimension=0, tiled=True, axis_index_groups=low_groups()
    )


def gather_low(rows):
    return lax.all_gather(rows, "dp", axis=0, tiled=False, axis_index_groups=low_groups())


def scatter_stage(stage, grads):
    size, part, routes = dp_routes()[stage]
    rows = grads.shape[1] // size
    cut = lambda place: lax.dynamic_slice_in_dim(grads, place * rows, rows, 1)
    total = cut(part).astype(F32)
    for step, route in enumerate(routes, 1):
        send = cut((part + step) % size).astype(BF16)
        total = total + lax.ppermute(send, "dp", route).astype(F32)
    return total


def half_sum(own, other):
    return own.astype(F32) + half_swap(other.astype(BF16)).astype(F32)


VMEM_LIMIT = 60 * 1024 * 1024


def cost(micros):
    return pl.CostEstimate(flops=0, transcendentals=0, bytes_accessed=int(micros * 3.3e6))


def call(kernel, micros, outs, ins, name, grid=None, in_specs=None, out_specs=None, scratch=()):
    extra = {}
    if grid:
        extra = {"grid": grid, "in_specs": in_specs, "out_specs": out_specs}
    return pl.pallas_call(
        kernel,
        out_shape=outs,
        scratch_shapes=scratch,
        compiler_params=pltpu.CompilerParams(
            vmem_limit_bytes=VMEM_LIMIT,
            dimension_semantics=("arbitrary",) * len(grid) if grid else None,
        ),
        cost_estimate=cost(micros),
        name=name,
        **extra,
    )(*ins)


def dot(left, right):
    return lax.dot_general(left, right, (((1,), (0,)), ((), ())), preferred_element_type=F32)


def dot_t(left, right):
    return lax.dot_general(left, right, (((1,), (1,)), ((), ())), preferred_element_type=F32)


def t_dot(left, right):
    return lax.dot_general(left, right, (((0,), (0,)), ((), ())), preferred_element_type=F32)


def norm_parts(rows):
    centered = rows - jnp.mean(rows, -1, keepdims=True)
    scale = lax.rsqrt(jnp.mean(centered * centered, -1, keepdims=True) + 1e-06)
    return centered * scale, scale


def norm_back(unit, scale, gain, grad):
    weighted = grad * gain
    rows = scale * (
        weighted
        - jnp.mean(weighted, -1, keepdims=True)
        - unit * jnp.mean(weighted * unit, -1, keepdims=True)
    )
    return rows, jnp.sum(grad * unit, 0, keepdims=True)


def add_all(refs):
    total = refs[0][...].astype(F32)
    for ref in refs[1:]:
        total = total + ref[...].astype(F32)
    return total


def stack(parts):
    return jnp.concatenate(parts, 0)


HBM = pl.BlockSpec(memory_space=pltpu.HBM)


def load_blocks(refs, x_ref, sems):
    rows = x_ref.shape[0] // len(refs)
    copies = [
        pltpu.make_async_copy(
            ref.at[pl.ds(0, rows)], x_ref.at[pl.ds(i * rows, rows)], sems.at[i]
        )
        for i, ref in enumerate(refs)
    ]
    for copy in copies:
        copy.start()
    for copy in copies:
        copy.wait()


def put_blocks(refs, value):
    rows = refs[0].shape[0]
    for i, ref in enumerate(refs):
        ref[...] = value[i * rows : (i + 1) * rows].astype(BF16)


def struct(shape, kind):
    return jax.ShapeDtypeStruct(shape, kind)


def whole(shape):
    return pl.BlockSpec(shape, lambda *place: (0,) * len(shape))


def at(shape, row):
    return pl.BlockSpec(shape, lambda *place: (row,) + (0,) * (len(shape) - 1))


def swap(rows):
    quarter = rows.shape[1] // 4
    cut = [rows[:, i * quarter : (i + 1) * quarter] for i in range(4)]
    return jnp.concatenate([cut[1], cut[0], cut[3], cut[2]], 1)


def pack_spec(rows, width, place, share=16):
    return pl.BlockSpec((rows // share, share, width), lambda *step: (0, place // share, 0))


def pack_rows(pack_ref):
    return pack_ref[...].reshape(-1, pack_ref.shape[2])


def first_norms(got, skip_gain, norm1_gain, shift, along):
    count, rows, width = got.shape

    def kernel(got_ref, skip_ref, gain_ref, shift_ref, along_ref, merged_ref, hidden_ref, out_ref):
        merged = add_all([got_ref.at[i] for i in range(count)])
        merged_ref[...] = merged
        hidden = norm_parts(merged)[0] * skip_ref[...]
        hidden_ref[...] = hidden
        out_ref[:rows] = (norm_parts(hidden)[0] * gain_ref[...] + shift_ref[...]).astype(BF16)
        out_ref[rows:] = along_ref[...]

    outs = (
        struct((rows, width), F32),
        struct((rows, width), F32),
        struct((rows + along.shape[0], width), BF16),
    )
    ins = (got, skip_gain[None], norm1_gain[None], shift[None], along)
    return call(kernel, 2.5, outs, ins, "first_norms")


def mid_norm(pieces, hidden, gain):
    def kernel(*refs):
        hidden_ref, gain_ref, new_ref, out_ref = refs[len(pieces) :]
        new = hidden_ref[...] + add_all(refs[: len(pieces)])
        new_ref[...] = new
        out_ref[...] = (norm_parts(new)[0] * gain_ref[...]).astype(BF16)

    outs = (struct(hidden.shape, F32), struct(hidden.shape, BF16))
    return call(kernel, 1.5, outs, (*pieces, hidden, gain[None]), "mid_norm")


def mid_norm_back(pieces, residual, hidden, gain):
    def kernel(*refs):
        res_ref, hidden_ref, gain_ref, new_ref, out_ref, dgain_ref = refs[len(pieces) :]
        unit, scale = norm_parts(hidden_ref[...])
        grad, dgain = norm_back(unit, scale, gain_ref[...], add_all(refs[: len(pieces)]))
        dgain_ref[...] = dgain
        new = res_ref[...].astype(F32) + grad
        new_ref[...] = new
        out_ref[...] = new.astype(BF16)

    width = hidden.shape[1]
    outs = (struct(hidden.shape, F32), struct(hidden.shape, BF16), struct((1, width), F32))
    return call(kernel, 2, outs, (*pieces, residual, hidden, gain[None]), "mid_norm_back")


def last_norms(pieces, hidden_zero, merged, residual, gains, rows_two, rows_three, misc):
    rows, width = merged.shape
    many = len(pieces)

    def kernel(*refs):
        h0_ref, merged_ref, res_ref, g1_ref, gs_ref, two_ref, three_ref, misc_ref, out_ref = refs[many:]
        grad = add_all(refs[:many])
        shift_grad = jnp.sum(grad, 0, keepdims=True)
        unit, scale = norm_parts(h0_ref[...])
        step, norm1_grad = norm_back(unit, scale, g1_ref[...], grad)
        residual = res_ref[...] + step
        unit, scale = norm_parts(merged_ref[...])
        step, skip_grad = norm_back(unit, scale, gs_ref[...], residual)
        small = [skip_grad, norm1_grad, two_ref[...], three_ref[...], shift_grad, misc_ref[...]]
        small = stack(small + [jnp.zeros((16 - len(small), width), F32)]).astype(BF16)
        out_ref[:rows] = step.astype(BF16)
        out_ref[rows:] = small

    ins = (*pieces, hidden_zero, merged, residual, gains[0][None], gains[1][None])
    ins += (rows_two, rows_three, misc)
    return call(kernel, 3, struct((rows + 16, width), BF16), ins, "last_norms")


def project(parts, weight, other, cos_wide, sin_wide, qgain, kgain):
    width = parts[0].shape[1]
    tokens = cos_wide.shape[0]
    wide = weight.shape[0]
    each = wide // 3
    head = qgain.shape[0]
    heads = each // head
    many = len(parts)

    def kernel(*refs):
        w_ref, o_ref, cos_ref, sin_ref, qg_ref, kg_ref = refs[many : many + 6]
        x_ref, unit_ref, scale_ref, q_ref, kv_ref, sems = refs[many + 6 :]
        load_blocks(refs[:many], x_ref, sems)
        cos, sin = cos_ref[...], sin_ref[...]
        for s in range(2):
            out = dot_t(x_ref[...], w_ref[...] if s == 0 else pack_rows(o_ref))
            base = 2 * each * s
            kv_ref[:, base + each : base + 2 * each] = out[:, 2 * each :].astype(BF16)
            for h in range(heads):
                cut = lambda start: slice(start + h * head, start + (h + 1) * head)
                turn = lambda v: (v * cos + swap(v) * sin).astype(BF16)
                for part, gain_ref in ((0, qg_ref), (1, kg_ref)):
                    unit, scale = norm_parts(out[:, cut(part * each)])
                    n = (s * 2 + part) * heads + h
                    unit_ref[:, cut(base + part * each)] = unit
                    scale_ref[:, n : n + 1] = scale
                    if part == 0:
                        q_ref[:, cut(each * s)] = turn(unit * gain_ref[...])
                    else:
                        kv_ref[:, cut(base)] = turn(unit * gain_ref[...])

    outs = (
        struct((tokens, width), BF16),
        struct((tokens, 4 * each), F32),
        struct((tokens, 4 * heads), F32),
        struct((tokens, 2 * each), BF16),
        struct((tokens, 4 * each), BF16),
    )
    ins = (*parts, weight, other, cos_wide, sin_wide, qgain[None], kgain[None])
    specs = [HBM] * many + [whole(item.shape) for item in ins[many:]]
    specs[many + 1] = pack_spec(wide, width, 0, 48)
    return call(
        kernel, 6, outs, ins, "project", (1,), specs, tuple(whole(o.shape) for o in outs),
        (pltpu.SemaphoreType.DMA((many,)),),
    )


def key_rows(refs, shard, start, size, each):
    first = 2 * each * shard + start
    second = 2 * each * (1 - shard) + start
    return stack(
        [
            ref[:, first : first + size] if i < 2 else ref[:, second : second + size]
            for i, ref in enumerate(refs)
        ]
    )


def self_attention(queries, pairs, out_w, pack, head):
    tokens, both = queries.shape
    each = both // 2
    heads = each // head
    width = out_w.shape[1]
    scaling = head ** (-0.5)

    def kernel(q_ref, a_ref, b_ref, c_ref, d_ref, w_ref, o_ref, mixed_ref, total_ref, *out_refs):
        refs = (a_ref, b_ref, c_ref, d_ref)
        for s in range(2):
            for h in range(heads):
                n = s * heads + h
                cut = slice(n * head, (n + 1) * head)
                scores = dot_t(q_ref[:, cut], key_rows(refs, s, h * head, head, each)) * scaling
                most = jnp.max(scores, -1, keepdims=True)
                total = most + jnp.log(jnp.sum(jnp.exp(scores - most), -1, keepdims=True))
                total_ref[:, n : n + 1] = total
                shares = jnp.exp(scores - total).astype(BF16)
                mixture = dot(shares, key_rows(refs, s, each + h * head, head, each))
                mixed_ref[:, cut] = mixture.astype(BF16)
        out = dot(mixed_ref[:, :each], w_ref[...])
        out = out + dot(mixed_ref[:, each:], pack_rows(o_ref))
        put_blocks(out_refs, out)

    outs = (
        struct((tokens, both), BF16),
        struct((tokens, 2 * heads), F32),
    ) + (struct((tokens // 4, width), BF16),) * 4
    ins = (queries, *pairs, out_w, pack)
    specs = [whole(item.shape) for item in ins]
    specs[-1] = pack_spec(each, width, 48)
    return call(
        kernel, 5, outs, ins, "self_attention", (1,), specs, tuple(whole(o.shape) for o in outs)
    )


def self_attention_back(queries, pairs, totals, parts, out_w, pack, head):
    tokens, both = queries.shape
    each = both // 2
    heads = each // head
    rows, width = parts[0].shape
    scaling = head ** (-0.5)
    many = len(parts)

    def kernel(*refs):
        q_ref, a_ref, b_ref, c_ref, d_ref, total_ref, w_ref, o_ref = refs[many : many + 8]
        x_ref, dq_ref, own_ref, half_ref, core_ref, far_ref, dm_ref, sems = refs[many + 8 :]
        pair_refs = (a_ref, b_ref, c_ref, d_ref)
        load_blocks(refs[:many], x_ref, sems)
        dm_ref[:, :each] = dot_t(x_ref[...], w_ref[...]).astype(BF16)
        dm_ref[:, each:] = dot_t(x_ref[...], pack_rows(o_ref)).astype(BF16)

        def put(grads, shard, start):
            first = 2 * each * shard + start
            second = 2 * each * (1 - shard) + start
            cut = lambda i: grads[i * tokens : (i + 1) * tokens]
            own_ref[:, first : first + head] = cut(0)
            core_ref[:, first : first + head] = cut(1).astype(BF16)
            half_ref[:, second : second + head] = cut(2).astype(BF16)
            far_ref[:, second : second + head] = cut(3).astype(BF16)

        for s in range(2):
            for h in range(heads):
                n = s * heads + h
                cut = slice(n * head, (n + 1) * head)
                mine, grads = q_ref[:, cut], dm_ref[:, cut]
                keys_h = key_rows(pair_refs, s, h * head, head, each)
                values_h = key_rows(pair_refs, s, each + h * head, head, each)
                shares = jnp.exp(dot_t(mine, keys_h) * scaling - total_ref[:, n : n + 1])
                dshares = dot_t(grads, values_h)
                put(t_dot(shares.astype(BF16), grads), s, each + h * head)
                weighted = jnp.sum(shares * dshares, -1, keepdims=True)
                dscores = (shares * (dshares - weighted) * scaling).astype(BF16)
                dq_ref[:, cut] = dot(dscores, keys_h)
                put(t_dot(dscores, mine), s, h * head)

    outs = (
        struct((tokens, width), BF16),
        struct((tokens, both), F32),
        struct((tokens, 4 * each), F32),
        struct((tokens, 4 * each), BF16),
        struct((tokens, 4 * each), BF16),
        struct((tokens, 4 * each), BF16),
    )
    ins = (*parts, queries, *pairs, totals, out_w, pack)
    specs = [HBM] * many + [whole(item.shape) for item in ins[many:]]
    specs[-1] = pack_spec(each, width, 48)
    return call(
        kernel, 9, outs, ins, "self_attention_back", (1,), specs,
        tuple(whole(o.shape) for o in outs),
        (pltpu.VMEM((tokens, both), BF16), pltpu.SemaphoreType.DMA((many,))),
    )


def project_back(units, scales, cos_wide, sin_wide, qgain, kgain, dq, own, core, half, far, weight, other):
    tokens = units.shape[0]
    wide, width = weight.shape
    each = wide // 3
    head = qgain.shape[0]
    heads = each // head

    def kernel(unit_ref, scale_ref, cos_ref, sin_ref, qg_ref, kg_ref, dq_ref, own_ref, core_ref, half_ref, far_ref, w_ref, o_ref,
               mine_ref, other_ref, dqg_ref, dkg_ref, *out_refs):
        cos, sin = cos_ref[...], sin_ref[...]
        dkv = own_ref[...] + core_ref[...].astype(F32)
        dkv = dkv + half_ref[...].astype(F32) + far_ref[...].astype(F32)
        dgains = [jnp.zeros((1, head), F32), jnp.zeros((1, head), F32)]
        for s, to_ref in ((0, mine_ref), (1, other_ref)):
            base = 2 * each * s
            to_ref[:, 2 * each : 3 * each] = dkv[:, base + each : base + 2 * each].astype(BF16)
            for h in range(heads):
                cut = lambda start: slice(start + h * head, start + (h + 1) * head)
                for part, gain_ref in ((0, qg_ref), (1, kg_ref)):
                    turned = dq_ref[:, cut(each * s)] if part == 0 else dkv[:, cut(base)]
                    grad = turned * cos - swap(turned) * sin
                    n = (s * 2 + part) * heads + h
                    unit = unit_ref[:, cut(base + part * each)]
                    grad, dgain = norm_back(unit, scale_ref[:, n : n + 1], gain_ref[...], grad)
                    dgains[part] = dgains[part] + dgain
                    to_ref[:, cut(part * each)] = grad.astype(BF16)
        dqg_ref[...], dkg_ref[...] = dgains
        out = dot(mine_ref[...], w_ref[...])
        put_blocks(out_refs, out + dot(other_ref[...], pack_rows(o_ref)))

    outs = (
        struct((tokens, wide), BF16),
        struct((tokens, wide), BF16),
        struct((1, head), F32),
        struct((1, head), F32),
    ) + (struct((tokens // 4, width), BF16),) * 4
    ins = (units, scales, cos_wide, sin_wide, qgain[None], kgain[None], dq, own, core, half, far, weight, other)
    specs = [whole(item.shape) for item in ins]
    specs[-1] = pack_spec(wide, width, 0, 48)
    return call(
        kernel, 8, outs, ins, "project_back", (1,), specs, tuple(whole(o.shape) for o in outs)
    )


def text_shares(scores, scaling, count):
    place = lax.broadcasted_iota(jnp.int32, scores.shape, 1)
    scores = jnp.where(place < count, scores * scaling, -1e30)
    most = jnp.max(scores, -1, keepdims=True)
    total = most + jnp.log(jnp.sum(jnp.exp(scores - most), -1, keepdims=True))
    return jnp.exp(scores - total)


def cross_layer(parts, cq_w, out_w, pack, text, other_text, gain, text_count):
    rows, width = parts[0].shape
    tokens = rows * len(parts)
    each = cq_w.shape[0]
    head = gain.shape[0]
    heads = each // head
    scaling = head ** (-0.5)
    many = len(parts)

    def kernel(*refs):
        cq_ref, w_ref, ocq_ref, ow_ref, text_ref, otext_ref, gain_ref = refs[many : many + 7]
        x_ref, raw_ref, mixed_ref, *out_refs, sems = refs[many + 7 :]
        load_blocks(refs[:many], x_ref, sems)
        raw_ref[:, :each] = dot_t(x_ref[...], cq_ref[...])
        raw_ref[:, each:] = dot_t(x_ref[...], pack_rows(ocq_ref))
        for s, keys_ref in ((0, text_ref), (1, otext_ref)):
            for h in range(heads):
                n = s * heads + h
                cut = slice(n * head, (n + 1) * head)
                mine = (norm_parts(raw_ref[:, cut])[0] * gain_ref[...]).astype(BF16)
                scores = dot_t(mine, keys_ref[:, h * head : (h + 1) * head])
                shares = text_shares(scores, scaling, text_count).astype(BF16)
                values = keys_ref[:, each + h * head : each + (h + 1) * head]
                mixed_ref[:, cut] = dot(shares, values).astype(BF16)
        out = dot(mixed_ref[:, :each], w_ref[...])
        out = out + dot(mixed_ref[:, each:], pack_rows(ow_ref))
        put_blocks(out_refs, out)

    outs = (
        struct((tokens, width), BF16),
        struct((tokens, 2 * each), F32),
        struct((tokens, 2 * each), BF16),
    ) + (struct((rows, width), BF16),) * many
    ins = (*parts, cq_w, out_w, pack, pack, text, other_text, gain[None])
    specs = [HBM] * many + [whole(item.shape) for item in ins[many:]]
    specs[many + 2] = pack_spec(each, width, 0)
    specs[many + 3] = pack_spec(each, width, 16)
    return call(
        kernel, 7, outs, ins, "cross_layer", (1,), specs, tuple(whole(o.shape) for o in outs),
        (pltpu.SemaphoreType.DMA((many,)),),
    )


def cross_layer_back(parts, raw, cq_w, out_w, pack, text, other_text, gain, text_count):
    rows, width = parts[0].shape
    tokens = rows * len(parts)
    each = cq_w.shape[0]
    head = gain.shape[0]
    heads = each // head
    scaling = head ** (-0.5)
    many = len(parts)

    def kernel(*refs):
        raw_ref, cq_ref, w_ref, ocq_ref, ow_ref, text_ref, otext_ref, gain_ref = refs[many : many + 8]
        x_ref, draw_ref, dtext_ref, dother_ref, dgain_ref, *out_refs, dm_ref, sems = refs[many + 8 :]
        load_blocks(refs[:many], x_ref, sems)
        dm_ref[:, :each] = dot_t(x_ref[...], w_ref[...]).astype(BF16)
        dm_ref[:, each:] = dot_t(x_ref[...], pack_rows(ow_ref)).astype(BF16)
        dgain = jnp.zeros((1, head), F32)
        for s, keys_ref, to_ref in ((0, text_ref, dtext_ref), (1, otext_ref, dother_ref)):
            for h in range(heads):
                n = s * heads + h
                cut = slice(n * head, (n + 1) * head)
                kcut = slice(h * head, (h + 1) * head)
                vcut = slice(each + h * head, each + (h + 1) * head)
                unit, scale = norm_parts(raw_ref[:, cut])
                mine = (unit * gain_ref[...]).astype(BF16)
                shares = text_shares(dot_t(mine, keys_ref[:, kcut]), scaling, text_count)
                dshares = dot_t(dm_ref[:, cut], keys_ref[:, vcut])
                to_ref[:, vcut] = t_dot(shares.astype(BF16), dm_ref[:, cut]).astype(BF16)
                weighted = jnp.sum(shares * dshares, -1, keepdims=True)
                dscores = (shares * (dshares - weighted) * scaling).astype(BF16)
                to_ref[:, kcut] = t_dot(dscores, mine).astype(BF16)
                grad, step = norm_back(unit, scale, gain_ref[...], dot(dscores, keys_ref[:, kcut]))
                dgain = dgain + step
                draw_ref[:, cut] = grad.astype(BF16)
        dgain_ref[...] = dgain
        out = dot(draw_ref[:, :each], cq_ref[...])
        out = out + dot(draw_ref[:, each:], pack_rows(ocq_ref))
        put_blocks(out_refs, out)

    outs = (
        struct((tokens, width), BF16),
        struct((tokens, 2 * each), BF16),
        struct(text.shape, BF16),
        struct(text.shape, BF16),
        struct((1, head), F32),
    ) + (struct((rows, width), BF16),) * many
    ins = (*parts, raw, cq_w, out_w, pack, pack, text, other_text, gain[None])
    specs = [HBM] * many + [whole(item.shape) for item in ins[many:]]
    specs[many + 3] = pack_spec(each, width, 0)
    specs[many + 4] = pack_spec(each, width, 16)
    return call(
        kernel, 10, outs, ins, "cross_layer_back", (1,), specs,
        tuple(whole(o.shape) for o in outs),
        (pltpu.VMEM((tokens, 2 * each), BF16), pltpu.SemaphoreType.DMA((many,))),
    )


def feed_forward(parts, cot, fc1_w, fc2_w, pack):
    rows, width = parts[0].shape
    tokens = rows * len(parts)
    hidden = fc2_w.shape[0]
    block = hidden // 2
    places = pack.shape[0]
    each = hidden // places
    both = 2 * each
    root = (2 / 3.141592653589793) ** 0.5
    many = len(parts)

    def kernel(*refs):
        cot_ref, w1_ref, w2_ref, pack_ref, x_ref, acts_ref, *out_refs, acc_ref, sum_ref, sems = refs[many:]
        step = pl.program_id(0)

        @pl.when(step == 0)
        def _():
            load_blocks(refs[:many], x_ref, sems)
            acc_ref[...] = jnp.zeros_like(acc_ref)
            sum_ref[...] = jnp.zeros_like(sum_ref)

        def work(pre, w2, back):
            square = pre * pre
            bent = jnp.tanh(root * pre * (1 + 0.044715 * square))
            part = 0.5 * (1 + bent)
            slope = part + 0.5 * pre * (1 - bent * bent) * root * (1 + 3 * 0.044715 * square)
            grad = (dot_t(cot_ref[...], w2) * slope).astype(BF16)
            acts_ref[0, 0] = grad
            active = (pre * part).astype(BF16)
            acts_ref[0, 1] = active
            acc_ref[...] += back(grad)
            sum_ref[...] += dot(active, w2)

        @pl.when(step < 2)
        def _():
            weight = w1_ref[...]
            work(dot(x_ref[...], weight), w2_ref[...], lambda grad: dot_t(grad, weight))

        @pl.when(step >= 2)
        def _():
            weight = pack_ref[:, :each].reshape(block, width)
            second = pack_ref[:, each:].reshape(block, width)
            work(dot_t(x_ref[...], weight), second, lambda grad: dot(grad, weight))

        @pl.when(step == 3)
        def _():
            put_blocks(out_refs[:many], acc_ref[...])
            put_blocks(out_refs[many:], sum_ref[...])

    low = lambda i: jnp.minimum(i, 1)
    high = lambda i: jnp.maximum(i - 2, 0)
    outs = (
        struct((tokens, width), BF16),
        struct((2, 2, tokens, hidden), BF16),
    ) + (struct((rows, width), BF16),) * (2 * many)
    out_specs = (
        whole((tokens, width)),
        pl.BlockSpec((1, 2, tokens, block), lambda i: (i // 2, 0, 0, i % 2)),
    ) + (whole((rows, width)),) * (2 * many)
    in_specs = [HBM] * many + [
        whole(cot.shape),
        pl.BlockSpec((width, block), lambda i: (0, low(i))),
        pl.BlockSpec((block, width), lambda i: (low(i), 0)),
        pl.BlockSpec((places // 2, both, width), lambda i: (high(i), 0, 0)),
    ]
    return call(
        kernel, 9, outs, (*parts, cot, fc1_w, fc2_w, pack), "feed_forward", (4,), in_specs, out_specs,
        (
            pltpu.VMEM((tokens, width), F32),
            pltpu.VMEM((tokens, width), F32),
            pltpu.SemaphoreType.DMA((many,)),
        ),
    )


def feed_forward_grads(acts, rows_in, cot, places):
    _, _, tokens, hidden = acts.shape
    width = cot.shape[1]
    share = 2 * hidden // places

    def kernel(acts_ref, x_ref, cot_ref, out_ref):
        which = pl.program_id(1)

        def put(right_ref):
            grads = t_dot(acts_ref[0, 0], right_ref[...]).astype(BF16)
            out_ref[...] = grads.reshape(out_ref.shape)

        pl.when(which == 0)(lambda: put(x_ref))
        pl.when(which == 1)(lambda: put(cot_ref))

    return call(
        kernel,
        7,
        struct((places, 2, share, width), BF16),
        (acts, rows_in, cot),
        "feed_forward_grads",
        (2, 2),
        [
            pl.BlockSpec((1, 1, tokens, hidden), lambda s, w: (s, w, 0, 0)),
            whole(rows_in.shape),
            whole(cot.shape),
        ],
        pl.BlockSpec((places // 2, 1, share, width), lambda s, w: (w, s, 0, 0)),
    )


def put_shares(out_ref, shard, to, share, rows_ref):
    stop, width = rows_ref.shape
    for place in range(out_ref.shape[0]):
        begin = min(place * share, stop)
        count = min(share, stop - begin)
        if count:
            out_ref[place, shard, to : to + count] = rows_ref[begin : begin + count]
        if count < share:
            out_ref[place, shard, to + count : to + share] = jnp.zeros((share - count, width), BF16)


def cross_grads(draw, mixed, rows_in, grad_rows, places, share):
    each = draw.shape[1] // 2
    width = rows_in.shape[1]

    def kernel(draw_ref, mixed_ref, x_ref, d_ref, out_ref, hold_ref):
        for s in range(2):
            cut = slice(s * each, (s + 1) * each)
            hold_ref[:each] = t_dot(draw_ref[:, cut], x_ref[...]).astype(BF16)
            hold_ref[each:] = t_dot(mixed_ref[:, cut], d_ref[...]).astype(BF16)
            put_shares(out_ref, s, 0, share, hold_ref)

    ins = (draw, mixed, rows_in, grad_rows)
    scratch = (pltpu.VMEM((2 * each, width), BF16),)
    return call(kernel, 4, struct((places, 2, share, width), BF16), ins, "cross_grads", scratch=scratch)


def self_grads(mine, other, mixed, rows_in, grad_rows, places, share):
    wide = mine.shape[1]
    each = wide // 3
    width = rows_in.shape[1]

    def kernel(mine_ref, other_ref, mixed_ref, x_ref, d_ref, out_ref, hold_ref):
        for s, grad_ref in ((0, mine_ref), (1, other_ref)):
            cut = slice(s * each, (s + 1) * each)
            hold_ref[:wide] = t_dot(grad_ref[...], x_ref[...]).astype(BF16)
            hold_ref[wide:] = t_dot(mixed_ref[:, cut], d_ref[...]).astype(BF16)
            put_shares(out_ref, s, 0, share, hold_ref)

    ins = (mine, other, mixed, rows_in, grad_rows)
    scratch = (pltpu.VMEM((wide + each, width), BF16),)
    return call(kernel, 5, struct((places, 2, share, width), BF16), ins, "self_grads", scratch=scratch)


def skip_grads(parts, joined_own, joined_other, long):
    rows, width = parts[0].shape
    small = 16
    rows -= small
    tokens, slab = joined_own.shape
    many = len(parts)

    def kernel(*refs):
        own_ref, other_ref, x_ref, out_ref, all_ref, sems = refs[many:]
        load_blocks(refs[:many], all_ref, sems)
        total = jnp.zeros((small, width), F32)
        for i in range(many):
            start = i * (rows + small)
            x_ref[i * rows : (i + 1) * rows] = all_ref[start : start + rows]
            total = total + all_ref[start + rows : start + rows + small].astype(F32)
        for s, left_ref in ((0, own_ref), (1, other_ref)):
            out_ref[s, :slab] = t_dot(left_ref[...], x_ref[...])
            out_ref[s, slab : slab + small] = total
            out_ref[s, slab + small :] = jnp.zeros((long - slab - small, width), F32)

    outs = (struct((tokens, width), BF16), struct((2, long, width), F32))
    ins = (*parts, joined_own, joined_other)
    return call(
        kernel, 4, outs, ins, "skip_grads", (1,),
        [HBM] * many + [whole(joined_own.shape), whole(joined_other.shape)],
        tuple(whole(o.shape) for o in outs),
        (pltpu.VMEM((many * (rows + small), width), BF16), pltpu.SemaphoreType.DMA((many,))),
    )


def joined_grads(rows_in, pack, slab):
    tokens, width = rows_in.shape
    held, count, deep, _ = pack.shape
    half = count // 2

    def kernel(x_ref, pack_ref, one_ref, two_ref):
        for step, out_ref in ((0, one_ref), (1, two_ref)):

            @pl.when(pl.program_id(0) == step)
            def _(out_ref=out_ref):
                for j in range(half):
                    weight = pack_ref[:, j].reshape(held * deep, width)[:slab]
                    out_ref[:, j * slab : (j + 1) * slab] = dot_t(x_ref[...], weight)

    outs = (struct((tokens, width), F32), struct((tokens, width), F32))
    return call(
        kernel, 9, outs, (rows_in, pack), "joined_grads", (2,),
        [
            whole(rows_in.shape),
            pl.BlockSpec((held, half, deep, width), lambda i: (0, i, 0, 0)),
        ],
        (whole((tokens, width)), whole((tokens, width))),
    )


def feed_forward_out(sums, share):
    places, _, width = sums.shape
    half = places // 2
    hidden = half * share

    def kernel(sum_ref, one_ref, two_ref):
        @pl.when(pl.program_id(0) == 0)
        def _():
            one_ref[...] = sum_ref[...].reshape(hidden, width).astype(F32).T

        @pl.when(pl.program_id(0) == 1)
        def _():
            two_ref[...] = sum_ref[...].reshape(hidden, width).astype(F32)

    outs = (struct((width, hidden), F32), struct((hidden, width), F32))
    return call(
        kernel, 6, outs, (sums,), "feed_forward_out", (2,),
        [pl.BlockSpec((half, share, width), lambda i: (i, 0, 0))],
        (whole((width, hidden)), whole((hidden, width))),
    )


def text_layer(tokens, ckv, gain, rows):
    count, width = tokens.shape
    packed = ckv.ndim == 3
    both = ckv.shape[2] // 4 if packed else ckv.shape[1]
    each = both // 2
    head = gain.shape[0]
    heads = each // head

    def kernel(x_ref, w_ref, gain_ref, pair_ref, unit_ref, scale_ref, *more):
        if packed:
            weight_ref = more[0]
            deep = w_ref.shape[1]
            for place in range(w_ref.shape[0]):
                for k in range(4):
                    start = (place * 4 + k) * deep
                    weight_ref[start : start + deep] = w_ref[place, :, k * both : (k + 1) * both]
        else:
            weight_ref = w_ref
        out = dot(x_ref[...], weight_ref[...])
        pair_ref[...] = jnp.zeros_like(pair_ref)
        pair_ref[:count, each:] = out[:, each:].astype(BF16)
        for h in range(heads):
            cut = slice(h * head, (h + 1) * head)
            unit, scale = norm_parts(out[:, cut])
            unit_ref[:, cut] = unit
            scale_ref[:, h : h + 1] = scale
            pair_ref[:count, cut] = (unit * gain_ref[...]).astype(BF16)

    outs = (
        struct((rows, both), BF16),
        struct((count, each), F32),
        struct((count, heads), F32),
    )
    specs = [whole(tokens.shape), whole(ckv.shape), whole((1, head))]
    if packed:
        outs += (struct((width, both), BF16),)
        deep = width // ckv.shape[0] // 4
        place = ckv.shape[1] // deep - 1
        specs[1] = pl.BlockSpec((ckv.shape[0], deep, ckv.shape[2]), lambda *step: (0, place, 0))
    return call(
        kernel, 4, outs, (tokens, ckv, gain[None]), "text_layer", (1,), specs,
        tuple(whole(o.shape) for o in outs),
    )


def text_layer_back(crosses, pairs, units, scales, tokens, ckvs, gain):
    count, width = tokens.shape
    both = ckvs[0].shape[1]
    each = both // 2
    head = gain.shape[0]
    heads = each // head
    places, _, first, wide = crosses.shape
    deep = 48
    more = 48
    long = more * places

    def kernel(first_ref, a_ref, b_ref, ua_ref, ub_ref, sa_ref, sb_ref, x_ref, wa_ref, wb_ref, gain_ref, out_ref, dw_ref, grad_ref, part_ref):
        dgain = jnp.zeros((1, head), F32)
        part = jnp.zeros((count, width), F32)
        for s, (pair_ref, unit_ref, scale_ref, w_ref) in enumerate(
            ((a_ref, ua_ref, sa_ref, wa_ref), (b_ref, ub_ref, sb_ref, wb_ref))
        ):
            grad_ref[:, each:] = pair_ref[:count, each:]
            for h in range(heads):
                cut = slice(h * head, (h + 1) * head)
                grad, step = norm_back(
                    unit_ref[:, cut], scale_ref[:, h : h + 1], gain_ref[...], pair_ref[:count, cut].astype(F32)
                )
                dgain = dgain + step
                grad_ref[:, cut] = grad.astype(BF16)
            dw_ref[...] = t_dot(grad_ref[...], x_ref[...]).astype(BF16)
            part = part + dot_t(grad_ref[...], w_ref[...])
            for place in range(places):
                begin = min(place * deep, both)
                held = min(deep, both - begin)
                out_ref[place, s, :first] = first_ref[place, s]
                out_ref[place, s, first : first + deep] = jnp.zeros((deep, wide), BF16)
                out_ref[place, s, first : first + held, :width] = dw_ref[begin : begin + held]
        part_ref[...] = jnp.zeros_like(part_ref)
        part_ref[:count, :width] = part
        part_ref[long - 1 :, :head] = dgain
        for place in range(places):
            rows = part_ref[place * more : (place + 1) * more].astype(BF16)
            for s in range(2):
                out_ref[place, s, first + deep :] = rows

    ins = (crosses, *pairs, *units, *scales, tokens, *ckvs, gain[None])
    scratch = (
        pltpu.VMEM((both, width), BF16),
        pltpu.VMEM((count, both), BF16),
        pltpu.VMEM((long, wide), F32),
    )
    return call(
        kernel, 9, struct((places, 2, first + deep + more, wide), BF16), ins, "text_layer_back", scratch=scratch
    )


def local(
    latent,
    skip_input,
    text_tokens,
    condition,
    positions,
    cotangent,
    skip_w,
    skip_gain,
    norm1_gain,
    mod_w,
    qkv_w,
    qnorm_gain,
    knorm_gain,
    attn_out_w,
    norm2_gain,
    cq_w,
    ckv_w,
    cqnorm_gain,
    cknorm_gain,
    cross_out_w,
    norm3_gain,
    fc1_w,
    fc2_w,
):
    token_count, model_width = latent.shape
    head_dim = qnorm_gain.shape[0]
    local_width = cq_w.shape[1]
    local_heads = local_width // head_dim
    slab_width = skip_w.shape[0]
    hidden_width = fc1_w.shape[1]
    text_count, text_width = text_tokens.shape
    tensor_place = lax.axis_index("tensor")
    tensor_count = lax.axis_size("tensor")
    dp_count = lax.axis_size("dp")
    low_count = len(low_groups()[0])
    part_count = token_count // tensor_count
    ring = tensor_count // 2
    ring_place, half = tensor_place % ring, tensor_place // ring
    qkv_rows = 3 * local_width

    def own_rows(rows):
        return lax.dynamic_slice_in_dim(rows, tensor_place * part_count, part_count, 0)

    def ring_rows(rows, which):
        first = which * ring
        return jnp.concatenate(
            [
                lax.dynamic_slice_in_dim(
                    rows, (first + (ring_place - k) % ring) * part_count, part_count, 0
                )
                for k in range(ring)
            ],
            0,
        )

    joined = jnp.concatenate([latent, skip_input], 1)
    joined_part = lax.dynamic_slice_in_dim(joined, tensor_place * slab_width, slab_width, 1)
    partial = jnp.dot(joined_part, skip_w, preferred_element_type=F32).astype(BF16)
    got = exchange(partial.reshape(tensor_count, part_count, model_width))

    dp_place = lax.axis_index("dp")
    qkv_flat = qkv_w.transpose(1, 2, 0).reshape(qkv_rows, model_width)
    cq_turned = cq_w.T
    shares = [dp_slice(qkv_flat, 48), dp_slice(attn_out_w, 16)]
    pack = lax.all_gather(half_swap(jnp.concatenate(shares, 0)), "dp", axis=0, tiled=False)
    ckv_flat = ckv_w.reshape(text_width, 2 * local_width)
    text_rows_in = pad_rows(text_tokens, model_width // 4)
    text_pair, text_units, text_scales = text_layer(
        text_rows_in, ckv_flat, cknorm_gain, model_width // 4
    )
    share = hidden_width // dp_count
    deep = text_width // dp_count // 4
    share = hidden_width // low_count
    low_place = dp_place % low_count
    ff_share = [
        lax.dynamic_slice_in_dim(fc1_w, low_place * share, share, 1).T,
        lax.dynamic_slice_in_dim(fc2_w, low_place * share, share, 0),
    ]
    ff_share = jnp.concatenate(ff_share, 0)
    ckv_share = lax.dynamic_slice_in_dim(ckv_flat, dp_place * 4 * deep, 4 * deep, 0)
    cross_share = [dp_slice(rows, 16) for rows in (cq_turned, cross_out_w)]
    cross_share.append(jnp.concatenate(jnp.split(ckv_share, 4), 1))
    cross_share = jnp.concatenate(cross_share, 0)
    silu_cond = jax.nn.silu(condition.astype(F32)).astype(BF16)
    shift = jnp.dot(silu_cond[None], mod_w, preferred_element_type=F32)[0]
    cos_wide, sin_wide = rotary_tables(ring_rows(positions, half), head_dim)
    cot_rows = ring_rows(cotangent, half)
    got, cos_wide, sin_wide, shift, text_pair, cot_rows, ff_share, cross_share = join(
        got, cos_wide, sin_wide, shift, text_pair, cot_rows, ff_share, cross_share
    )
    skip_share = low_slice(skip_w, 16)
    merged, hidden_zero, normed = first_norms(got, skip_gain, norm1_gain, shift, skip_share)
    normed_parts = ring_gather(normed)
    cross_share = half_swap(after(cross_share, normed))
    rows_one, units, scales, queries, own_pair = project(
        normed_parts, qkv_flat, pack, cos_wide, sin_wide, qnorm_gain, knorm_gain
    )
    own_pair, cross_share = join(own_pair, cross_share)
    cross_pack = lax.all_gather(cross_share, "dp", axis=0, tiled=False)
    core_pair = core_swap(own_pair)
    half_pair = half_swap(own_pair)
    pairs = (own_pair, core_pair, half_pair, core_swap(half_pair))
    mixed_one, totals, *partial = self_attention(
        queries, pairs, attn_out_w, pack, head_dim
    )
    ff_share = half_swap(after(ff_share, half_pair))
    hidden_one, normed = mid_norm(ring_scatter(partial), hidden_zero, norm2_gain)
    ff_pack = gather_low(after(ff_share, normed))
    skip_rows = jnp.concatenate([part[part_count:] for part in normed_parts], 0)
    skip_half = half_swap(after(skip_rows, normed))
    other_text, other_units, other_scales, other_ckv = text_layer(
        text_rows_in, after(cross_pack, normed), cknorm_gain, model_width // 4
    )
    *normed_parts, other_text = join(*ring_gather(normed), other_text)
    rows_two, cross_raw, mixed_two, *partial = cross_layer(
        normed_parts,
        cq_turned,
        cross_out_w,
        cross_pack,
        text_pair,
        other_text,
        cqnorm_gain,
        text_count,
    )
    *partial, skip_half = join(*partial, skip_half)
    skip_rows = place_blocks(jnp.split(skip_rows, ring), jnp.split(skip_half, ring))
    *pieces, skip_rows = join(*ring_scatter(partial), skip_rows)
    hidden_two, normed = mid_norm(pieces, hidden_one, norm3_gain)
    skip_pack = gather_low(
        skip_rows.reshape(tensor_count, -1, model_width)
    )
    rows_three, acts, *partial = feed_forward(
        ring_gather(normed), cot_rows, fc1_w, fc2_w, ff_pack
    )
    partial, last_partial = partial[:ring], partial[ring:]

    fc_grads = feed_forward_grads(acts, rows_three, cot_rows, low_count)
    *pieces, fc_grads = join(*ring_scatter(partial), fc_grads.reshape(-1, model_width))
    fc_grads = scatter_low(after(fc_grads, skip_pack))
    residual, out_grad, norm3_grad = mid_norm_back(
        pieces, own_rows(cotangent), hidden_two, norm3_gain
    )
    out_parts = ring_gather(out_grad)
    grad_rows_two, cross_raw_grad, text_own, text_other, cqnorm_grad, *partial = cross_layer_back(
        out_parts,
        cross_raw,
        cq_turned,
        cross_out_w,
        cross_pack,
        text_pair,
        other_text,
        cqnorm_gain,
        text_count,
    )
    crosses = cross_grads(
        cross_raw_grad, mixed_two, rows_two, grad_rows_two, low_count, 48
    )
    *pieces, crosses = join(*ring_scatter(partial), crosses)
    residual, out_grad, norm2_grad = mid_norm_back(pieces, residual, hidden_one, norm2_gain)
    early_sums = text_layer_back(
        crosses,
        (text_own, text_other),
        (text_units, other_units),
        (text_scales, other_scales),
        after(text_rows_in, out_grad),
        (ckv_flat, other_ckv),
        cknorm_gain,
    )
    *out_parts, early_sums, fc_grads = join(*ring_gather(out_grad), early_sums, fc_grads)
    early_sums = scatter_low(early_sums.reshape(-1, model_width))
    grad_rows_one, query_grad, pair_grad, half_grad, core_grad, far_grad = self_attention_back(
        queries,
        pairs,
        totals,
        out_parts,
        attn_out_w,
        pack,
        head_dim,
    )
    core_grad = core_swap(core_grad)
    half_grad = half_swap(half_grad)
    far_grad = far_swap(far_grad)
    core_grad, half_grad, far_grad = join(core_grad, half_grad, far_grad)
    fc_grads = after(fc_grads, half_grad)
    share = fc_grads.shape[0] // 2
    fc_grads = half_sum(fc_grads[:share], fc_grads[share:])
    projected_grad, projected_other, qnorm_grad, knorm_grad, *partial = project_back(
        units,
        scales,
        cos_wide,
        sin_wide,
        qnorm_gain,
        knorm_gain,
        query_grad,
        pair_grad,
        core_grad,
        half_grad,
        far_grad,
        qkv_flat,
        pack,
    )
    *partial, fc_grads = join(*partial, fc_grads)
    fc_grads = fc_grads + low_swap(fc_grads.astype(BF16)).astype(F32)
    late_sums = self_grads(
        projected_grad, projected_other, mixed_one, rows_one, grad_rows_one, low_count, 96
    )
    early_sums = after(early_sums, qnorm_grad)
    early_share = early_sums.shape[0] // 2
    early_sums = half_sum(early_sums[:early_share], early_sums[early_share:])
    *pieces, late_sums, fc_grads, early_sums = join(
        *ring_scatter(partial), late_sums, fc_grads, early_sums
    )
    late_sums = scatter_low(late_sums.reshape(-1, model_width))
    misc = jnp.concatenate([qnorm_grad, knorm_grad, cqnorm_grad], 1)
    misc = jnp.pad(misc, ((0, 0), (0, model_width - misc.shape[1])))
    merged_out = last_norms(
        pieces,
        hidden_zero,
        merged,
        residual,
        (norm1_gain, skip_gain),
        norm2_grad,
        norm3_grad,
        misc,
    )
    joined_rows = ring_rows(joined, half)
    joined_own = lax.dynamic_slice_in_dim(joined_rows, tensor_place * slab_width, slab_width, 1)
    joined_other = lax.dynamic_slice_in_dim(
        joined_rows, (tensor_place + ring) % tensor_count * slab_width, slab_width, 1
    )
    merged_out, early_sums = join(merged_out, early_sums)
    early_sums = early_sums + low_swap(early_sums.astype(BF16)).astype(F32)
    *merged_parts, joined_own, joined_other, early_sums = join(
        *ring_gather(merged_out), joined_own, joined_other, early_sums
    )

    text_rows = early_sums[-48:]
    for part in ring_gather(text_rows.astype(BF16))[1:]:
        text_rows = text_rows + part.astype(F32)

    last_rows = -(-(slab_width + 16) // (8 * dp_count)) * 8 * dp_count
    merged_rows, last_sums = skip_grads(merged_parts, joined_own, joined_other, last_rows)
    merged_rows, last_sums, text_rows = join(merged_rows, last_sums, text_rows)
    early_sums = jnp.concatenate([fc_grads, early_sums[:-48], text_rows], 0).astype(BF16)
    early_sums = gather_low(after(early_sums, late_sums))
    merged_half = half_swap(merged_rows)
    last_sums = scatter_stage(0, last_sums)
    output = hidden_two
    for piece in ring_scatter(after_all(last_partial, last_sums)):
        output = output + piece.astype(F32)
    last_sums = scatter_stage(1, last_sums)
    last_sums, output, merged_half = join(last_sums, output, merged_half)
    share = late_sums.shape[0] // 2
    own_sums = jnp.concatenate([late_sums[:share].astype(F32), last_sums[0]], 0)
    other_sums = jnp.concatenate([late_sums[share:], last_sums[1].astype(BF16)], 0)
    last_sums = half_sum(own_sums, other_sums)
    output = jnp.concatenate(ring_gather(output.astype(BF16)), 0)
    last_sums, output = join(last_sums, output)
    last_sums = last_sums + low_swap(last_sums.astype(BF16)).astype(F32)
    merged_grad = place_blocks(jnp.split(merged_rows, ring), jnp.split(merged_half, ring))
    latent_grad, skip_grad = joined_grads(merged_grad, skip_pack, slab_width)
    last_sums = gather_low(after(last_sums, early_sums).astype(BF16))
    output_half = half_swap(after(output, early_sums))
    fc_share = fc_grads.shape[0]
    fc1_grad, fc2_grad = feed_forward_out(early_sums, fc_share)
    output = place_blocks(jnp.split(output, ring), jnp.split(output_half, ring))
    cross_sums = early_sums[:, fc_share : fc_share + 48].reshape(-1, model_width)
    cq_grad = cross_sums[:local_width].T.astype(F32)
    cross_out_grad = cross_sums[local_width : 2 * local_width].astype(F32)
    ckv_grad = early_sums[:, fc_share + 48 : fc_share + 96].reshape(-1, model_width)
    ckv_grad = ckv_grad[: 2 * local_width, :text_width].astype(F32)
    ckv_grad = ckv_grad.T.reshape(text_width, 2, local_width)
    text_rows = early_sums[:, fc_share + 96 :].reshape(-1, model_width).astype(F32)
    text_grad = text_rows[:text_count, :text_width]
    cknorm_grad = text_rows[-1, :head_dim]
    (
        last_sums,
        latent_grad,
        skip_grad,
        output,
        fc1_grad,
        fc2_grad,
        cq_grad,
        cross_out_grad,
        ckv_grad,
        text_grad,
        cknorm_grad,
    ) = join(
        last_sums,
        latent_grad,
        skip_grad,
        output,
        fc1_grad,
        fc2_grad,
        cq_grad,
        cross_out_grad,
        ckv_grad,
        text_grad,
        cknorm_grad,
    )
    self_sums = last_sums[:, :share].reshape(-1, model_width)
    qkv_grad = self_sums[:qkv_rows].T.astype(F32).reshape(model_width, 3, local_width)
    attn_out_grad = self_sums[qkv_rows : qkv_rows + local_width].astype(F32)
    last_sums = last_sums[:, share:].reshape(4, 2, -1, model_width).transpose(1, 0, 2, 3)
    last_sums = last_sums.reshape(-1, model_width)
    skip_w_grad = last_sums[:slab_width].astype(F32)
    small = last_sums[slab_width:].astype(F32)
    skip_gain_grad, norm1_grad, norm2_grad, norm3_grad, mod_vector = [small[i] for i in range(5)]
    qnorm_grad, knorm_grad, cqnorm_grad = [
        small[5, i * head_dim : (i + 1) * head_dim] for i in range(3)
    ]
    mod_grad = silu_cond.astype(F32)[:, None] * mod_vector[None, :]
    return (
        output,
        latent_grad,
        skip_grad,
        text_grad,
        skip_w_grad,
        skip_gain_grad,
        norm1_grad,
        mod_grad,
        qkv_grad,
        qnorm_grad,
        knorm_grad,
        attn_out_grad,
        norm2_grad,
        cq_grad,
        ckv_grad,
        cqnorm_grad,
        cknorm_grad,
        cross_out_grad,
        norm3_grad,
        fc1_grad,
        fc2_grad,
    )


def solution(mesh):
    placed = (
        P("dp", None),
        P("dp", None),
        P(),
        P(),
        P("dp", None),
        P("dp", None),
        P("tensor", None),
        P(),
        P(),
        P(),
        P(None, None, "tensor"),
        P(),
        P(),
        P("tensor", None),
        P(),
        P(None, "tensor"),
        P(None, None, "tensor"),
        P(),
        P(),
        P("tensor", None),
        P(),
        P(None, "tensor"),
        P("tensor", None),
    )
    return jax.shard_map(
        local,
        mesh=mesh,
        in_specs=placed,
        out_specs=(
            P("dp", None),
            P("dp", None),
            P("dp", None),
            P(),
            P("tensor", None),
            P(),
            P(),
            P(),
            P(None, None, "tensor"),
            P(),
            P(),
            P("tensor", None),
            P(),
            P(None, "tensor"),
            P(None, None, "tensor"),
            P(),
            P(),
            P("tensor", None),
            P(),
            P(None, "tensor"),
            P("tensor", None),
        ),
        check_vma=False,
    )
```

```python
import jax
import jax.numpy as jnp
from jax import lax
from jax.experimental import pallas as pl
from jax.experimental.pallas import tpu as pltpu
from jax.sharding import PartitionSpec as P

BF16 = jnp.bfloat16
F32 = jnp.float32


def layer_norm(inputs, norm_gain):
    centered = inputs - jnp.mean(inputs, -1, keepdims=True)
    variance = jnp.mean(centered * centered, -1, keepdims=True)
    return centered * lax.rsqrt(variance + 1e-06) * norm_gain


def rotary_tables(positions, head_dim):
    quarter = head_dim // 4
    frequency = 10000.0 ** (-jnp.arange(quarter).astype(F32) / quarter)
    angles = positions.astype(F32)[:, :, None] * frequency
    cosine, sine = jnp.cos(angles), jnp.sin(angles)
    cos_wide = jnp.stack([cosine, cosine], 2).reshape(positions.shape[0], head_dim)
    sin_wide = jnp.stack([-sine, sine], 2).reshape(positions.shape[0], head_dim)
    return cos_wide, sin_wide


def left_product(inputs, grads):
    return lax.dot_general(
        inputs, grads, (((0,), (0,)), ((), ())), preferred_element_type=jnp.float32
    )


def right_product(grads, weight):
    return lax.dot_general(
        grads, weight, (((1,), (1,)), ((), ())), preferred_element_type=jnp.float32
    )


def exchange(blocks, axis="tensor"):
    return lax.all_to_all(blocks, axis, 0, 0, tiled=True)


def spread(block, axis="tensor"):
    count = lax.axis_size(axis)
    return jnp.broadcast_to(block[None], (count,) + block.shape)


def after(value, *earlier):
    return lax.optimization_barrier((value,) + earlier)[0]


def after_all(values, *earlier):
    return lax.optimization_barrier((tuple(values),) + earlier)[0]


def pad_rows(rows, multiple):
    extra = -rows.shape[0] % multiple
    return jnp.pad(rows, ((0, extra),) + ((0, 0),) * (rows.ndim - 1))


def ring_route(step):
    count = lax.axis_size("tensor")
    ring = count // 2
    return [(i, i // ring * ring + (i + step) % ring) for i in range(count)]


def ring_gather(block):
    ring = lax.axis_size("tensor") // 2
    got = {k: lax.ppermute(block, "tensor", ring_route(k)) for k in (1, 3, 2)}
    return [block] + [got[k] for k in range(1, ring)]


def ring_scatter(blocks):
    got = {k: lax.ppermute(blocks[k], "tensor", ring_route(-k)) for k in (1, 3, 2)}
    return [blocks[0]] + [got[k] for k in range(1, len(blocks))]


def place_blocks(blocks, half_blocks):
    ring = len(blocks)
    place = lax.axis_index("tensor")
    ring_place, half = place % ring, place // ring
    rows = blocks[0].shape[0]
    out = jnp.zeros((2 * ring * rows,) + blocks[0].shape[1:], blocks[0].dtype)
    for k in range(ring):
        at_ring = (ring_place - k) % ring
        for which, block in ((half, blocks[k]), (1 - half, half_blocks[k])):
            out = lax.dynamic_update_slice_in_dim(out, block, (which * ring + at_ring) * rows, 0)
    return out


def half_swap(block):
    count = lax.axis_size("tensor")
    return lax.ppermute(block, "tensor", [(i, (i + count // 2) % count) for i in range(count)])


def core_swap(block):
    count = lax.axis_size("dp")
    return lax.ppermute(block, "dp", [(i, i ^ 1) for i in range(count)])


def dp_slice(rows, unit):
    places = lax.axis_size("dp")
    each = -(-rows.shape[0] // (places * unit)) * unit
    rows = pad_rows(rows, each * places)
    return lax.dynamic_slice_in_dim(rows, lax.axis_index("dp") * each, each, 0)


def dp_routes():
    count = lax.axis_size("dp")
    place = lax.axis_index("dp")
    stages = []
    for low, size in ((0, 2), (1, 4), (3, 2)):
        part = place // (1 << low) % size
        routes = []
        for step in range(1, size):
            route = []
            for source in range(count):
                here = source // (1 << low) % size
                there = (here + step) % size
                route.append((source, source + ((there - here) << low)))
            routes.append(route)
        stages.append((size, part, routes))
    return stages


def join(*values):
    return lax.optimization_barrier(values)


def low_slice(rows, unit):
    places = len(low_groups()[0])
    each = -(-rows.shape[0] // (places * unit)) * unit
    rows = pad_rows(rows, each * places)
    return lax.dynamic_slice_in_dim(rows, lax.axis_index("dp") % places * each, each, 0)


def far_swap(block):
    dp_count, count = lax.axis_size("dp"), lax.axis_size("tensor")
    route = [
        (d * count + t, (d ^ 1) * count + (t + count // 2) % count)
        for d in range(dp_count)
        for t in range(count)
    ]
    return lax.ppermute(block, ("dp", "tensor"), route)


def low_swap(block):
    count = lax.axis_size("dp")
    return lax.ppermute(block, "dp", [(i, i ^ 8) for i in range(count)])


def low_groups():
    return [list(range(8)), list(range(8, 16))]


def scatter_low(rows):
    return lax.psum_scatter(
        rows, "dp", scatter_dimension=0, tiled=True, axis_index_groups=low_groups()
    )


def gather_low(rows):
    return lax.all_gather(rows, "dp", axis=0, tiled=False, axis_index_groups=low_groups())


def scatter_stage(stage, grads):
    size, part, routes = dp_routes()[stage]
    rows = grads.shape[1] // size
    cut = lambda place: lax.dynamic_slice_in_dim(grads, place * rows, rows, 1)
    total = cut(part).astype(F32)
    for step, route in enumerate(routes, 1):
        send = cut((part + step) % size).astype(BF16)
        total = total + lax.ppermute(send, "dp", route).astype(F32)
    return total


def half_sum(own, other):
    return own.astype(F32) + half_swap(other.astype(BF16)).astype(F32)


VMEM_LIMIT = 60 * 1024 * 1024


def cost(micros):
    return pl.CostEstimate(flops=0, transcendentals=0, bytes_accessed=int(micros * 3.3e6))


def call(kernel, micros, outs, ins, name, grid=None, in_specs=None, out_specs=None, scratch=()):
    extra = {}
    if grid:
        extra = {"grid": grid, "in_specs": in_specs, "out_specs": out_specs}
    return pl.pallas_call(
        kernel,
        out_shape=outs,
        scratch_shapes=scratch,
        compiler_params=pltpu.CompilerParams(
            vmem_limit_bytes=VMEM_LIMIT,
            dimension_semantics=("arbitrary",) * len(grid) if grid else None,
        ),
        cost_estimate=cost(micros),
        name=name,
        **extra,
    )(*ins)


def dot(left, right):
    return lax.dot_general(left, right, (((1,), (0,)), ((), ())), preferred_element_type=F32)


def dot_t(left, right):
    return lax.dot_general(left, right, (((1,), (1,)), ((), ())), preferred_element_type=F32)


def t_dot(left, right):
    return lax.dot_general(left, right, (((0,), (0,)), ((), ())), preferred_element_type=F32)


def norm_parts(rows):
    centered = rows - jnp.mean(rows, -1, keepdims=True)
    scale = lax.rsqrt(jnp.mean(centered * centered, -1, keepdims=True) + 1e-06)
    return centered * scale, scale


def norm_back(unit, scale, gain, grad):
    weighted = grad * gain
    rows = scale * (
        weighted
        - jnp.mean(weighted, -1, keepdims=True)
        - unit * jnp.mean(weighted * unit, -1, keepdims=True)
    )
    return rows, jnp.sum(grad * unit, 0, keepdims=True)


def add_all(refs):
    total = refs[0][...].astype(F32)
    for ref in refs[1:]:
        total = total + ref[...].astype(F32)
    return total


def stack(parts):
    return jnp.concatenate(parts, 0)


HBM = pl.BlockSpec(memory_space=pltpu.HBM)


def load_blocks(refs, x_ref, sems):
    rows = x_ref.shape[0] // len(refs)
    copies = [
        pltpu.make_async_copy(
            ref.at[pl.ds(0, rows)], x_ref.at[pl.ds(i * rows, rows)], sems.at[i]
        )
        for i, ref in enumerate(refs)
    ]
    for copy in copies:
        copy.start()
    for copy in copies:
        copy.wait()


def put_blocks(refs, value):
    rows = refs[0].shape[0]
    for i, ref in enumerate(refs):
        ref[...] = value[i * rows : (i + 1) * rows].astype(BF16)


def struct(shape, kind):
    return jax.ShapeDtypeStruct(shape, kind)


def whole(shape):
    return pl.BlockSpec(shape, lambda *place: (0,) * len(shape))


def at(shape, row):
    return pl.BlockSpec(shape, lambda *place: (row,) + (0,) * (len(shape) - 1))


def swap(rows):
    quarter = rows.shape[1] // 4
    cut = [rows[:, i * quarter : (i + 1) * quarter] for i in range(4)]
    return jnp.concatenate([cut[1], cut[0], cut[3], cut[2]], 1)


def pack_spec(rows, width, place, share=16):
    return pl.BlockSpec((rows // share, share, width), lambda *step: (0, place // share, 0))


def pack_rows(pack_ref):
    return pack_ref[...].reshape(-1, pack_ref.shape[2])


def first_norms(got, skip_gain, norm1_gain, shift, along):
    count, rows, width = got.shape

    def kernel(got_ref, skip_ref, gain_ref, shift_ref, along_ref, merged_ref, hidden_ref, out_ref):
        merged = add_all([got_ref.at[i] for i in range(count)])
        merged_ref[...] = merged
        hidden = norm_parts(merged)[0] * skip_ref[...]
        hidden_ref[...] = hidden
        out_ref[:rows] = (norm_parts(hidden)[0] * gain_ref[...] + shift_ref[...]).astype(BF16)
        out_ref[rows:] = along_ref[...]

    outs = (
        struct((rows, width), F32),
        struct((rows, width), F32),
        struct((rows + along.shape[0], width), BF16),
    )
    ins = (got, skip_gain[None], norm1_gain[None], shift[None], along)
    return call(kernel, 2.5, outs, ins, "first_norms")


def mid_norm(pieces, hidden, gain):
    def kernel(*refs):
        hidden_ref, gain_ref, new_ref, out_ref = refs[len(pieces) :]
        new = hidden_ref[...] + add_all(refs[: len(pieces)])
        new_ref[...] = new
        out_ref[...] = (norm_parts(new)[0] * gain_ref[...]).astype(BF16)

    outs = (struct(hidden.shape, F32), struct(hidden.shape, BF16))
    return call(kernel, 1.5, outs, (*pieces, hidden, gain[None]), "mid_norm")


def mid_norm_back(pieces, residual, hidden, gain):
    def kernel(*refs):
        res_ref, hidden_ref, gain_ref, new_ref, out_ref, dgain_ref = refs[len(pieces) :]
        unit, scale = norm_parts(hidden_ref[...])
        grad, dgain = norm_back(unit, scale, gain_ref[...], add_all(refs[: len(pieces)]))
        dgain_ref[...] = dgain
        new = res_ref[...].astype(F32) + grad
        new_ref[...] = new
        out_ref[...] = new.astype(BF16)

    width = hidden.shape[1]
    outs = (struct(hidden.shape, F32), struct(hidden.shape, BF16), struct((1, width), F32))
    return call(kernel, 2, outs, (*pieces, residual, hidden, gain[None]), "mid_norm_back")


def last_norms(pieces, hidden_zero, merged, residual, gains, rows_two, rows_three, misc):
    rows, width = merged.shape
    many = len(pieces)

    def kernel(*refs):
        h0_ref, merged_ref, res_ref, g1_ref, gs_ref, two_ref, three_ref, misc_ref, out_ref = refs[many:]
        grad = add_all(refs[:many])
        shift_grad = jnp.sum(grad, 0, keepdims=True)
        unit, scale = norm_parts(h0_ref[...])
        step, norm1_grad = norm_back(unit, scale, g1_ref[...], grad)
        residual = res_ref[...] + step
        unit, scale = norm_parts(merged_ref[...])
        step, skip_grad = norm_back(unit, scale, gs_ref[...], residual)
        small = [skip_grad, norm1_grad, two_ref[...], three_ref[...], shift_grad, misc_ref[...]]
        small = stack(small + [jnp.zeros((16 - len(small), width), F32)]).astype(BF16)
        out_ref[:rows] = step.astype(BF16)
        out_ref[rows:] = small

    ins = (*pieces, hidden_zero, merged, residual, gains[0][None], gains[1][None])
    ins += (rows_two, rows_three, misc)
    return call(kernel, 3, struct((rows + 16, width), BF16), ins, "last_norms")


def project(parts, weight, other, cos_wide, sin_wide, qgain, kgain):
    width = parts[0].shape[1]
    tokens = cos_wide.shape[0]
    wide = weight.shape[0]
    each = wide // 3
    head = qgain.shape[0]
    heads = each // head
    many = len(parts)

    def kernel(*refs):
        w_ref, o_ref, cos_ref, sin_ref, qg_ref, kg_ref = refs[many : many + 6]
        x_ref, unit_ref, scale_ref, q_ref, kv_ref, sems = refs[many + 6 :]
        load_blocks(refs[:many], x_ref, sems)
        cos, sin = cos_ref[...], sin_ref[...]
        for s in range(2):
            out = dot_t(x_ref[...], w_ref[...] if s == 0 else pack_rows(o_ref))
            base = 2 * each * s
            kv_ref[:, base + each : base + 2 * each] = out[:, 2 * each :].astype(BF16)
            for h in range(heads):
                cut = lambda start: slice(start + h * head, start + (h + 1) * head)
                turn = lambda v: (v * cos + swap(v) * sin).astype(BF16)
                for part, gain_ref in ((0, qg_ref), (1, kg_ref)):
                    unit, scale = norm_parts(out[:, cut(part * each)])
                    n = (s * 2 + part) * heads + h
                    unit_ref[:, cut(base + part * each)] = unit
                    scale_ref[:, n : n + 1] = scale
                    if part == 0:
                        q_ref[:, cut(each * s)] = turn(unit * gain_ref[...])
                    else:
                        kv_ref[:, cut(base)] = turn(unit * gain_ref[...])

    outs = (
        struct((tokens, width), BF16),
        struct((tokens, 4 * each), F32),
        struct((tokens, 4 * heads), F32),
        struct((tokens, 2 * each), BF16),
        struct((tokens, 4 * each), BF16),
    )
    ins = (*parts, weight, other, cos_wide, sin_wide, qgain[None], kgain[None])
    specs = [HBM] * many + [whole(item.shape) for item in ins[many:]]
    specs[many + 1] = pack_spec(wide, width, 0, 48)
    return call(
        kernel, 6, outs, ins, "project", (1,), specs, tuple(whole(o.shape) for o in outs),
        (pltpu.SemaphoreType.DMA((many,)),),
    )


def key_rows(refs, shard, start, size, each):
    first = 2 * each * shard + start
    second = 2 * each * (1 - shard) + start
    return stack(
        [
            ref[:, first : first + size] if i < 2 else ref[:, second : second + size]
            for i, ref in enumerate(refs)
        ]
    )


def self_attention(queries, pairs, out_w, pack, head):
    tokens, both = queries.shape
    each = both // 2
    heads = each // head
    width = out_w.shape[1]
    scaling = head ** (-0.5)

    def kernel(q_ref, a_ref, b_ref, c_ref, d_ref, w_ref, o_ref, mixed_ref, total_ref, *out_refs):
        refs = (a_ref, b_ref, c_ref, d_ref)
        for s in range(2):
            for h in range(heads):
                n = s * heads + h
                cut = slice(n * head, (n + 1) * head)
                scores = dot_t(q_ref[:, cut], key_rows(refs, s, h * head, head, each)) * scaling
                most = jnp.max(scores, -1, keepdims=True)
                total = most + jnp.log(jnp.sum(jnp.exp(scores - most), -1, keepdims=True))
                total_ref[:, n : n + 1] = total
                shares = jnp.exp(scores - total).astype(BF16)
                mixture = dot(shares, key_rows(refs, s, each + h * head, head, each))
                mixed_ref[:, cut] = mixture.astype(BF16)
        out = dot(mixed_ref[:, :each], w_ref[...])
        out = out + dot(mixed_ref[:, each:], pack_rows(o_ref))
        put_blocks(out_refs, out)

    outs = (
        struct((tokens, both), BF16),
        struct((tokens, 2 * heads), F32),
    ) + (struct((tokens // 4, width), BF16),) * 4
    ins = (queries, *pairs, out_w, pack)
    specs = [whole(item.shape) for item in ins]
    specs[-1] = pack_spec(each, width, 48)
    return call(
        kernel, 5, outs, ins, "self_attention", (1,), specs, tuple(whole(o.shape) for o in outs)
    )


def self_attention_back(queries, pairs, totals, parts, out_w, pack, head):
    tokens, both = queries.shape
    each = both // 2
    heads = each // head
    rows, width = parts[0].shape
    scaling = head ** (-0.5)
    many = len(parts)

    def kernel(*refs):
        q_ref, a_ref, b_ref, c_ref, d_ref, total_ref, w_ref, o_ref = refs[many : many + 8]
        x_ref, dq_ref, own_ref, half_ref, core_ref, far_ref, dm_ref, sems = refs[many + 8 :]
        pair_refs = (a_ref, b_ref, c_ref, d_ref)
        load_blocks(refs[:many], x_ref, sems)
        dm_ref[:, :each] = dot_t(x_ref[...], w_ref[...]).astype(BF16)
        dm_ref[:, each:] = dot_t(x_ref[...], pack_rows(o_ref)).astype(BF16)

        def put(grads, shard, start):
            first = 2 * each * shard + start
            second = 2 * each * (1 - shard) + start
            cut = lambda i: grads[i * tokens : (i + 1) * tokens]
            own_ref[:, first : first + head] = cut(0)
            core_ref[:, first : first + head] = cut(1).astype(BF16)
            half_ref[:, second : second + head] = cut(2).astype(BF16)
            far_ref[:, second : second + head] = cut(3).astype(BF16)

        for s in range(2):
            for h in range(heads):
                n = s * heads + h
                cut = slice(n * head, (n + 1) * head)
                mine, grads = q_ref[:, cut], dm_ref[:, cut]
                keys_h = key_rows(pair_refs, s, h * head, head, each)
                values_h = key_rows(pair_refs, s, each + h * head, head, each)
                shares = jnp.exp(dot_t(mine, keys_h) * scaling - total_ref[:, n : n + 1])
                dshares = dot_t(grads, values_h)
                put(t_dot(shares.astype(BF16), grads), s, each + h * head)
                weighted = jnp.sum(shares * dshares, -1, keepdims=True)
                dscores = (shares * (dshares - weighted) * scaling).astype(BF16)
                dq_ref[:, cut] = dot(dscores, keys_h)
                put(t_dot(dscores, mine), s, h * head)

    outs = (
        struct((tokens, width), BF16),
        struct((tokens, both), F32),
        struct((tokens, 4 * each), F32),
        struct((tokens, 4 * each), BF16),
        struct((tokens, 4 * each), BF16),
        struct((tokens, 4 * each), BF16),
    )
    ins = (*parts, queries, *pairs, totals, out_w, pack)
    specs = [HBM] * many + [whole(item.shape) for item in ins[many:]]
    specs[-1] = pack_spec(each, width, 48)
    return call(
        kernel, 9, outs, ins, "self_attention_back", (1,), specs,
        tuple(whole(o.shape) for o in outs),
        (pltpu.VMEM((tokens, both), BF16), pltpu.SemaphoreType.DMA((many,))),
    )


def project_back(units, scales, cos_wide, sin_wide, qgain, kgain, dq, own, core, half, far, weight, other):
    tokens = units.shape[0]
    wide, width = weight.shape
    each = wide // 3
    head = qgain.shape[0]
    heads = each // head

    def kernel(unit_ref, scale_ref, cos_ref, sin_ref, qg_ref, kg_ref, dq_ref, own_ref, core_ref, half_ref, far_ref, w_ref, o_ref,
               mine_ref, other_ref, dqg_ref, dkg_ref, *out_refs):
        cos, sin = cos_ref[...], sin_ref[...]
        dkv = own_ref[...] + core_ref[...].astype(F32)
        dkv = dkv + half_ref[...].astype(F32) + far_ref[...].astype(F32)
        dgains = [jnp.zeros((1, head), F32), jnp.zeros((1, head), F32)]
        for s, to_ref in ((0, mine_ref), (1, other_ref)):
            base = 2 * each * s
            to_ref[:, 2 * each : 3 * each] = dkv[:, base + each : base + 2 * each].astype(BF16)
            for h in range(heads):
                cut = lambda start: slice(start + h * head, start + (h + 1) * head)
                for part, gain_ref in ((0, qg_ref), (1, kg_ref)):
                    turned = dq_ref[:, cut(each * s)] if part == 0 else dkv[:, cut(base)]
                    grad = turned * cos - swap(turned) * sin
                    n = (s * 2 + part) * heads + h
                    unit = unit_ref[:, cut(base + part * each)]
                    grad, dgain = norm_back(unit, scale_ref[:, n : n + 1], gain_ref[...], grad)
                    dgains[part] = dgains[part] + dgain
                    to_ref[:, cut(part * each)] = grad.astype(BF16)
        dqg_ref[...], dkg_ref[...] = dgains
        out = dot(mine_ref[...], w_ref[...])
        put_blocks(out_refs, out + dot(other_ref[...], pack_rows(o_ref)))

    outs = (
        struct((tokens, wide), BF16),
        struct((tokens, wide), BF16),
        struct((1, head), F32),
        struct((1, head), F32),
    ) + (struct((tokens // 4, width), BF16),) * 4
    ins = (units, scales, cos_wide, sin_wide, qgain[None], kgain[None], dq, own, core, half, far, weight, other)
    specs = [whole(item.shape) for item in ins]
    specs[-1] = pack_spec(wide, width, 0, 48)
    return call(
        kernel, 8, outs, ins, "project_back", (1,), specs, tuple(whole(o.shape) for o in outs)
    )


def text_shares(scores, scaling, count):
    place = lax.broadcasted_iota(jnp.int32, scores.shape, 1)
    scores = jnp.where(place < count, scores * scaling, -1e30)
    most = jnp.max(scores, -1, keepdims=True)
    total = most + jnp.log(jnp.sum(jnp.exp(scores - most), -1, keepdims=True))
    return jnp.exp(scores - total)


def cross_layer(parts, cq_w, out_w, pack, text, other_text, gain, text_count):
    rows, width = parts[0].shape
    tokens = rows * len(parts)
    each = cq_w.shape[0]
    head = gain.shape[0]
    heads = each // head
    scaling = head ** (-0.5)
    many = len(parts)

    def kernel(*refs):
        cq_ref, w_ref, ocq_ref, ow_ref, text_ref, otext_ref, gain_ref = refs[many : many + 7]
        x_ref, raw_ref, mixed_ref, *out_refs, sems = refs[many + 7 :]
        load_blocks(refs[:many], x_ref, sems)
        raw_ref[:, :each] = dot_t(x_ref[...], cq_ref[...])
        raw_ref[:, each:] = dot_t(x_ref[...], pack_rows(ocq_ref))
        for s, keys_ref in ((0, text_ref), (1, otext_ref)):
            for h in range(heads):
                n = s * heads + h
                cut = slice(n * head, (n + 1) * head)
                mine = (norm_parts(raw_ref[:, cut])[0] * gain_ref[...]).astype(BF16)
                scores = dot_t(mine, keys_ref[:, h * head : (h + 1) * head])
                shares = text_shares(scores, scaling, text_count).astype(BF16)
                values = keys_ref[:, each + h * head : each + (h + 1) * head]
                mixed_ref[:, cut] = dot(shares, values).astype(BF16)
        out = dot(mixed_ref[:, :each], w_ref[...])
        out = out + dot(mixed_ref[:, each:], pack_rows(ow_ref))
        put_blocks(out_refs, out)

    outs = (
        struct((tokens, width), BF16),
        struct((tokens, 2 * each), F32),
        struct((tokens, 2 * each), BF16),
    ) + (struct((rows, width), BF16),) * many
    ins = (*parts, cq_w, out_w, pack, pack, text, other_text, gain[None])
    specs = [HBM] * many + [whole(item.shape) for item in ins[many:]]
    specs[many + 2] = pack_spec(each, width, 0)
    specs[many + 3] = pack_spec(each, width, 16)
    return call(
        kernel, 7, outs, ins, "cross_layer", (1,), specs, tuple(whole(o.shape) for o in outs),
        (pltpu.SemaphoreType.DMA((many,)),),
    )


def cross_layer_back(parts, raw, cq_w, out_w, pack, text, other_text, gain, text_count):
    rows, width = parts[0].shape
    tokens = rows * len(parts)
    each = cq_w.shape[0]
    head = gain.shape[0]
    heads = each // head
    scaling = head ** (-0.5)
    many = len(parts)

    def kernel(*refs):
        raw_ref, cq_ref, w_ref, ocq_ref, ow_ref, text_ref, otext_ref, gain_ref = refs[many : many + 8]
        x_ref, draw_ref, dtext_ref, dother_ref, dgain_ref, *out_refs, dm_ref, sems = refs[many + 8 :]
        load_blocks(refs[:many], x_ref, sems)
        dm_ref[:, :each] = dot_t(x_ref[...], w_ref[...]).astype(BF16)
        dm_ref[:, each:] = dot_t(x_ref[...], pack_rows(ow_ref)).astype(BF16)
        dgain = jnp.zeros((1, head), F32)
        for s, keys_ref, to_ref in ((0, text_ref, dtext_ref), (1, otext_ref, dother_ref)):
            for h in range(heads):
                n = s * heads + h
                cut = slice(n * head, (n + 1) * head)
                kcut = slice(h * head, (h + 1) * head)
                vcut = slice(each + h * head, each + (h + 1) * head)
                unit, scale = norm_parts(raw_ref[:, cut])
                mine = (unit * gain_ref[...]).astype(BF16)
                shares = text_shares(dot_t(mine, keys_ref[:, kcut]), scaling, text_count)
                dshares = dot_t(dm_ref[:, cut], keys_ref[:, vcut])
                to_ref[:, vcut] = t_dot(shares.astype(BF16), dm_ref[:, cut]).astype(BF16)
                weighted = jnp.sum(shares * dshares, -1, keepdims=True)
                dscores = (shares * (dshares - weighted) * scaling).astype(BF16)
                to_ref[:, kcut] = t_dot(dscores, mine).astype(BF16)
                grad, step = norm_back(unit, scale, gain_ref[...], dot(dscores, keys_ref[:, kcut]))
                dgain = dgain + step
                draw_ref[:, cut] = grad.astype(BF16)
        dgain_ref[...] = dgain
        out = dot(draw_ref[:, :each], cq_ref[...])
        out = out + dot(draw_ref[:, each:], pack_rows(ocq_ref))
        put_blocks(out_refs, out)

    outs = (
        struct((tokens, width), BF16),
        struct((tokens, 2 * each), BF16),
        struct(text.shape, BF16),
        struct(text.shape, BF16),
        struct((1, head), F32),
    ) + (struct((rows, width), BF16),) * many
    ins = (*parts, raw, cq_w, out_w, pack, pack, text, other_text, gain[None])
    specs = [HBM] * many + [whole(item.shape) for item in ins[many:]]
    specs[many + 3] = pack_spec(each, width, 0)
    specs[many + 4] = pack_spec(each, width, 16)
    return call(
        kernel, 10, outs, ins, "cross_layer_back", (1,), specs,
        tuple(whole(o.shape) for o in outs),
        (pltpu.VMEM((tokens, 2 * each), BF16), pltpu.SemaphoreType.DMA((many,))),
    )


def feed_forward(parts, cot, fc1_w, fc2_w, pack):
    rows, width = parts[0].shape
    tokens = rows * len(parts)
    hidden = fc2_w.shape[0]
    block = hidden // 2
    places = pack.shape[0]
    each = hidden // places
    both = 2 * each
    root = (2 / 3.141592653589793) ** 0.5
    many = len(parts)

    def kernel(*refs):
        cot_ref, w1_ref, w2_ref, pack_ref, x_ref, acts_ref, *out_refs, acc_ref, sum_ref, sems = refs[many:]
        step = pl.program_id(0)

        @pl.when(step == 0)
        def _():
            load_blocks(refs[:many], x_ref, sems)
            acc_ref[...] = jnp.zeros_like(acc_ref)
            sum_ref[...] = jnp.zeros_like(sum_ref)

        def work(pre, w2, back):
            square = pre * pre
            bent = jnp.tanh(root * pre * (1 + 0.044715 * square))
            part = 0.5 * (1 + bent)
            slope = part + 0.5 * pre * (1 - bent * bent) * root * (1 + 3 * 0.044715 * square)
            grad = (dot_t(cot_ref[...], w2) * slope).astype(BF16)
            acts_ref[0, 0] = grad
            active = (pre * part).astype(BF16)
            acts_ref[0, 1] = active
            acc_ref[...] += back(grad)
            sum_ref[...] += dot(active, w2)

        @pl.when(step < 2)
        def _():
            weight = w1_ref[...]
            work(dot(x_ref[...], weight), w2_ref[...], lambda grad: dot_t(grad, weight))

        @pl.when(step >= 2)
        def _():
            weight = pack_ref[:, :each].reshape(block, width)
            second = pack_ref[:, each:].reshape(block, width)
            work(dot_t(x_ref[...], weight), second, lambda grad: dot(grad, weight))

        @pl.when(step == 3)
        def _():
            put_blocks(out_refs[:many], acc_ref[...])
            put_blocks(out_refs[many:], sum_ref[...])

    low = lambda i: jnp.minimum(i, 1)
    high = lambda i: jnp.maximum(i - 2, 0)
    outs = (
        struct((tokens, width), BF16),
        struct((2, 2, tokens, hidden), BF16),
    ) + (struct((rows, width), BF16),) * (2 * many)
    out_specs = (
        whole((tokens, width)),
        pl.BlockSpec((1, 2, tokens, block), lambda i: (i // 2, 0, 0, i % 2)),
    ) + (whole((rows, width)),) * (2 * many)
    in_specs = [HBM] * many + [
        whole(cot.shape),
        pl.BlockSpec((width, block), lambda i: (0, low(i))),
        pl.BlockSpec((block, width), lambda i: (low(i), 0)),
        pl.BlockSpec((places // 2, both, width), lambda i: (high(i), 0, 0)),
    ]
    return call(
        kernel, 9, outs, (*parts, cot, fc1_w, fc2_w, pack), "feed_forward", (4,), in_specs, out_specs,
        (
            pltpu.VMEM((tokens, width), F32),
            pltpu.VMEM((tokens, width), F32),
            pltpu.SemaphoreType.DMA((many,)),
        ),
    )


def feed_forward_grads(acts, rows_in, cot, places):
    _, _, tokens, hidden = acts.shape
    width = cot.shape[1]
    share = 2 * hidden // places

    def kernel(acts_ref, x_ref, cot_ref, out_ref):
        which = pl.program_id(1)

        def put(right_ref):
            grads = t_dot(acts_ref[0, 0], right_ref[...]).astype(BF16)
            out_ref[...] = grads.reshape(out_ref.shape)

        pl.when(which == 0)(lambda: put(x_ref))
        pl.when(which == 1)(lambda: put(cot_ref))

    return call(
        kernel,
        7,
        struct((places, 2, share, width), BF16),
        (acts, rows_in, cot),
        "feed_forward_grads",
        (2, 2),
        [
            pl.BlockSpec((1, 1, tokens, hidden), lambda s, w: (s, w, 0, 0)),
            whole(rows_in.shape),
            whole(cot.shape),
        ],
        pl.BlockSpec((places // 2, 1, share, width), lambda s, w: (w, s, 0, 0)),
    )


def put_shares(out_ref, shard, to, share, rows_ref):
    stop, width = rows_ref.shape
    for place in range(out_ref.shape[0]):
        begin = min(place * share, stop)
        count = min(share, stop - begin)
        if count:
            out_ref[place, shard, to : to + count] = rows_ref[begin : begin + count]
        if count < share:
            out_ref[place, shard, to + count : to + share] = jnp.zeros((share - count, width), BF16)


def cross_grads(draw, mixed, rows_in, grad_rows, places, share):
    each = draw.shape[1] // 2
    width = rows_in.shape[1]

    def kernel(draw_ref, mixed_ref, x_ref, d_ref, out_ref, hold_ref):
        for s in range(2):
            cut = slice(s * each, (s + 1) * each)
            hold_ref[:each] = t_dot(draw_ref[:, cut], x_ref[...]).astype(BF16)
            hold_ref[each:] = t_dot(mixed_ref[:, cut], d_ref[...]).astype(BF16)
            put_shares(out_ref, s, 0, share, hold_ref)

    ins = (draw, mixed, rows_in, grad_rows)
    scratch = (pltpu.VMEM((2 * each, width), BF16),)
    return call(kernel, 4, struct((places, 2, share, width), BF16), ins, "cross_grads", scratch=scratch)


def self_grads(mine, other, mixed, rows_in, grad_rows, places, share):
    wide = mine.shape[1]
    each = wide // 3
    width = rows_in.shape[1]

    def kernel(mine_ref, other_ref, mixed_ref, x_ref, d_ref, out_ref, hold_ref):
        for s, grad_ref in ((0, mine_ref), (1, other_ref)):
            cut = slice(s * each, (s + 1) * each)
            hold_ref[:wide] = t_dot(grad_ref[...], x_ref[...]).astype(BF16)
            hold_ref[wide:] = t_dot(mixed_ref[:, cut], d_ref[...]).astype(BF16)
            put_shares(out_ref, s, 0, share, hold_ref)

    ins = (mine, other, mixed, rows_in, grad_rows)
    scratch = (pltpu.VMEM((wide + each, width), BF16),)
    return call(kernel, 5, struct((places, 2, share, width), BF16), ins, "self_grads", scratch=scratch)


def skip_grads(parts, joined_own, joined_other, long):
    rows, width = parts[0].shape
    small = 16
    rows -= small
    tokens, slab = joined_own.shape
    many = len(parts)

    def kernel(*refs):
        own_ref, other_ref, x_ref, out_ref, all_ref, sems = refs[many:]
        load_blocks(refs[:many], all_ref, sems)
        total = jnp.zeros((small, width), F32)
        for i in range(many):
            start = i * (rows + small)
            x_ref[i * rows : (i + 1) * rows] = all_ref[start : start + rows]
            total = total + all_ref[start + rows : start + rows + small].astype(F32)
        for s, left_ref in ((0, own_ref), (1, other_ref)):
            out_ref[s, :slab] = t_dot(left_ref[...], x_ref[...])
            out_ref[s, slab : slab + small] = total
            out_ref[s, slab + small :] = jnp.zeros((long - slab - small, width), F32)

    outs = (struct((tokens, width), BF16), struct((2, long, width), F32))
    ins = (*parts, joined_own, joined_other)
    return call(
        kernel, 4, outs, ins, "skip_grads", (1,),
        [HBM] * many + [whole(joined_own.shape), whole(joined_other.shape)],
        tuple(whole(o.shape) for o in outs),
        (pltpu.VMEM((many * (rows + small), width), BF16), pltpu.SemaphoreType.DMA((many,))),
    )


def joined_grads(rows_in, pack, slab):
    tokens, width = rows_in.shape
    held, count, deep, _ = pack.shape
    half = count // 2

    def kernel(x_ref, pack_ref, one_ref, two_ref):
        for step, out_ref in ((0, one_ref), (1, two_ref)):

            @pl.when(pl.program_id(0) == step)
            def _(out_ref=out_ref):
                for j in range(half):
                    weight = pack_ref[:, j].reshape(held * deep, width)[:slab]
                    out_ref[:, j * slab : (j + 1) * slab] = dot_t(x_ref[...], weight)

    outs = (struct((tokens, width), F32), struct((tokens, width), F32))
    return call(
        kernel, 9, outs, (rows_in, pack), "joined_grads", (2,),
        [
            whole(rows_in.shape),
            pl.BlockSpec((held, half, deep, width), lambda i: (0, i, 0, 0)),
        ],
        (whole((tokens, width)), whole((tokens, width))),
    )


def feed_forward_out(sums, share):
    places, _, width = sums.shape
    half = places // 2
    hidden = half * share

    def kernel(sum_ref, one_ref, two_ref):
        @pl.when(pl.program_id(0) == 0)
        def _():
            one_ref[...] = sum_ref[...].reshape(hidden, width).astype(F32).T

        @pl.when(pl.program_id(0) == 1)
        def _():
            two_ref[...] = sum_ref[...].reshape(hidden, width).astype(F32)

    outs = (struct((width, hidden), F32), struct((hidden, width), F32))
    return call(
        kernel, 6, outs, (sums,), "feed_forward_out", (2,),
        [pl.BlockSpec((half, share, width), lambda i: (i, 0, 0))],
        (whole((width, hidden)), whole((hidden, width))),
    )


def text_layer(tokens, ckv, gain, rows):
    count, width = tokens.shape
    packed = ckv.ndim == 3
    both = ckv.shape[2] // 4 if packed else ckv.shape[1]
    each = both // 2
    head = gain.shape[0]
    heads = each // head

    def kernel(x_ref, w_ref, gain_ref, pair_ref, unit_ref, scale_ref, *more):
        if packed:
            weight_ref = more[0]
            deep = w_ref.shape[1]
            for place in range(w_ref.shape[0]):
                for k in range(4):
                    start = (place * 4 + k) * deep
                    weight_ref[start : start + deep] = w_ref[place, :, k * both : (k + 1) * both]
        else:
            weight_ref = w_ref
        out = dot(x_ref[...], weight_ref[...])
        pair_ref[...] = jnp.zeros_like(pair_ref)
        pair_ref[:count, each:] = out[:, each:].astype(BF16)
        for h in range(heads):
            cut = slice(h * head, (h + 1) * head)
            unit, scale = norm_parts(out[:, cut])
            unit_ref[:, cut] = unit
            scale_ref[:, h : h + 1] = scale
            pair_ref[:count, cut] = (unit * gain_ref[...]).astype(BF16)

    outs = (
        struct((rows, both), BF16),
        struct((count, each), F32),
        struct((count, heads), F32),
    )
    specs = [whole(tokens.shape), whole(ckv.shape), whole((1, head))]
    if packed:
        outs += (struct((width, both), BF16),)
        deep = width // ckv.shape[0] // 4
        place = ckv.shape[1] // deep - 1
        specs[1] = pl.BlockSpec((ckv.shape[0], deep, ckv.shape[2]), lambda *step: (0, place, 0))
    return call(
        kernel, 4, outs, (tokens, ckv, gain[None]), "text_layer", (1,), specs,
        tuple(whole(o.shape) for o in outs),
    )


def text_layer_back(crosses, pairs, units, scales, tokens, ckvs, gain):
    count, width = tokens.shape
    both = ckvs[0].shape[1]
    each = both // 2
    head = gain.shape[0]
    heads = each // head
    places, _, first, wide = crosses.shape
    deep = 48
    more = 48
    long = more * places

    def kernel(first_ref, a_ref, b_ref, ua_ref, ub_ref, sa_ref, sb_ref, x_ref, wa_ref, wb_ref, gain_ref, out_ref, dw_ref, grad_ref, part_ref):
        dgain = jnp.zeros((1, head), F32)
        part = jnp.zeros((count, width), F32)
        for s, (pair_ref, unit_ref, scale_ref, w_ref) in enumerate(
            ((a_ref, ua_ref, sa_ref, wa_ref), (b_ref, ub_ref, sb_ref, wb_ref))
        ):
            grad_ref[:, each:] = pair_ref[:count, each:]
            for h in range(heads):
                cut = slice(h * head, (h + 1) * head)
                grad, step = norm_back(
                    unit_ref[:, cut], scale_ref[:, h : h + 1], gain_ref[...], pair_ref[:count, cut].astype(F32)
                )
                dgain = dgain + step
                grad_ref[:, cut] = grad.astype(BF16)
            dw_ref[...] = t_dot(grad_ref[...], x_ref[...]).astype(BF16)
            part = part + dot_t(grad_ref[...], w_ref[...])
            for place in range(places):
                begin = min(place * deep, both)
                held = min(deep, both - begin)
                out_ref[place, s, :first] = first_ref[place, s]
                out_ref[place, s, first : first + deep] = jnp.zeros((deep, wide), BF16)
                out_ref[place, s, first : first + held, :width] = dw_ref[begin : begin + held]
        part_ref[...] = jnp.zeros_like(part_ref)
        part_ref[:count, :width] = part
        part_ref[long - 1 :, :head] = dgain
        for place in range(places):
            rows = part_ref[place * more : (place + 1) * more].astype(BF16)
            for s in range(2):
                out_ref[place, s, first + deep :] = rows

    ins = (crosses, *pairs, *units, *scales, tokens, *ckvs, gain[None])
    scratch = (
        pltpu.VMEM((both, width), BF16),
        pltpu.VMEM((count, both), BF16),
        pltpu.VMEM((long, wide), F32),
    )
    return call(
        kernel, 9, struct((places, 2, first + deep + more, wide), BF16), ins, "text_layer_back", scratch=scratch
    )


def local(
    latent,
    skip_input,
    text_tokens,
    condition,
    positions,
    cotangent,
    skip_w,
    skip_gain,
    norm1_gain,
    mod_w,
    qkv_w,
    qnorm_gain,
    knorm_gain,
    attn_out_w,
    norm2_gain,
    cq_w,
    ckv_w,
    cqnorm_gain,
    cknorm_gain,
    cross_out_w,
    norm3_gain,
    fc1_w,
    fc2_w,
):
    token_count, model_width = latent.shape
    head_dim = qnorm_gain.shape[0]
    local_width = cq_w.shape[1]
    local_heads = local_width // head_dim
    slab_width = skip_w.shape[0]
    hidden_width = fc1_w.shape[1]
    text_count, text_width = text_tokens.shape
    tensor_place = lax.axis_index("tensor")
    tensor_count = lax.axis_size("tensor")
    dp_count = lax.axis_size("dp")
    low_count = len(low_groups()[0])
    part_count = token_count // tensor_count
    ring = tensor_count // 2
    ring_place, half = tensor_place % ring, tensor_place // ring
    qkv_rows = 3 * local_width

    def own_rows(rows):
        return lax.dynamic_slice_in_dim(rows, tensor_place * part_count, part_count, 0)

    def ring_rows(rows, which):
        first = which * ring
        return jnp.concatenate(
            [
                lax.dynamic_slice_in_dim(
                    rows, (first + (ring_place - k) % ring) * part_count, part_count, 0
                )
                for k in range(ring)
            ],
            0,
        )

    joined = jnp.concatenate([latent, skip_input], 1)
    joined_part = lax.dynamic_slice_in_dim(joined, tensor_place * slab_width, slab_width, 1)
    partial = jnp.dot(joined_part, skip_w, preferred_element_type=F32).astype(BF16)

    dp_place = lax.axis_index("dp")
    qkv_flat = qkv_w.transpose(1, 2, 0).reshape(qkv_rows, model_width)
    cq_turned = cq_w.T
    shares = [dp_slice(qkv_flat, 48), dp_slice(attn_out_w, 16)]
    share, partial = join(half_swap(jnp.concatenate(shares, 0)), partial)
    got = exchange(partial.reshape(tensor_count, part_count, model_width))
    pack = lax.all_gather(share, "dp", axis=0, tiled=False)
    ckv_flat = ckv_w.reshape(text_width, 2 * local_width)
    text_rows_in = pad_rows(text_tokens, model_width // 4)
    text_pair, text_units, text_scales = text_layer(
        text_rows_in, ckv_flat, cknorm_gain, model_width // 4
    )
    share = hidden_width // dp_count
    deep = text_width // dp_count // 4
    share = hidden_width // low_count
    low_place = dp_place % low_count
    ff_share = [
        lax.dynamic_slice_in_dim(fc1_w, low_place * share, share, 1).T,
        lax.dynamic_slice_in_dim(fc2_w, low_place * share, share, 0),
    ]
    ff_share = jnp.concatenate(ff_share, 0)
    ckv_share = lax.dynamic_slice_in_dim(ckv_flat, dp_place * 4 * deep, 4 * deep, 0)
    cross_share = [dp_slice(rows, 16) for rows in (cq_turned, cross_out_w)]
    cross_share.append(jnp.concatenate(jnp.split(ckv_share, 4), 1))
    cross_share = jnp.concatenate(cross_share, 0)
    silu_cond = jax.nn.silu(condition.astype(F32)).astype(BF16)
    shift = jnp.dot(silu_cond[None], mod_w, preferred_element_type=F32)[0]
    cos_wide, sin_wide = rotary_tables(ring_rows(positions, half), head_dim)
    cot_rows = ring_rows(cotangent, half)
    got, cos_wide, sin_wide, shift, text_pair, cot_rows, ff_share, cross_share = join(
        got, cos_wide, sin_wide, shift, text_pair, cot_rows, ff_share, cross_share
    )
    skip_share = low_slice(skip_w, 16)
    merged, hidden_zero, normed = first_norms(got, skip_gain, norm1_gain, shift, skip_share)
    normed_parts = ring_gather(normed)
    cross_share = half_swap(after(cross_share, normed))
    rows_one, units, scales, queries, own_pair = project(
        normed_parts, qkv_flat, pack, cos_wide, sin_wide, qnorm_gain, knorm_gain
    )
    own_pair, cross_share = join(own_pair, cross_share)
    cross_pack = lax.all_gather(cross_share, "dp", axis=0, tiled=False)
    core_pair = core_swap(own_pair)
    half_pair = half_swap(own_pair)
    pairs = (own_pair, core_pair, half_pair, core_swap(half_pair))
    mixed_one, totals, *partial = self_attention(
        queries, pairs, attn_out_w, pack, head_dim
    )
    ff_share = half_swap(after(ff_share, half_pair))
    hidden_one, normed = mid_norm(ring_scatter(partial), hidden_zero, norm2_gain)
    ff_pack = gather_low(after(ff_share, normed))
    skip_rows = jnp.concatenate([part[part_count:] for part in normed_parts], 0)
    skip_half = half_swap(after(skip_rows, normed))
    other_text, other_units, other_scales, other_ckv = text_layer(
        text_rows_in, after(cross_pack, normed), cknorm_gain, model_width // 4
    )
    *normed_parts, other_text = join(*ring_gather(normed), other_text)
    rows_two, cross_raw, mixed_two, *partial = cross_layer(
        normed_parts,
        cq_turned,
        cross_out_w,
        cross_pack,
        text_pair,
        other_text,
        cqnorm_gain,
        text_count,
    )
    *partial, skip_half = join(*partial, skip_half)
    skip_rows = place_blocks(jnp.split(skip_rows, ring), jnp.split(skip_half, ring))
    *pieces, skip_rows = join(*ring_scatter(partial), skip_rows)
    hidden_two, normed = mid_norm(pieces, hidden_one, norm3_gain)
    skip_pack = gather_low(
        skip_rows.reshape(tensor_count, -1, model_width)
    )
    rows_three, acts, *partial = feed_forward(
        ring_gather(normed), cot_rows, fc1_w, fc2_w, ff_pack
    )
    partial, last_partial = partial[:ring], partial[ring:]

    fc_grads = feed_forward_grads(acts, rows_three, cot_rows, low_count)
    *pieces, fc_grads = join(*ring_scatter(partial), fc_grads.reshape(-1, model_width))
    fc_grads = scatter_low(after(fc_grads, skip_pack))
    residual, out_grad, norm3_grad = mid_norm_back(
        pieces, own_rows(cotangent), hidden_two, norm3_gain
    )
    out_parts = ring_gather(out_grad)
    grad_rows_two, cross_raw_grad, text_own, text_other, cqnorm_grad, *partial = cross_layer_back(
        out_parts,
        cross_raw,
        cq_turned,
        cross_out_w,
        cross_pack,
        text_pair,
        other_text,
        cqnorm_gain,
        text_count,
    )
    crosses = cross_grads(
        cross_raw_grad, mixed_two, rows_two, grad_rows_two, low_count, 48
    )
    *pieces, crosses = join(*ring_scatter(partial), crosses)
    residual, out_grad, norm2_grad = mid_norm_back(pieces, residual, hidden_one, norm2_gain)
    early_sums = text_layer_back(
        crosses,
        (text_own, text_other),
        (text_units, other_units),
        (text_scales, other_scales),
        after(text_rows_in, out_grad),
        (ckv_flat, other_ckv),
        cknorm_gain,
    )
    *out_parts, early_sums, fc_grads = join(*ring_gather(out_grad), early_sums, fc_grads)
    early_sums = scatter_low(early_sums.reshape(-1, model_width))
    grad_rows_one, query_grad, pair_grad, half_grad, core_grad, far_grad = self_attention_back(
        queries,
        pairs,
        totals,
        out_parts,
        attn_out_w,
        pack,
        head_dim,
    )
    core_grad = core_swap(core_grad)
    half_grad = half_swap(half_grad)
    far_grad = far_swap(far_grad)
    core_grad, half_grad, far_grad = join(core_grad, half_grad, far_grad)
    fc_grads = after(fc_grads, half_grad)
    share = fc_grads.shape[0] // 2
    fc_grads = half_sum(fc_grads[:share], fc_grads[share:])
    projected_grad, projected_other, qnorm_grad, knorm_grad, *partial = project_back(
        units,
        scales,
        cos_wide,
        sin_wide,
        qnorm_gain,
        knorm_gain,
        query_grad,
        pair_grad,
        core_grad,
        half_grad,
        far_grad,
        qkv_flat,
        pack,
    )
    *partial, fc_grads = join(*partial, fc_grads)
    fc_grads = fc_grads + low_swap(fc_grads.astype(BF16)).astype(F32)
    late_sums = self_grads(
        projected_grad, projected_other, mixed_one, rows_one, grad_rows_one, low_count, 96
    )
    early_sums = after(early_sums, qnorm_grad)
    early_share = early_sums.shape[0] // 2
    early_sums = half_sum(early_sums[:early_share], early_sums[early_share:])
    *pieces, late_sums, fc_grads, early_sums = join(
        *ring_scatter(partial), late_sums, fc_grads, early_sums
    )
    late_sums = scatter_low(late_sums.reshape(-1, model_width))
    misc = jnp.concatenate([qnorm_grad, knorm_grad, cqnorm_grad], 1)
    misc = jnp.pad(misc, ((0, 0), (0, model_width - misc.shape[1])))
    merged_out = last_norms(
        pieces,
        hidden_zero,
        merged,
        residual,
        (norm1_gain, skip_gain),
        norm2_grad,
        norm3_grad,
        misc,
    )
    joined_rows = ring_rows(joined, half)
    joined_own = lax.dynamic_slice_in_dim(joined_rows, tensor_place * slab_width, slab_width, 1)
    joined_other = lax.dynamic_slice_in_dim(
        joined_rows, (tensor_place + ring) % tensor_count * slab_width, slab_width, 1
    )
    merged_out, early_sums = join(merged_out, early_sums)
    early_sums = early_sums + low_swap(early_sums.astype(BF16)).astype(F32)
    *merged_parts, joined_own, joined_other, early_sums = join(
        *ring_gather(merged_out), joined_own, joined_other, early_sums
    )

    text_rows = early_sums[-48:]
    for part in ring_gather(text_rows.astype(BF16))[1:]:
        text_rows = text_rows + part.astype(F32)

    last_rows = -(-(slab_width + 16) // (8 * dp_count)) * 8 * dp_count
    merged_rows, last_sums = skip_grads(merged_parts, joined_own, joined_other, last_rows)
    merged_rows, last_sums, text_rows = join(merged_rows, last_sums, text_rows)
    early_sums = jnp.concatenate([fc_grads, early_sums[:-48], text_rows], 0).astype(BF16)
    early_sums = gather_low(after(early_sums, late_sums))
    merged_half = half_swap(merged_rows)
    last_sums = scatter_stage(0, last_sums)
    output = hidden_two
    for piece in ring_scatter(after_all(last_partial, last_sums)):
        output = output + piece.astype(F32)
    last_sums = scatter_stage(1, last_sums)
    last_sums, output, merged_half = join(last_sums, output, merged_half)
    share = late_sums.shape[0] // 2
    own_sums = jnp.concatenate([late_sums[:share].astype(F32), last_sums[0]], 0)
    other_sums = jnp.concatenate([late_sums[share:], last_sums[1].astype(BF16)], 0)
    last_sums = half_sum(own_sums, other_sums)
    output = jnp.concatenate(ring_gather(output.astype(BF16)), 0)
    last_sums, output = join(last_sums, output)
    last_sums = last_sums + low_swap(last_sums.astype(BF16)).astype(F32)
    merged_grad = place_blocks(jnp.split(merged_rows, ring), jnp.split(merged_half, ring))
    latent_grad, skip_grad = joined_grads(merged_grad, skip_pack, slab_width)
    last_sums = gather_low(after(last_sums, early_sums).astype(BF16))
    output_half = half_swap(after(output, early_sums))
    fc_share = fc_grads.shape[0]
    fc1_grad, fc2_grad = feed_forward_out(early_sums, fc_share)
    output = place_blocks(jnp.split(output, ring), jnp.split(output_half, ring))
    cross_sums = early_sums[:, fc_share : fc_share + 48].reshape(-1, model_width)
    cq_grad = cross_sums[:local_width].T.astype(F32)
    cross_out_grad = cross_sums[local_width : 2 * local_width].astype(F32)
    ckv_grad = early_sums[:, fc_share + 48 : fc_share + 96].reshape(-1, model_width)
    ckv_grad = ckv_grad[: 2 * local_width, :text_width].astype(F32)
    ckv_grad = ckv_grad.T.reshape(text_width, 2, local_width)
    text_rows = early_sums[:, fc_share + 96 :].reshape(-1, model_width).astype(F32)
    text_grad = text_rows[:text_count, :text_width]
    cknorm_grad = text_rows[-1, :head_dim]
    (
        last_sums,
        latent_grad,
        skip_grad,
        output,
        fc1_grad,
        fc2_grad,
        cq_grad,
        cross_out_grad,
        ckv_grad,
        text_grad,
        cknorm_grad,
    ) = join(
        last_sums,
        latent_grad,
        skip_grad,
        output,
        fc1_grad,
        fc2_grad,
        cq_grad,
        cross_out_grad,
        ckv_grad,
        text_grad,
        cknorm_grad,
    )
    self_sums = last_sums[:, :share].reshape(-1, model_width)
    qkv_grad = self_sums[:qkv_rows].T.astype(F32).reshape(model_width, 3, local_width)
    attn_out_grad = self_sums[qkv_rows : qkv_rows + local_width].astype(F32)
    last_sums = last_sums[:, share:].reshape(4, 2, -1, model_width).transpose(1, 0, 2, 3)
    last_sums = last_sums.reshape(-1, model_width)
    skip_w_grad = last_sums[:slab_width].astype(F32)
    small = last_sums[slab_width:].astype(F32)
    skip_gain_grad, norm1_grad, norm2_grad, norm3_grad, mod_vector = [small[i] for i in range(5)]
    qnorm_grad, knorm_grad, cqnorm_grad = [
        small[5, i * head_dim : (i + 1) * head_dim] for i in range(3)
    ]
    mod_grad = silu_cond.astype(F32)[:, None] * mod_vector[None, :]
    return (
        output,
        latent_grad,
        skip_grad,
        text_grad,
        skip_w_grad,
        skip_gain_grad,
        norm1_grad,
        mod_grad,
        qkv_grad,
        qnorm_grad,
        knorm_grad,
        attn_out_grad,
        norm2_grad,
        cq_grad,
        ckv_grad,
        cqnorm_grad,
        cknorm_grad,
        cross_out_grad,
        norm3_grad,
        fc1_grad,
        fc2_grad,
    )


def solution(mesh):
    placed = (
        P("dp", None),
        P("dp", None),
        P(),
        P(),
        P("dp", None),
        P("dp", None),
        P("tensor", None),
        P(),
        P(),
        P(),
        P(None, None, "tensor"),
        P(),
        P(),
        P("tensor", None),
        P(),
        P(None, "tensor"),
        P(None, None, "tensor"),
        P(),
        P(),
        P("tensor", None),
        P(),
        P(None, "tensor"),
        P("tensor", None),
    )
    return jax.shard_map(
        local,
        mesh=mesh,
        in_specs=placed,
        out_specs=(
            P("dp", None),
            P("dp", None),
            P("dp", None),
            P(),
            P("tensor", None),
            P(),
            P(),
            P(),
            P(None, None, "tensor"),
            P(),
            P(),
            P("tensor", None),
            P(),
            P(None, "tensor"),
            P(None, None, "tensor"),
            P(),
            P(),
            P("tensor", None),
            P(),
            P(None, "tensor"),
            P("tensor", None),
        ),
        check_vma=False,
    )
```
